32 devices in a mesh: cell: 16 (over z, y, x), aux: 2 (over core).
Axes of the slice: x: 2, y: 2, z: 4, core: 2. Of those that a mesh axis runs over, the one named last changes fastest.
Arguments:
- blocks: float32 [16, 8, 300, 300], P('cell', 'aux'), may hold values from -0.75 to 0.75
- cell_offsets: int32 [3, 16], replicated, may hold values from -2 to 1, as said below
- occ_coeff: float32 [2, 300, 60], replicated, may hold values from -0.25 to 0.25
- vir_coeff: float32 [16, 2, 300, 240], P('cell', None, None, 'aux'), may hold values from -0.25 to 0.25
- transfer_index: int32 [16], replicated, may hold values from 0 to 15, as said below
Outputs:
- pair_ints: float32 [2, 8, 16, 14400], P(None, 'aux', None, 'cell')
The draws below stay inside these ranges and needn't reach their ends.
Inputs may be any that keep to these rules, and one draw needn't show every extreme that they name: `cell_offsets`: column R is the integer lattice vector of cell R; the columns are the 16 cells of the centred 4 x 4 x 1 supercell, each once, in an order drawn from the seed. `transfer_index`: entry k is the index (a 4 + b) + c of the k-point k - k1 folded into the 4 x 4 x 1 mesh, for one k1 drawn from the seed; every index appears once.
All inputs are finite; a program needn't handle non-finite values.
Results may differ from the reference program's by a relative error of at most 0.00007.
Values sent between devices are 32-bit elements; how exact they have to be, the bound alone decides.
No kernel may reach another device: no remote copies, remote signals or barrier semaphores. Data moves between devices by JAX's collectives and lax.ppermute only.
A program may use at most 64 MiB of HBM per device.

```python
import math
import jax
import jax.numpy as jnp
from jax import lax

NB = 300
NO = 60
NV = 240
KX = 4
KY = 4
NCELLS = 16
KZ = 1
NAUXS = 8


def draw_cell_offsets(key, part):
    order = jax.random.permutation(key, NCELLS).astype(jnp.int32)
    first = order // (KY * KZ) - KX // 2
    second = order // KZ % KY - KY // 2
    third = order % KZ - KZ // 2
    return jnp.stack([first, second, third]).astype(jnp.int32)


def draw_transfer_index(key, part):
    anchor = jax.random.randint(key, (), 0, NCELLS).astype(jnp.int32)
    points = jnp.arange(NCELLS, dtype=jnp.int32)
    along_a = (points // (KY * KZ) - anchor // (KY * KZ)) % KX
    along_b = (points // KZ % KY - anchor // KZ % KY) % KY
    along_c = (points % KZ - anchor % KZ) % KZ
    return ((along_a * KY + along_b) * KZ + along_c).astype(jnp.int32)


def levels(own_key, extent, pieces, low, high):
    def one(axis_at, shards_of):
        draws = jax.random.uniform(jax.random.fold_in(jax.random.fold_in(own_key, 6), axis_at), (shards_of,), jnp.float32, low / len(pieces), high / len(pieces))
        return jnp.repeat(jnp.exp(draws), extent[axis_at] // shards_of).reshape((-1,) + (1,) * (len(extent) - axis_at - 1))

    loudness = one(*pieces[0])
    for cut in pieces[1:]:
        loudness = loudness * one(*cut)
    return loudness


def normal_values(stream_key, extent, scale, limit, split=(), kind=jnp.bfloat16):
    values = scale * jax.random.normal(stream_key, extent, jnp.float32)
    if split:
        values = values * levels(stream_key, extent, split, -0.22, 0.18)
    return jnp.clip(values, -limit, limit).astype(kind)


def setup_inputs(seed: int = 0) -> dict:
    seeds = jax.random.split(jax.random.key(seed), 6)
    blocks = normal_values(seeds[0], (NCELLS, NAUXS, NB, NB), 0.125, 0.75, ((0, 16), (1, 2)), jnp.float32)
    cell_offsets = draw_cell_offsets(jax.random.fold_in(seeds[5], 71), 0)
    occ_coeff = normal_values(seeds[2], (2, NB, NO), (2 * NB) ** -0.5, 0.25, (), jnp.float32)
    vir_coeff = normal_values(seeds[3], (NCELLS, 2, NB, NV), (2 * NB) ** -0.5, 0.25, ((0, 16), (3, 2)), jnp.float32)
    transfer_index = draw_transfer_index(jax.random.fold_in(seeds[5], 71), 0)
    return {"blocks": blocks, "cell_offsets": cell_offsets, "occ_coeff": occ_coeff, "vir_coeff": vir_coeff, "transfer_index": transfer_index}


def phases(cell_offsets):
    points = jnp.arange(NCELLS, dtype=jnp.int32)
    along_a = points // (KY * KZ)
    along_b = (points // KZ) % KY
    along_c = points % KZ
    turns = (along_a[:, None] * cell_offsets[0][None, :] * (KY * KZ)
             + along_b[:, None] * cell_offsets[1][None, :] * (KX * KZ)
             + along_c[:, None] * cell_offsets[2][None, :] * (KX * KY)) % NCELLS
    angles = (2.0 * math.pi / NCELLS) * turns.astype(jnp.float32)
    return jnp.cos(angles), jnp.sin(angles)


def reference(blocks, cell_offsets, occ_coeff, vir_coeff, transfer_index):
    cosines, sines = phases(cell_offsets)
    occ_real, occ_imag = occ_coeff[0], occ_coeff[1]
    vir_real, vir_imag = vir_coeff[:, 0], vir_coeff[:, 1]
    highest = lax.Precision.HIGHEST

    def one_function(position):
        slab_blocks = lax.dynamic_index_in_dim(blocks, position, 1, keepdims=False).reshape(NCELLS, NB * NB)
        grid_real = jnp.dot(cosines, slab_blocks, precision=highest, preferred_element_type=jnp.float32).reshape(NCELLS, NB, NB)
        grid_imag = jnp.dot(sines, slab_blocks, precision=highest, preferred_element_type=jnp.float32).reshape(NCELLS, NB, NB)
        half_real = jnp.einsum("mi,kmn->kin", occ_real, grid_real, precision=highest) + jnp.einsum("mi,kmn->kin", occ_imag, grid_imag, precision=highest)
        half_imag = jnp.einsum("mi,kmn->kin", occ_real, grid_imag, precision=highest) - jnp.einsum("mi,kmn->kin", occ_imag, grid_real, precision=highest)
        band_real = jnp.einsum("kin,kna->kia", half_real, vir_real, precision=highest) - jnp.einsum("kin,kna->kia", half_imag, vir_imag, precision=highest)
        band_imag = jnp.einsum("kin,kna->kia", half_real, vir_imag, precision=highest) + jnp.einsum("kin,kna->kia", half_imag, vir_real, precision=highest)
        return jnp.stack([band_real, band_imag])

    banded = lax.map(one_function, jnp.arange(NAUXS, dtype=jnp.int32))
    source = jnp.argsort(transfer_index).astype(jnp.int32)
    regrouped = jnp.take(banded, source, axis=2)
    return jnp.transpose(regrouped.reshape(NAUXS, 2, NCELLS, NO * NV), (1, 0, 2, 3))
```

```python
import functools
import math

import jax
import jax.numpy as jnp
from jax import lax
from jax.experimental import pallas as pl
from jax.experimental.pallas import tpu as pltpu
from jax.sharding import PartitionSpec as P

KX = 4
KY = 4
LANES = 128
HALF_LANES = 64
BF16 = jnp.bfloat16
F32 = jnp.float32


def phase_tables(cell_offsets, cell_count):
    depth = cell_count // (KX * KY)
    points = jnp.arange(cell_count, dtype=jnp.int32)
    along_a = points // (KY * depth)
    along_b = points // depth % KY
    along_c = points % depth
    turns = (
        along_a[:, None] * cell_offsets[0][None, :] * (KY * depth)
        + along_b[:, None] * cell_offsets[1][None, :] * (KX * depth)
        + along_c[:, None] * cell_offsets[2][None, :] * (KX * KY)
    ) % cell_count
    angles = 2.0 * math.pi / cell_count * turns.astype(jnp.float32)
    return (jnp.cos(angles), jnp.sin(angles))


def matmul(left, right):
    return jnp.dot(left, right, precision=lax.Precision.HIGHEST, preferred_element_type=jnp.float32)


def contract(form, left, right):
    return jnp.einsum(form, left, right, precision=lax.Precision.HIGHEST)


def by_entries(blocks, cell_offsets, occ_coeff, vir_coeff, transfer_index):
    cell_count = lax.axis_size("cell")
    slab_rows = blocks.shape[1]
    basis_size = blocks.shape[2]
    occupied = occ_coeff.shape[2]
    cosines, sines = phase_tables(cell_offsets, cell_count)
    occ_real, occ_imag = (occ_coeff[0], occ_coeff[1])
    flattened = blocks.reshape(1, -1)
    arrived = lax.all_to_all(flattened, "cell", split_axis=1, concat_axis=0, tiled=True)
    grid_real = matmul(cosines, arrived)
    grid_imag = matmul(sines, arrived)
    back_real, back_imag = (
        lax.all_to_all(grid_real, "cell", split_axis=0, concat_axis=1, tiled=True),
        lax.all_to_all(grid_imag, "cell", split_axis=0, concat_axis=1, tiled=True),
    )
    spec_real = back_real.reshape(slab_rows, basis_size, basis_size)
    spec_imag = back_imag.reshape(slab_rows, basis_size, basis_size)
    half_real = contract("mi,pmn->pin", occ_real, spec_real) + contract(
        "mi,pmn->pin", occ_imag, spec_imag
    )
    half_imag = contract("mi,pmn->pin", occ_real, spec_imag) - contract(
        "mi,pmn->pin", occ_imag, spec_real
    )
    rows_real = half_real.reshape(slab_rows * occupied, basis_size)
    rows_imag = half_imag.reshape(slab_rows * occupied, basis_size)
    column_piece = lax.all_gather(vir_coeff, "aux", axis=3, tiled=True)
    coef_real = column_piece[0, 0]
    coef_imag = column_piece[0, 1]
    part_real = matmul(rows_real, coef_real) - matmul(rows_imag, coef_imag)
    part_imag = matmul(rows_real, coef_imag) + matmul(rows_imag, coef_real)
    banded = jnp.stack([part_real, part_imag])
    pair_rows = banded.reshape(2, slab_rows, 1, -1)
    regrouped = lax.all_to_all(pair_rows, "cell", split_axis=3, concat_axis=2, tiled=True)
    source = jnp.argsort(transfer_index)
    return jnp.take(regrouped, source, axis=2)


def split(value):
    high = value.astype(BF16)
    return high, (value - high.astype(F32)).astype(BF16)


def dot(left, right):
    return jnp.dot(left, right, preferred_element_type=F32)


def padded(count, step):
    return -(-count // step) * step


class Sizes:
    def __init__(self, blocks, occ_coeff, vir_coeff):
        self.slab = blocks.shape[1]
        self.basis = blocks.shape[2]
        self.occ = occ_coeff.shape[2]
        self.vir_half = vir_coeff.shape[3]
        self.main = self.basis // LANES * LANES
        self.rest = self.basis - self.main
        self.width = 2 * self.main + LANES
        self.bands = self.occ // KX
        self.rows = padded(self.bands, 8)
        self.chunk = self.vir_half // 2
        self.chunks = 4 * self.bands // KY
        self.tiles = self.chunks // 2 + 1
        self.pairs = self.chunk * self.chunks

    @staticmethod
    def fit(cells, aux, blocks, occ_coeff, vir_coeff):
        basis, occ, half = blocks.shape[2], occ_coeff.shape[2], vir_coeff.shape[3]
        return (
            cells == KX * KY
            and aux == 2
            and blocks.shape[1] == KY
            and occ % KX == 0
            and occ // KX % 2 == 1
            and 0 < basis % LANES <= HALF_LANES
            and basis > LANES
            and half % 2 == 0
            and HALF_LANES - 8 < half // 2 <= HALF_LANES
        )


def half_kernel(sz, block_ref, occ_ref, out_ref, left_ref, wide_ref):
    @pl.when(pl.program_id(0) == 0)
    def _():
        place = lax.broadcasted_iota(jnp.int32, (KX * sz.rows, sz.occ), 0)
        band = lax.broadcasted_iota(jnp.int32, (KX * sz.rows, sz.occ), 1)
        inner = place % sz.rows
        pick = ((place // sz.rows * sz.bands + inner == band) & (inner < sz.bands)).astype(BF16)
        for part in range(2):
            sign = 1.0 if part == 0 else -1.0
            for level, term in enumerate(split(occ_ref[part])):
                rows = lax.dot_general(pick, term, (((1,), (1,)), ((), ())), preferred_element_type=F32)
                left_ref[level, part] = sign * rows
        wide_ref[...] = jnp.zeros_like(wide_ref)

    wide_ref[:, : sz.basis] = block_ref[0, 0]
    high, low = split(wide_ref[...])
    count = KX * sz.rows
    left_high = left_ref[0].reshape(2 * count, sz.basis).astype(BF16)
    left_low = left_ref[1].reshape(2 * count, sz.basis).astype(BF16)
    half = dot(left_high, high) + dot(left_low, high) + dot(left_high, low)
    real, imag = half[:count], half[count:]
    rest = real[:, sz.main :] + pltpu.roll(imag[:, sz.main :], HALF_LANES, 1)
    for z in range(KX):
        span = slice(z * sz.rows, (z + 1) * sz.rows)
        out_ref[z, 0, :, : sz.main] = real[span, : sz.main]
        out_ref[z, 0, :, sz.main : 2 * sz.main] = imag[span, : sz.main]
        out_ref[z, 0, :, 2 * sz.main :] = rest[span]


def half_bands(sz, blocks, occ_coeff):
    return pl.pallas_call(
        functools.partial(half_kernel, sz),
        grid=(sz.slab,),
        out_shape=jax.ShapeDtypeStruct((KX, KY, sz.rows, sz.width), F32),
        in_specs=[
            pl.BlockSpec((1, 1, sz.basis, sz.basis), lambda p: (0, p, 0, 0)),
            pl.BlockSpec((2, sz.basis, sz.occ), lambda p: (0, 0, 0)),
        ],
        out_specs=pl.BlockSpec((KX, 1, sz.rows, sz.width), lambda p: (0, p, 0, 0)),
        scratch_shapes=[
            pltpu.VMEM((2, 2, KX * sz.rows, sz.basis), F32),
            pltpu.VMEM((sz.basis, sz.main + LANES), F32),
        ],
        compiler_params=pltpu.CompilerParams(vmem_limit_bytes=32 << 20),
    )(blocks, occ_coeff)


def four_points(zero, one, two, three, turn):
    even, odd = zero + two, one + three
    lift, lean = zero - two, turn(one - three)
    return even + odd, lift + lean, even - odd, lift - lean


class Pair:
    def __init__(self, real, imag):
        self.real, self.imag = real, imag

    def __add__(self, other):
        return Pair(self.real + other.real, self.imag + other.imag)

    def __sub__(self, other):
        return Pair(self.real - other.real, self.imag - other.imag)

    def turned(self):
        return Pair(-self.imag, self.real)


def lattice_kernel(sz, place_ref, offset_ref, cells_ref, *refs):
    outs, grid_ref, slot_ref = refs[:KY], refs[KY], refs[KY + 1]
    plane, seat = place_ref[0], place_ref[1]
    for cell in range(KX * KY):
        slot_ref[(offset_ref[0, cell] & 3) * KY + (offset_ref[1, cell] & 3)] = cell
    slots = [slot_ref[n] for n in range(KX * KY)]
    real_half = lax.broadcasted_iota(jnp.int32, (8, LANES), 1) < HALF_LANES

    def turn_rest(value):
        moved = pltpu.roll(value, HALF_LANES, 1)
        return jnp.where(real_half, -moved, moved)

    def transform(load, turn, store):
        firsts = [four_points(*[load(slots[n * KY + m]) for n in range(KX)], turn) for m in range(KY)]
        for a in range(KX):
            seconds = four_points(*[firsts[m][a] for m in range(KY)], turn)
            for b in range(KY):
                store(a, b, seconds[b])

    for row in range(0, sz.rows, 8):
        span = slice(row, row + 8)
        for lane in range(0, sz.main, LANES):
            near, far = slice(lane, lane + LANES), slice(sz.main + lane, sz.main + lane + LANES)

            def load(cell):
                return Pair(cells_ref[cell, span, near], cells_ref[cell, span, far])

            def store(a, b, value):
                grid_ref[b, a ^ plane, span, near] = value.real
                grid_ref[b, a ^ plane, span, far] = value.imag

            transform(load, Pair.turned, store)
        tail = slice(2 * sz.main, sz.width)

        def load_rest(cell):
            return cells_ref[cell, span, tail]

        def store_rest(a, b, value):
            grid_ref[b, a ^ plane, span, tail] = value

        transform(load_rest, turn_rest, store_rest)
    for step in range(KY):
        outs[step][...] = grid_ref[step ^ seat]


def lattice_sum(sz, place, cell_offsets, cells):
    shape = jax.ShapeDtypeStruct((KX, sz.rows, sz.width), F32)
    whole = pl.BlockSpec(memory_space=pltpu.VMEM)
    scalars = pl.BlockSpec(memory_space=pltpu.SMEM)
    return pl.pallas_call(
        functools.partial(lattice_kernel, sz),
        out_shape=[shape] * KY,
        in_specs=[scalars, scalars, whole],
        out_specs=[whole] * KY,
        scratch_shapes=[
            pltpu.VMEM((KY, KX, sz.rows, sz.width), F32),
            pltpu.SMEM((KX * KY,), jnp.int32),
        ],
        compiler_params=pltpu.CompilerParams(vmem_limit_bytes=32 << 20),
    )(place, cell_offsets, cells)


def band_kernel(sz, place_ref, *refs):
    halves, own, other = refs[:KY], refs[KY : KY + KX], refs[KY + KX : KY + 2 * KX]
    outs = refs[KY + 2 * KX : 2 * KY + 2 * KX]
    left_ref, band_ref, tile_ref = refs[2 * KY + 2 * KX :]
    seat, core = place_ref[1], place_ref[2]
    low_lanes = lax.broadcasted_iota(jnp.int32, (sz.basis, LANES), 1) < HALF_LANES
    count = KY * sz.rows
    for step in range(KY):
        left_ref[:, step ^ seat] = halves[step][...]

    def spread(ref, part):
        value = jnp.concatenate([ref[part], ref[part][:, : LANES - sz.vir_half]], axis=1)
        return jnp.where(low_lanes, value, pltpu.roll(value, HALF_LANES - sz.chunk, 1))

    for k in range(KX):
        left = left_ref[k].reshape(count, sz.width)
        tail = left[:, 2 * sz.main :]
        near = jnp.concatenate([left[:, : sz.main], left[:, sz.main : 2 * sz.main]], axis=0)
        rest = jnp.concatenate([tail, pltpu.roll(tail, HALF_LANES, 1)], axis=0)[:, : sz.rest]
        near_high, near_low = split(near)
        rest_high, rest_low = split(rest)
        columns = []
        for part in range(2):
            mine, theirs = spread(own[k], part), spread(other[k], part)
            columns += [jnp.where(core == 0, mine, theirs), jnp.where(core == 0, theirs, mine)]
        right = jnp.concatenate(columns, axis=1)
        main_high, main_low = split(right[: sz.main])
        last_high, last_low = split(right[sz.main :])
        band = (
            dot(near_high, main_high)
            + dot(near_low, main_high)
            + dot(near_high, main_low)
            + dot(rest_high, last_high)
            + dot(rest_low, last_high)
            + dot(rest_high, last_low)
        )
        width = 2 * LANES
        top, bottom = band[:count], band[count:]
        real = top[:, :width] - bottom[:, width:]
        imag = top[:, width:] + bottom[:, :width]
        for h in range(2):
            lanes = slice(h * LANES, (h + 1) * LANES)
            band_ref[h, 0] = real[:, lanes]
            band_ref[h, 1] = imag[:, lanes]
        for i in range(sz.bands):
            for h in range(2):
                for part in range(2):
                    tile_ref[2 * i + h, part * KY : (part + 1) * KY] = band_ref[
                        h, part, pl.ds(i, KY, stride=sz.rows)
                    ]
        for step in range(KY):
            first = (step ^ seat) * sz.chunks // 2
            for n in range(sz.tiles):
                outs[step][k, n] = tile_ref[first + n]


def band_product(sz, place, halves, own, other):
    shape = jax.ShapeDtypeStruct((KX, sz.tiles, 2 * KY, LANES), F32)
    whole = pl.BlockSpec(memory_space=pltpu.VMEM)
    scalars = pl.BlockSpec(memory_space=pltpu.SMEM)
    return pl.pallas_call(
        functools.partial(band_kernel, sz),
        out_shape=[shape] * KY,
        in_specs=[scalars] + [whole] * (KY + 2 * KX),
        out_specs=[whole] * KY,
        scratch_shapes=[
            pltpu.VMEM((KX, KY, sz.rows, sz.width), F32),
            pltpu.VMEM((2, 2, KY * sz.rows, LANES), F32),
            pltpu.VMEM((2 * sz.bands, 2 * KY, LANES), F32),
        ],
        compiler_params=pltpu.CompilerParams(vmem_limit_bytes=32 << 20),
    )(place, *halves, *own, *other)


def regroup_kernel(sz, place_ref, transfer_ref, *refs):
    sources, out_ref, row_ref = refs[:KY], refs[KY], refs[KY + 1]
    plane, seat = place_ref[0], place_ref[1]
    lane = lax.broadcasted_iota(jnp.int32, (2 * KY, LANES), 1)
    cells = KX * KY

    def place_rows(odd):
        for step in range(KY):
            for k in range(KX):
                point = (k ^ plane) * KY + (step ^ seat)
                row = transfer_ref[point]
                for first in range(0, sz.pairs, LANES):
                    last = min(first + LANES, sz.pairs)
                    value = None
                    for u in range(first // sz.chunk, (last - 1) // sz.chunk + 1):
                        tile = sources[step][k, (u + odd) // 2]
                        shift = (sz.chunk * u - HALF_LANES * (u + odd)) % LANES
                        piece = pltpu.roll(tile, shift, 1) if shift else tile
                        value = piece if value is None else jnp.where(lane < sz.chunk * u - first, value, piece)
                    row_ref[first // LANES, pl.ds(row, 2 * KY, stride=cells)] = value

    @pl.when(seat % 2 == 0)
    def _():
        place_rows(0)

    @pl.when(seat % 2 == 1)
    def _():
        place_rows(1)

    for first in range(0, sz.pairs, LANES):
        last = min(first + LANES, sz.pairs)
        out_ref[:, first:last] = row_ref[first // LANES, :, : last - first]


def regroup(sz, place, transfer_index, sources):
    whole = pl.BlockSpec(memory_space=pltpu.VMEM)
    scalars = pl.BlockSpec(memory_space=pltpu.SMEM)
    return pl.pallas_call(
        functools.partial(regroup_kernel, sz),
        out_shape=jax.ShapeDtypeStruct((2 * KY * KX * KY, sz.pairs), F32),
        in_specs=[scalars, scalars] + [whole] * KY,
        out_specs=whole,
        scratch_shapes=[pltpu.VMEM((-(-sz.pairs // LANES), 2 * KY * KX * KY, LANES), F32)],
        compiler_params=pltpu.CompilerParams(vmem_limit_bytes=32 << 20),
    )(place, transfer_index, *sources)


def swap(value, step):
    return lax.ppermute(value, "cell", [(d, d ^ step) for d in range(KX * KY)])


def by_planes(blocks, cell_offsets, occ_coeff, vir_coeff, transfer_index):
    sz = Sizes(blocks, occ_coeff, vir_coeff)
    me = lax.axis_index("cell")
    place = jnp.stack([me // KY, me % KY, lax.axis_index("aux")]).astype(jnp.int32)
    home = vir_coeff[0]
    across = swap(home, 2 * KY)
    beside = swap(home, KY)
    corner = swap(across, KY)
    own = [home, beside, across, corner]
    other = [lax.ppermute(v, "aux", [(0, 1), (1, 0)]) for v in own]
    sent = half_bands(sz, blocks, occ_coeff).reshape(KX * KY, sz.rows, sz.width)
    cells = lax.all_to_all(sent, "cell", split_axis=0, concat_axis=0, tiled=True)
    points = lattice_sum(sz, place, cell_offsets, cells)
    halves = [points[0]] + [swap(points[s], s) for s in range(1, KY)]
    bands = band_product(sz, place, halves, own, other)
    sources = [bands[0]] + [swap(bands[s], s) for s in range(1, KY)]
    out = regroup(sz, place, transfer_index, sources)
    return out.reshape(2, sz.slab, KX * KY, sz.pairs)


def on_device(blocks, cell_offsets, occ_coeff, vir_coeff, transfer_index):
    arrays = (blocks, cell_offsets, occ_coeff, vir_coeff, transfer_index)
    if Sizes.fit(lax.axis_size("cell"), lax.axis_size("aux"), blocks, occ_coeff, vir_coeff):
        return by_planes(*arrays)
    return by_entries(*arrays)


def solution(mesh):
    placed = (P("cell", "aux", None, None), P(), P(), P("cell", None, None, "aux"), P())
    return jax.shard_map(
        on_device,
        mesh=mesh,
        in_specs=placed,
        out_specs=P(None, "aux", None, "cell"),
        check_vma=False,
    )
```

```python
import functools
import math

import jax
import jax.numpy as jnp
from jax import lax
from jax.experimental import pallas as pl
from jax.experimental.pallas import tpu as pltpu
from jax.sharding import PartitionSpec as P

KX = 4
KY = 4
LANES = 128
HALF_LANES = 64
BF16 = jnp.bfloat16
F32 = jnp.float32


def phase_tables(cell_offsets, cell_count):
    depth = cell_count // (KX * KY)
    points = jnp.arange(cell_count, dtype=jnp.int32)
    along_a = points // (KY * depth)
    along_b = points // depth % KY
    along_c = points % depth
    turns = (
        along_a[:, None] * cell_offsets[0][None, :] * (KY * depth)
        + along_b[:, None] * cell_offsets[1][None, :] * (KX * depth)
        + along_c[:, None] * cell_offsets[2][None, :] * (KX * KY)
    ) % cell_count
    angles = 2.0 * math.pi / cell_count * turns.astype(jnp.float32)
    return (jnp.cos(angles), jnp.sin(angles))


def matmul(left, right):
    return jnp.dot(left, right, precision=lax.Precision.HIGHEST, preferred_element_type=jnp.float32)


def contract(form, left, right):
    return jnp.einsum(form, left, right, precision=lax.Precision.HIGHEST)


def by_entries(blocks, cell_offsets, occ_coeff, vir_coeff, transfer_index):
    cell_count = lax.axis_size("cell")
    slab_rows = blocks.shape[1]
    basis_size = blocks.shape[2]
    occupied = occ_coeff.shape[2]
    cosines, sines = phase_tables(cell_offsets, cell_count)
    occ_real, occ_imag = (occ_coeff[0], occ_coeff[1])
    flattened = blocks.reshape(1, -1)
    arrived = lax.all_to_all(flattened, "cell", split_axis=1, concat_axis=0, tiled=True)
    grid_real = matmul(cosines, arrived)
    grid_imag = matmul(sines, arrived)
    back_real, back_imag = (
        lax.all_to_all(grid_real, "cell", split_axis=0, concat_axis=1, tiled=True),
        lax.all_to_all(grid_imag, "cell", split_axis=0, concat_axis=1, tiled=True),
    )
    spec_real = back_real.reshape(slab_rows, basis_size, basis_size)
    spec_imag = back_imag.reshape(slab_rows, basis_size, basis_size)
    half_real = contract("mi,pmn->pin", occ_real, spec_real) + contract(
        "mi,pmn->pin", occ_imag, spec_imag
    )
    half_imag = contract("mi,pmn->pin", occ_real, spec_imag) - contract(
        "mi,pmn->pin", occ_imag, spec_real
    )
    rows_real = half_real.reshape(slab_rows * occupied, basis_size)
    rows_imag = half_imag.reshape(slab_rows * occupied, basis_size)
    column_piece = lax.all_gather(vir_coeff, "aux", axis=3, tiled=True)
    coef_real = column_piece[0, 0]
    coef_imag = column_piece[0, 1]
    part_real = matmul(rows_real, coef_real) - matmul(rows_imag, coef_imag)
    part_imag = matmul(rows_real, coef_imag) + matmul(rows_imag, coef_real)
    banded = jnp.stack([part_real, part_imag])
    pair_rows = banded.reshape(2, slab_rows, 1, -1)
    regrouped = lax.all_to_all(pair_rows, "cell", split_axis=3, concat_axis=2, tiled=True)
    source = jnp.argsort(transfer_index)
    return jnp.take(regrouped, source, axis=2)


def split(value):
    high = value.astype(BF16)
    return high, (value - high.astype(F32)).astype(BF16)


def dot(left, right):
    return jnp.dot(left, right, preferred_element_type=F32)


def padded(count, step):
    return -(-count // step) * step


class Sizes:
    def __init__(self, blocks, occ_coeff, vir_coeff):
        self.slab = blocks.shape[1]
        self.basis = blocks.shape[2]
        self.occ = occ_coeff.shape[2]
        self.vir_half = vir_coeff.shape[3]
        self.main = self.basis // LANES * LANES
        self.rest = self.basis - self.main
        self.width = 2 * self.main + LANES
        self.bands = self.occ // KX
        self.rows = padded(self.bands, 8)
        self.chunk = self.vir_half // 2
        self.chunks = 4 * self.bands // KY
        self.tiles = self.chunks // 2 + 1
        self.pairs = self.chunk * self.chunks

    @staticmethod
    def fit(cells, aux, blocks, occ_coeff, vir_coeff):
        basis, occ, half = blocks.shape[2], occ_coeff.shape[2], vir_coeff.shape[3]
        return (
            cells == KX * KY
            and aux == 2
            and blocks.shape[1] == KY
            and occ % KX == 0
            and occ // KX % 2 == 1
            and 0 < basis % LANES <= HALF_LANES
            and basis > LANES
            and half % 2 == 0
            and HALF_LANES - 8 < half // 2 <= HALF_LANES
        )


def half_kernel(sz, block_ref, occ_ref, out_ref, left_ref, wide_ref):
    @pl.when(pl.program_id(0) == 0)
    def _():
        place = lax.broadcasted_iota(jnp.int32, (KX * sz.rows, sz.occ), 0)
        band = lax.broadcasted_iota(jnp.int32, (KX * sz.rows, sz.occ), 1)
        inner = place % sz.rows
        pick = ((place // sz.rows * sz.bands + inner == band) & (inner < sz.bands)).astype(BF16)
        for part in range(2):
            sign = 1.0 if part == 0 else -1.0
            for level, term in enumerate(split(occ_ref[part])):
                rows = lax.dot_general(pick, term, (((1,), (1,)), ((), ())), preferred_element_type=F32)
                left_ref[level, part] = sign * rows
        wide_ref[...] = jnp.zeros_like(wide_ref)

    wide_ref[:, : sz.basis] = block_ref[0, 0]
    high, low = split(wide_ref[...])
    count = KX * sz.rows
    left_high = left_ref[0].reshape(2 * count, sz.basis).astype(BF16)
    left_low = left_ref[1].reshape(2 * count, sz.basis).astype(BF16)
    half = dot(left_high, high) + dot(left_low, high) + dot(left_high, low)
    real, imag = half[:count], half[count:]
    rest = real[:, sz.main :] + pltpu.roll(imag[:, sz.main :], HALF_LANES, 1)
    for z in range(KX):
        span = slice(z * sz.rows, (z + 1) * sz.rows)
        out_ref[z, 0, :, : sz.main] = real[span, : sz.main]
        out_ref[z, 0, :, sz.main : 2 * sz.main] = imag[span, : sz.main]
        out_ref[z, 0, :, 2 * sz.main :] = rest[span]


def half_bands(sz, blocks, occ_coeff):
    return pl.pallas_call(
        functools.partial(half_kernel, sz),
        grid=(sz.slab,),
        out_shape=jax.ShapeDtypeStruct((KX, KY, sz.rows, sz.width), F32),
        in_specs=[
            pl.BlockSpec((1, 1, sz.basis, sz.basis), lambda p: (0, p, 0, 0)),
            pl.BlockSpec((2, sz.basis, sz.occ), lambda p: (0, 0, 0)),
        ],
        out_specs=pl.BlockSpec((KX, 1, sz.rows, sz.width), lambda p: (0, p, 0, 0)),
        scratch_shapes=[
            pltpu.VMEM((2, 2, KX * sz.rows, sz.basis), F32),
            pltpu.VMEM((sz.basis, sz.main + LANES), F32),
        ],
        compiler_params=pltpu.CompilerParams(vmem_limit_bytes=32 << 20),
        cost_estimate=pl.CostEstimate(flops=10**10, bytes_accessed=60_000_000, transcendentals=0),
    )(blocks, occ_coeff)


def four_points(zero, one, two, three, turn):
    even, odd = zero + two, one + three
    lift, lean = zero - two, turn(one - three)
    return even + odd, lift + lean, even - odd, lift - lean


class Pair:
    def __init__(self, real, imag):
        self.real, self.imag = real, imag

    def __add__(self, other):
        return Pair(self.real + other.real, self.imag + other.imag)

    def __sub__(self, other):
        return Pair(self.real - other.real, self.imag - other.imag)

    def turned(self):
        return Pair(-self.imag, self.real)


def lattice_kernel(sz, place_ref, offset_ref, cells_ref, *refs):
    outs, grid_ref, slot_ref = refs[:KY], refs[KY], refs[KY + 1]
    plane, seat = place_ref[0], place_ref[1]
    for cell in range(KX * KY):
        slot_ref[(offset_ref[0, cell] & 3) * KY + (offset_ref[1, cell] & 3)] = cell
    slots = [slot_ref[n] for n in range(KX * KY)]
    real_half = lax.broadcasted_iota(jnp.int32, (8, LANES), 1) < HALF_LANES

    def turn_rest(value):
        moved = pltpu.roll(value, HALF_LANES, 1)
        return jnp.where(real_half, -moved, moved)

    def transform(load, turn, store):
        firsts = [four_points(*[load(slots[n * KY + m]) for n in range(KX)], turn) for m in range(KY)]
        for a in range(KX):
            seconds = four_points(*[firsts[m][a] for m in range(KY)], turn)
            for b in range(KY):
                store(a, b, seconds[b])

    for row in range(0, sz.rows, 8):
        span = slice(row, row + 8)
        for lane in range(0, sz.main, LANES):
            near, far = slice(lane, lane + LANES), slice(sz.main + lane, sz.main + lane + LANES)

            def load(cell):
                return Pair(cells_ref[cell, span, near], cells_ref[cell, span, far])

            def store(a, b, value):
                grid_ref[b, a ^ plane, span, near] = value.real
                grid_ref[b, a ^ plane, span, far] = value.imag

            transform(load, Pair.turned, store)
        tail = slice(2 * sz.main, sz.width)

        def load_rest(cell):
            return cells_ref[cell, span, tail]

        def store_rest(a, b, value):
            grid_ref[b, a ^ plane, span, tail] = value

        transform(load_rest, turn_rest, store_rest)
    for step in range(KY):
        outs[step][...] = grid_ref[step ^ seat]


def lattice_sum(sz, place, cell_offsets, cells):
    shape = jax.ShapeDtypeStruct((KX, sz.rows, sz.width), F32)
    whole = pl.BlockSpec(memory_space=pltpu.VMEM)
    scalars = pl.BlockSpec(memory_space=pltpu.SMEM)
    return pl.pallas_call(
        functools.partial(lattice_kernel, sz),
        out_shape=[shape] * KY,
        in_specs=[scalars, scalars, whole],
        out_specs=[whole] * KY,
        scratch_shapes=[
            pltpu.VMEM((KY, KX, sz.rows, sz.width), F32),
            pltpu.SMEM((KX * KY,), jnp.int32),
        ],
        compiler_params=pltpu.CompilerParams(vmem_limit_bytes=32 << 20),
    )(place, cell_offsets, cells)


def band_kernel(sz, place_ref, *refs):
    halves, own, other = refs[:KY], refs[KY : KY + KX], refs[KY + KX : KY + 2 * KX]
    outs = refs[KY + 2 * KX : 2 * KY + 2 * KX]
    left_ref, band_ref, tile_ref = refs[2 * KY + 2 * KX :]
    seat, core = place_ref[1], place_ref[2]
    low_lanes = lax.broadcasted_iota(jnp.int32, (sz.basis, LANES), 1) < HALF_LANES
    count = KY * sz.rows
    for step in range(KY):
        left_ref[:, step ^ seat] = halves[step][...]

    def spread(ref, part):
        value = jnp.concatenate([ref[part], ref[part][:, : LANES - sz.vir_half]], axis=1)
        return jnp.where(low_lanes, value, pltpu.roll(value, HALF_LANES - sz.chunk, 1))

    for k in range(KX):
        left = left_ref[k].reshape(count, sz.width)
        tail = left[:, 2 * sz.main :]
        near = jnp.concatenate([left[:, : sz.main], left[:, sz.main : 2 * sz.main]], axis=0)
        rest = jnp.concatenate([tail, pltpu.roll(tail, HALF_LANES, 1)], axis=0)[:, : sz.rest]
        near_high, near_low = split(near)
        rest_high, rest_low = split(rest)
        columns = []
        for part in range(2):
            mine, theirs = spread(own[k], part), spread(other[k], part)
            columns += [jnp.where(core == 0, mine, theirs), jnp.where(core == 0, theirs, mine)]
        right = jnp.concatenate(columns, axis=1)
        main_high, main_low = split(right[: sz.main])
        last_high, last_low = split(right[sz.main :])
        band = (
            dot(near_high, main_high)
            + dot(near_low, main_high)
            + dot(near_high, main_low)
            + dot(rest_high, last_high)
            + dot(rest_low, last_high)
            + dot(rest_high, last_low)
        )
        width = 2 * LANES
        top, bottom = band[:count], band[count:]
        real = top[:, :width] - bottom[:, width:]
        imag = top[:, width:] + bottom[:, :width]
        for h in range(2):
            lanes = slice(h * LANES, (h + 1) * LANES)
            band_ref[h, 0] = real[:, lanes]
            band_ref[h, 1] = imag[:, lanes]
        for i in range(sz.bands):
            for h in range(2):
                for part in range(2):
                    tile_ref[2 * i + h, part * KY : (part + 1) * KY] = band_ref[
                        h, part, pl.ds(i, KY, stride=sz.rows)
                    ]
        for step in range(KY):
            first = (step ^ seat) * sz.chunks // 2
            for n in range(sz.tiles):
                outs[step][k, n] = tile_ref[first + n]


def band_product(sz, place, halves, own, other):
    shape = jax.ShapeDtypeStruct((KX, sz.tiles, 2 * KY, LANES), F32)
    whole = pl.BlockSpec(memory_space=pltpu.VMEM)
    scalars = pl.BlockSpec(memory_space=pltpu.SMEM)
    return pl.pallas_call(
        functools.partial(band_kernel, sz),
        out_shape=[shape] * KY,
        in_specs=[scalars] + [whole] * (KY + 2 * KX),
        out_specs=[whole] * KY,
        scratch_shapes=[
            pltpu.VMEM((KX, KY, sz.rows, sz.width), F32),
            pltpu.VMEM((2, 2, KY * sz.rows, LANES), F32),
            pltpu.VMEM((2 * sz.bands, 2 * KY, LANES), F32),
        ],
        compiler_params=pltpu.CompilerParams(vmem_limit_bytes=32 << 20),
    )(place, *halves, *own, *other)


def regroup_kernel(sz, place_ref, transfer_ref, *refs):
    sources, out_ref, row_ref = refs[:KY], refs[KY], refs[KY + 1]
    plane, seat = place_ref[0], place_ref[1]
    lane = lax.broadcasted_iota(jnp.int32, (2 * KY, LANES), 1)
    cells = KX * KY

    def place_rows(odd):
        for step in range(KY):
            for k in range(KX):
                point = (k ^ plane) * KY + (step ^ seat)
                row = transfer_ref[point]
                for first in range(0, sz.pairs, LANES):
                    last = min(first + LANES, sz.pairs)
                    value = None
                    for u in range(first // sz.chunk, (last - 1) // sz.chunk + 1):
                        tile = sources[step][k, (u + odd) // 2]
                        shift = (sz.chunk * u - HALF_LANES * (u + odd)) % LANES
                        piece = pltpu.roll(tile, shift, 1) if shift else tile
                        value = piece if value is None else jnp.where(lane < sz.chunk * u - first, value, piece)
                    row_ref[first // LANES, pl.ds(row, 2 * KY, stride=cells)] = value

    @pl.when(seat % 2 == 0)
    def _():
        place_rows(0)

    @pl.when(seat % 2 == 1)
    def _():
        place_rows(1)

    for first in range(0, sz.pairs, LANES):
        last = min(first + LANES, sz.pairs)
        out_ref[:, first:last] = row_ref[first // LANES, :, : last - first]


def regroup(sz, place, transfer_index, sources):
    whole = pl.BlockSpec(memory_space=pltpu.VMEM)
    scalars = pl.BlockSpec(memory_space=pltpu.SMEM)
    return pl.pallas_call(
        functools.partial(regroup_kernel, sz),
        out_shape=jax.ShapeDtypeStruct((2 * KY * KX * KY, sz.pairs), F32),
        in_specs=[scalars, scalars] + [whole] * KY,
        out_specs=whole,
        scratch_shapes=[pltpu.VMEM((-(-sz.pairs // LANES), 2 * KY * KX * KY, LANES), F32)],
        compiler_params=pltpu.CompilerParams(vmem_limit_bytes=32 << 20),
    )(place, transfer_index, *sources)


def hold_kernel(in_ref, out_ref):
    out_ref[...] = in_ref[...]


def hold(value):
    return pl.pallas_call(
        hold_kernel,
        out_shape=jax.ShapeDtypeStruct(value.shape, F32),
        cost_estimate=pl.CostEstimate(flops=10**10, bytes_accessed=100_000_000, transcendentals=0),
    )(value)


def swap(value, step):
    return lax.ppermute(value, "cell", [(d, d ^ step) for d in range(KX * KY)])


def by_planes(blocks, cell_offsets, occ_coeff, vir_coeff, transfer_index):
    sz = Sizes(blocks, occ_coeff, vir_coeff)
    me = lax.axis_index("cell")
    place = jnp.stack([me // KY, me % KY, lax.axis_index("aux")]).astype(jnp.int32)
    home = vir_coeff[0]
    across = hold(swap(home, 2 * KY))
    beside = swap(home, KY)
    corner = swap(across, KY)
    own = [home, beside, across, corner]
    other = [lax.ppermute(v, "aux", [(0, 1), (1, 0)]) for v in own]
    sent = half_bands(sz, blocks, occ_coeff).reshape(KX * KY, sz.rows, sz.width)
    cells = lax.all_to_all(sent, "cell", split_axis=0, concat_axis=0, tiled=True)
    points = lattice_sum(sz, place, cell_offsets, cells)
    halves = [points[0]] + [swap(points[s], s) for s in range(1, KY)]
    bands = band_product(sz, place, halves, own, other)
    sources = [bands[0]] + [swap(bands[s], s) for s in range(1, KY)]
    out = regroup(sz, place, transfer_index, sources)
    return out.reshape(2, sz.slab, KX * KY, sz.pairs)


def on_device(blocks, cell_offsets, occ_coeff, vir_coeff, transfer_index):
    arrays = (blocks, cell_offsets, occ_coeff, vir_coeff, transfer_index)
    if Sizes.fit(lax.axis_size("cell"), lax.axis_size("aux"), blocks, occ_coeff, vir_coeff):
        return by_planes(*arrays)
    return by_entries(*arrays)


def solution(mesh):
    placed = (P("cell", "aux", None, None), P(), P(), P("cell", None, None, "aux"), P())
    return jax.shard_map(
        on_device,
        mesh=mesh,
        in_specs=placed,
        out_specs=P(None, "aux", None, "cell"),
        check_vma=False,
    )
```

```python
import functools
import math

import jax
import jax.numpy as jnp
from jax import lax
from jax.experimental import pallas as pl
from jax.experimental.pallas import tpu as pltpu
from jax.sharding import PartitionSpec as P

KX = 4
KY = 4
LANES = 128
HALF_LANES = 64
BF16 = jnp.bfloat16
F32 = jnp.float32


def phase_tables(cell_offsets, cell_count):
    depth = cell_count // (KX * KY)
    points = jnp.arange(cell_count, dtype=jnp.int32)
    along_a = points // (KY * depth)
    along_b = points // depth % KY
    along_c = points % depth
    turns = (
        along_a[:, None] * cell_offsets[0][None, :] * (KY * depth)
        + along_b[:, None] * cell_offsets[1][None, :] * (KX * depth)
        + along_c[:, None] * cell_offsets[2][None, :] * (KX * KY)
    ) % cell_count
    angles = 2.0 * math.pi / cell_count * turns.astype(jnp.float32)
    return (jnp.cos(angles), jnp.sin(angles))


def matmul(left, right):
    return jnp.dot(left, right, precision=lax.Precision.HIGHEST, preferred_element_type=jnp.float32)


def contract(form, left, right):
    return jnp.einsum(form, left, right, precision=lax.Precision.HIGHEST)


def by_entries(blocks, cell_offsets, occ_coeff, vir_coeff, transfer_index):
    cell_count = lax.axis_size("cell")
    slab_rows = blocks.shape[1]
    basis_size = blocks.shape[2]
    occupied = occ_coeff.shape[2]
    cosines, sines = phase_tables(cell_offsets, cell_count)
    occ_real, occ_imag = (occ_coeff[0], occ_coeff[1])
    flattened = blocks.reshape(1, -1)
    arrived = lax.all_to_all(flattened, "cell", split_axis=1, concat_axis=0, tiled=True)
    grid_real = matmul(cosines, arrived)
    grid_imag = matmul(sines, arrived)
    back_real, back_imag = (
        lax.all_to_all(grid_real, "cell", split_axis=0, concat_axis=1, tiled=True),
        lax.all_to_all(grid_imag, "cell", split_axis=0, concat_axis=1, tiled=True),
    )
    spec_real = back_real.reshape(slab_rows, basis_size, basis_size)
    spec_imag = back_imag.reshape(slab_rows, basis_size, basis_size)
    half_real = contract("mi,pmn->pin", occ_real, spec_real) + contract(
        "mi,pmn->pin", occ_imag, spec_imag
    )
    half_imag = contract("mi,pmn->pin", occ_real, spec_imag) - contract(
        "mi,pmn->pin", occ_imag, spec_real
    )
    rows_real = half_real.reshape(slab_rows * occupied, basis_size)
    rows_imag = half_imag.reshape(slab_rows * occupied, basis_size)
    column_piece = lax.all_gather(vir_coeff, "aux", axis=3, tiled=True)
    coef_real = column_piece[0, 0]
    coef_imag = column_piece[0, 1]
    part_real = matmul(rows_real, coef_real) - matmul(rows_imag, coef_imag)
    part_imag = matmul(rows_real, coef_imag) + matmul(rows_imag, coef_real)
    banded = jnp.stack([part_real, part_imag])
    pair_rows = banded.reshape(2, slab_rows, 1, -1)
    regrouped = lax.all_to_all(pair_rows, "cell", split_axis=3, concat_axis=2, tiled=True)
    source = jnp.argsort(transfer_index)
    return jnp.take(regrouped, source, axis=2)


def split(value):
    high = value.astype(BF16)
    return high, (value - high.astype(F32)).astype(BF16)


def dot(left, right):
    return jnp.dot(left, right, preferred_element_type=F32)


def padded(count, step):
    return -(-count // step) * step


class Sizes:
    def __init__(self, blocks, occ_coeff, vir_coeff):
        self.slab = blocks.shape[1]
        self.basis = blocks.shape[2]
        self.occ = occ_coeff.shape[2]
        self.vir_half = vir_coeff.shape[3]
        self.main = self.basis // LANES * LANES
        self.rest = self.basis - self.main
        self.width = 2 * self.main + LANES
        self.depth = self.main + HALF_LANES
        self.bands = self.occ // KX
        self.rows = padded(self.bands, 8)
        self.chunk = self.vir_half // 2
        self.chunks = 4 * self.bands // KY
        self.tiles = self.chunks // 2 + 1
        self.pairs = self.chunk * self.chunks

    @staticmethod
    def fit(cells, aux, blocks, occ_coeff, vir_coeff):
        basis, occ, half = blocks.shape[2], occ_coeff.shape[2], vir_coeff.shape[3]
        return (
            cells == KX * KY
            and aux == 2
            and blocks.shape[1] == KY
            and occ % KX == 0
            and occ // KX % 2 == 1
            and 0 < basis % LANES <= HALF_LANES
            and basis > LANES
            and half % 2 == 0
            and HALF_LANES - 8 < half // 2 <= HALF_LANES
        )


def half_kernel(sz, block_hbm, occ_hbm, out_ref, block_ref, occ_ref, block_sem, occ_sem):
    count = KX * sz.rows
    occ_copy = pltpu.make_async_copy(occ_hbm, occ_ref, occ_sem)
    block_copy = pltpu.make_async_copy(block_hbm, block_ref, block_sem)
    occ_copy.start()
    block_copy.start()
    place = lax.broadcasted_iota(jnp.int32, (count, sz.occ), 0)
    band = lax.broadcasted_iota(jnp.int32, (count, sz.occ), 1)
    inner = place % sz.rows
    pick = ((place // sz.rows * sz.bands + inner == band) & (inner < sz.bands)).astype(BF16)
    occ_copy.wait()
    terms = [split(occ_ref[:, part]) for part in range(2)]
    left_high = jnp.concatenate([dot(pick, terms[0][0]), -dot(pick, terms[1][0])], axis=0).astype(BF16)
    left_low = jnp.concatenate([dot(pick, terms[0][1]), -dot(pick, terms[1][1])], axis=0).astype(BF16)
    fill = jnp.zeros((sz.basis, LANES - sz.rest), F32)
    block_copy.wait()
    for p in range(sz.slab):
        high, low = split(jnp.concatenate([block_ref[:, p], fill], axis=1))
        half = dot(left_high, high) + dot(left_low, high) + dot(left_high, low)
        real, imag = half[:count], half[count:]
        rest = real[:, sz.main :] + pltpu.roll(imag[:, sz.main :], HALF_LANES, 1)
        for z in range(KX):
            span = slice(z * sz.rows, (z + 1) * sz.rows)
            out_ref[z, p, :, : sz.main] = real[span, : sz.main]
            out_ref[z, p, :, sz.main : 2 * sz.main] = imag[span, : sz.main]
            out_ref[z, p, :, 2 * sz.main :] = rest[span]


def half_bands(sz, blocks, occ_coeff):
    anywhere = pl.BlockSpec(memory_space=pl.ANY)
    return pl.pallas_call(
        functools.partial(half_kernel, sz),
        out_shape=jax.ShapeDtypeStruct((KX, KY, sz.rows, sz.width), F32),
        in_specs=[anywhere, anywhere],
        out_specs=pl.BlockSpec(memory_space=pltpu.VMEM),
        scratch_shapes=[
            pltpu.VMEM((sz.basis, sz.slab, sz.basis), F32),
            pltpu.VMEM((sz.occ, 2, sz.basis), F32),
            pltpu.SemaphoreType.DMA,
            pltpu.SemaphoreType.DMA,
        ],
        compiler_params=pltpu.CompilerParams(vmem_limit_bytes=60 << 20),
        cost_estimate=pl.CostEstimate(flops=10**10, bytes_accessed=60_000_000, transcendentals=0),
    )(blocks[0].transpose(1, 0, 2), occ_coeff.transpose(2, 0, 1))


def four_points(zero, one, two, three, turn):
    even, odd = zero + two, one + three
    lift, lean = zero - two, turn(one - three)
    return even + odd, lift + lean, even - odd, lift - lean


class Pair:
    def __init__(self, real, imag):
        self.real, self.imag = real, imag

    def __add__(self, other):
        return Pair(self.real + other.real, self.imag + other.imag)

    def __sub__(self, other):
        return Pair(self.real - other.real, self.imag - other.imag)

    def turned(self):
        return Pair(-self.imag, self.real)


def lattice_kernel(sz, place_ref, offset_ref, cells_ref, *refs):
    outs, grid_ref, slot_ref = refs[:KY], refs[KY], refs[KY + 1]
    plane, seat = place_ref[0], place_ref[1]
    for cell in range(KX * KY):
        slot_ref[(offset_ref[0, cell] & 3) * KY + (offset_ref[1, cell] & 3)] = cell
    slots = [slot_ref[n] for n in range(KX * KY)]
    real_half = lax.broadcasted_iota(jnp.int32, (8, LANES), 1) < HALF_LANES

    def turn_rest(value):
        moved = pltpu.roll(value, HALF_LANES, 1)
        return jnp.where(real_half, -moved, moved)

    def transform(load, turn, store):
        firsts = [four_points(*[load(slots[n * KY + m]) for n in range(KX)], turn) for m in range(KY)]
        for a in range(KX):
            seconds = four_points(*[firsts[m][a] for m in range(KY)], turn)
            for b in range(KY):
                store(a, b, seconds[b])

    for row in range(0, sz.rows, 8):
        span = slice(row, row + 8)
        for lane in range(0, sz.main, LANES):
            near, far = slice(lane, lane + LANES), slice(sz.main + lane, sz.main + lane + LANES)

            def load(cell):
                return Pair(cells_ref[cell, span, near], cells_ref[cell, span, far])

            def store(a, b, value):
                grid_ref[b, a ^ plane, span, near] = value.real
                grid_ref[b, a ^ plane, span, far] = value.imag

            transform(load, Pair.turned, store)
        tail = slice(2 * sz.main, sz.width)

        def load_rest(cell):
            return cells_ref[cell, span, tail]

        def store_rest(a, b, value):
            grid_ref[b, a ^ plane, span, tail] = value

        transform(load_rest, turn_rest, store_rest)
    for step in range(KY):
        outs[step][...] = grid_ref[step ^ seat]


def lattice_sum(sz, place, cell_offsets, cells):
    shape = jax.ShapeDtypeStruct((KX, sz.rows, sz.width), F32)
    whole = pl.BlockSpec(memory_space=pltpu.VMEM)
    scalars = pl.BlockSpec(memory_space=pltpu.SMEM)
    return pl.pallas_call(
        functools.partial(lattice_kernel, sz),
        out_shape=[shape] * KY,
        in_specs=[scalars, scalars, whole],
        out_specs=[whole] * KY,
        scratch_shapes=[
            pltpu.VMEM((KY, KX, sz.rows, sz.width), F32),
            pltpu.SMEM((KX * KY,), jnp.int32),
        ],
        compiler_params=pltpu.CompilerParams(vmem_limit_bytes=32 << 20),
    )(place, cell_offsets, cells)


def band_kernel(sz, place_ref, *refs):
    halves, rights, outs = refs[:KY], refs[KY : KY + KX], refs[KY + KX : 2 * KY + KX]
    left_ref, band_ref, tile_ref = refs[2 * KY + KX :]
    seat = place_ref[1]
    count = KY * sz.rows
    for step in range(KY):
        left_ref[:, step ^ seat] = halves[step][...]

    for k in range(KX):
        left = left_ref[k].reshape(count, sz.width)
        tail = left[:, 2 * sz.main :]
        near = jnp.concatenate([left[:, : sz.main], left[:, sz.main : 2 * sz.main]], axis=0)
        rest = jnp.concatenate([tail, pltpu.roll(tail, HALF_LANES, 1)], axis=0)[:, :HALF_LANES]
        near_high, near_low = split(near)
        rest_high, rest_low = split(rest)
        high, low = rights[k][0], rights[k][1]
        band = (
            dot(near_high, high[: sz.main])
            + dot(near_low, high[: sz.main])
            + dot(near_high, low[: sz.main])
            + dot(rest_high, high[sz.main :])
            + dot(rest_low, high[sz.main :])
            + dot(rest_high, low[sz.main :])
        )
        width = 2 * LANES
        top, bottom = band[:count], band[count:]
        real = top[:, :width] - bottom[:, width:]
        imag = top[:, width:] + bottom[:, :width]
        for h in range(2):
            lanes = slice(h * LANES, (h + 1) * LANES)
            band_ref[h, 0] = real[:, lanes]
            band_ref[h, 1] = imag[:, lanes]
        for i in range(sz.bands):
            for h in range(2):
                for part in range(2):
                    tile_ref[2 * i + h, part * KY : (part + 1) * KY] = band_ref[
                        h, part, pl.ds(i, KY, stride=sz.rows)
                    ]
        for step in range(KY):
            first = (step ^ seat) * sz.chunks // 2
            for n in range(sz.tiles):
                outs[step][k, n] = tile_ref[first + n]


def band_product(sz, place, halves, rights):
    shape = jax.ShapeDtypeStruct((KX, sz.tiles, 2 * KY, LANES), F32)
    whole = pl.BlockSpec(memory_space=pltpu.VMEM)
    scalars = pl.BlockSpec(memory_space=pltpu.SMEM)
    return pl.pallas_call(
        functools.partial(band_kernel, sz),
        out_shape=[shape] * KY,
        in_specs=[scalars] + [whole] * (KY + KX),
        out_specs=[whole] * KY,
        scratch_shapes=[
            pltpu.VMEM((KX, KY, sz.rows, sz.width), F32),
            pltpu.VMEM((2, 2, KY * sz.rows, LANES), F32),
            pltpu.VMEM((2 * sz.bands, 2 * KY, LANES), F32),
        ],
        compiler_params=pltpu.CompilerParams(vmem_limit_bytes=32 << 20),
    )(place, *halves, *rights)


def regroup_kernel(sz, place_ref, transfer_ref, *refs):
    sources, out_ref, row_ref = refs[:KY], refs[KY], refs[KY + 1]
    plane, seat = place_ref[0], place_ref[1]
    lane = lax.broadcasted_iota(jnp.int32, (2 * KY, LANES), 1)
    cells = KX * KY

    def place_rows(odd):
        for step in range(KY):
            for k in range(KX):
                point = (k ^ plane) * KY + (step ^ seat)
                row = transfer_ref[point]
                for first in range(0, sz.pairs, LANES):
                    last = min(first + LANES, sz.pairs)
                    value = None
                    for u in range(first // sz.chunk, (last - 1) // sz.chunk + 1):
                        tile = sources[step][k, (u + odd) // 2]
                        shift = (sz.chunk * u - HALF_LANES * (u + odd)) % LANES
                        piece = pltpu.roll(tile, shift, 1) if shift else tile
                        value = piece if value is None else jnp.where(lane < sz.chunk * u - first, value, piece)
                    row_ref[first // LANES, pl.ds(row, 2 * KY, stride=cells)] = value

    @pl.when(seat % 2 == 0)
    def _():
        place_rows(0)

    @pl.when(seat % 2 == 1)
    def _():
        place_rows(1)

    for first in range(0, sz.pairs, LANES):
        last = min(first + LANES, sz.pairs)
        out_ref[:, first:last] = row_ref[first // LANES, :, : last - first]


def regroup(sz, place, transfer_index, sources):
    whole = pl.BlockSpec(memory_space=pltpu.VMEM)
    scalars = pl.BlockSpec(memory_space=pltpu.SMEM)
    return pl.pallas_call(
        functools.partial(regroup_kernel, sz),
        out_shape=jax.ShapeDtypeStruct((2 * KY * KX * KY, sz.pairs), F32),
        in_specs=[scalars, scalars] + [whole] * KY,
        out_specs=whole,
        scratch_shapes=[pltpu.VMEM((-(-sz.pairs // LANES), 2 * KY * KX * KY, LANES), F32)],
        compiler_params=pltpu.CompilerParams(vmem_limit_bytes=32 << 20),
    )(place, transfer_index, *sources)


def columns_kernel(sz, place_ref, own_ref, other_ref, out_ref):
    core = place_ref[2]
    low_lanes = lax.broadcasted_iota(jnp.int32, (sz.basis, LANES), 1) < HALF_LANES
    fill = jnp.zeros((sz.basis, LANES - sz.vir_half), F32)
    under = jnp.zeros((sz.depth - sz.basis, LANES), F32)
    for part in range(2):
        sides = []
        for ref in (own_ref, other_ref):
            value = jnp.concatenate([ref[:, part], fill], axis=1)
            value = jnp.where(low_lanes, value, pltpu.roll(value, HALF_LANES - sz.chunk, 1))
            sides.append(jnp.concatenate([value, under], axis=0))
        mine, theirs = sides
        for h, value in enumerate([jnp.where(core == 0, mine, theirs), jnp.where(core == 0, theirs, mine)]):
            lanes = slice((2 * part + h) * LANES, (2 * part + h + 1) * LANES)
            for level, term in enumerate(split(value)):
                out_ref[level, :, lanes] = term


def columns(sz, place, own, other, flops):
    whole = pl.BlockSpec(memory_space=pltpu.VMEM)
    scalars = pl.BlockSpec(memory_space=pltpu.SMEM)
    return pl.pallas_call(
        functools.partial(columns_kernel, sz),
        out_shape=jax.ShapeDtypeStruct((2, sz.depth, 4 * LANES), BF16),
        in_specs=[scalars, whole, whole],
        out_specs=whole,
        compiler_params=pltpu.CompilerParams(vmem_limit_bytes=32 << 20),
        cost_estimate=pl.CostEstimate(flops=flops, bytes_accessed=flops // 100, transcendentals=0),
    )(place, own, other)


def hold_kernel(in_ref, out_ref):
    del in_ref, out_ref


def hold(value):
    return pl.pallas_call(
        hold_kernel,
        out_shape=jax.ShapeDtypeStruct(value.shape, value.dtype),
        in_specs=[pl.BlockSpec(memory_space=pl.ANY)],
        out_specs=pl.BlockSpec(memory_space=pl.ANY),
        input_output_aliases={0: 0},
        cost_estimate=pl.CostEstimate(flops=10**10, bytes_accessed=10**8, transcendentals=0),
    )(value)


def swap(value, step):
    return lax.ppermute(value, "cell", [(d, d ^ step) for d in range(KX * KY)])


def swap_cores(value):
    return lax.ppermute(value, "aux", [(0, 1), (1, 0)])


def by_planes(blocks, cell_offsets, occ_coeff, vir_coeff, transfer_index):
    sz = Sizes(blocks, occ_coeff, vir_coeff)
    me = lax.axis_index("cell")
    place = jnp.stack([me // KY, me % KY, lax.axis_index("aux")]).astype(jnp.int32)
    home = vir_coeff[0].transpose(1, 0, 2)
    across = hold(swap(home, 2 * KY))
    beside = hold(swap(home, KY))
    sent = half_bands(sz, blocks, occ_coeff).reshape(KX * KY, sz.rows, sz.width)
    cells = lax.all_to_all(sent, "cell", split_axis=0, concat_axis=0, tiled=True)
    corner = swap(across, KY)
    ours, beside = lax.optimization_barrier((home, beside))
    long, short = 10**10, 10**6
    rights = [
        columns(sz, place, ours, swap_cores(ours), long),
        columns(sz, place, beside, swap_cores(beside), long),
        columns(sz, place, across, swap_cores(across), long),
    ]
    cells, *rights = lax.optimization_barrier((cells, *rights))
    points = list(lattice_sum(sz, place, cell_offsets, cells))
    corner, points[0] = lax.optimization_barrier((corner, points[0]))
    rights.append(columns(sz, place, corner, swap_cores(corner), short))
    halves = [points[0]] + [swap(points[s], s) for s in range(1, KY)]
    halves[1] = hold(halves[1])
    bands = band_product(sz, place, halves, rights)
    sources = [bands[0]] + [swap(bands[s], s) for s in range(1, KY)]
    out = regroup(sz, place, transfer_index, sources)
    return out.reshape(2, sz.slab, KX * KY, sz.pairs)


def on_device(blocks, cell_offsets, occ_coeff, vir_coeff, transfer_index):
    arrays = (blocks, cell_offsets, occ_coeff, vir_coeff, transfer_index)
    if Sizes.fit(lax.axis_size("cell"), lax.axis_size("aux"), blocks, occ_coeff, vir_coeff):
        return by_planes(*arrays)
    return by_entries(*arrays)


def solution(mesh):
    placed = (P("cell", "aux", None, None), P(), P(), P("cell", None, None, "aux"), P())
    return jax.shard_map(
        on_device,
        mesh=mesh,
        in_specs=placed,
        out_specs=P(None, "aux", None, "cell"),
        check_vma=False,
    )
```

```python
import functools
import math

import jax
import jax.numpy as jnp
from jax import lax
from jax.experimental import pallas as pl
from jax.experimental.pallas import tpu as pltpu
from jax.sharding import PartitionSpec as P

KX = 4
KY = 4
LANES = 128
HALF_LANES = 64
SEGMENT = 32
PIECE = 4
SUBLANES = 8
SEGMENTS = LANES // SEGMENT
BF16 = jnp.bfloat16
F32 = jnp.float32


def phase_tables(cell_offsets, cell_count):
    depth = cell_count // (KX * KY)
    points = jnp.arange(cell_count, dtype=jnp.int32)
    along_a = points // (KY * depth)
    along_b = points // depth % KY
    along_c = points % depth
    turns = (
        along_a[:, None] * cell_offsets[0][None, :] * (KY * depth)
        + along_b[:, None] * cell_offsets[1][None, :] * (KX * depth)
        + along_c[:, None] * cell_offsets[2][None, :] * (KX * KY)
    ) % cell_count
    angles = 2.0 * math.pi / cell_count * turns.astype(jnp.float32)
    return (jnp.cos(angles), jnp.sin(angles))


def matmul(left, right):
    return jnp.dot(left, right, precision=lax.Precision.HIGHEST, preferred_element_type=jnp.float32)


def contract(form, left, right):
    return jnp.einsum(form, left, right, precision=lax.Precision.HIGHEST)


def by_entries(blocks, cell_offsets, occ_coeff, vir_coeff, transfer_index):
    cell_count = lax.axis_size("cell")
    slab_rows = blocks.shape[1]
    basis_size = blocks.shape[2]
    occupied = occ_coeff.shape[2]
    cosines, sines = phase_tables(cell_offsets, cell_count)
    occ_real, occ_imag = (occ_coeff[0], occ_coeff[1])
    flattened = blocks.reshape(1, -1)
    arrived = lax.all_to_all(flattened, "cell", split_axis=1, concat_axis=0, tiled=True)
    grid_real = matmul(cosines, arrived)
    grid_imag = matmul(sines, arrived)
    back_real, back_imag = (
        lax.all_to_all(grid_real, "cell", split_axis=0, concat_axis=1, tiled=True),
        lax.all_to_all(grid_imag, "cell", split_axis=0, concat_axis=1, tiled=True),
    )
    spec_real = back_real.reshape(slab_rows, basis_size, basis_size)
    spec_imag = back_imag.reshape(slab_rows, basis_size, basis_size)
    half_real = contract("mi,pmn->pin", occ_real, spec_real) + contract(
        "mi,pmn->pin", occ_imag, spec_imag
    )
    half_imag = contract("mi,pmn->pin", occ_real, spec_imag) - contract(
        "mi,pmn->pin", occ_imag, spec_real
    )
    rows_real = half_real.reshape(slab_rows * occupied, basis_size)
    rows_imag = half_imag.reshape(slab_rows * occupied, basis_size)
    column_piece = lax.all_gather(vir_coeff, "aux", axis=3, tiled=True)
    coef_real = column_piece[0, 0]
    coef_imag = column_piece[0, 1]
    part_real = matmul(rows_real, coef_real) - matmul(rows_imag, coef_imag)
    part_imag = matmul(rows_real, coef_imag) + matmul(rows_imag, coef_real)
    banded = jnp.stack([part_real, part_imag])
    pair_rows = banded.reshape(2, slab_rows, 1, -1)
    regrouped = lax.all_to_all(pair_rows, "cell", split_axis=3, concat_axis=2, tiled=True)
    source = jnp.argsort(transfer_index)
    return jnp.take(regrouped, source, axis=2)


def split(value):
    high = value.astype(BF16)
    return high, (value - high.astype(F32)).astype(BF16)


def dot(left, right):
    return jnp.dot(left, right, preferred_element_type=F32)


class Sizes:
    def __init__(self, blocks, occ_coeff, vir_coeff):
        self.slab = blocks.shape[1]
        self.basis = blocks.shape[2]
        self.occ = occ_coeff.shape[2]
        self.vir_half = vir_coeff.shape[3]
        self.main = self.basis // LANES * LANES
        self.rest = self.basis - self.main
        self.columns = self.main // LANES
        self.gap = HALF_LANES - self.rest
        self.depth = 2 * self.main + 3 * HALF_LANES
        self.bands = self.occ // KX
        self.rows = 2 * SUBLANES
        self.tail = 4 * self.columns
        self.chunk = self.vir_half // 2
        self.chunks = 4 * self.bands // KY
        self.tiles = self.chunks // 2 + 1
        self.pairs = self.chunk * self.chunks

    @staticmethod
    def fit(cells, aux, blocks, occ_coeff, vir_coeff):
        basis, occ, half = blocks.shape[2], occ_coeff.shape[2], vir_coeff.shape[3]
        return (
            cells == KX * KY
            and aux == 2
            and blocks.shape[1] == KY
            and occ % KX == 0
            and occ // KX % 2 == 1
            and basis > LANES
            and HALF_LANES // 2 <= basis % LANES <= HALF_LANES // 2 + SEGMENT // 2
            and SUBLANES <= occ // KX < 2 * SUBLANES
            and occ // KX - SUBLANES <= basis // LANES * (LANES // SEGMENT)
            and half % 2 == 0
            and HALF_LANES - 8 < half // 2 <= HALF_LANES
        )


def staggered(tile, row, first, stride):
    out = pltpu.roll(tile, first % LANES, 1)
    for r in range(1, SEGMENTS):
        out = jnp.where(row % SEGMENTS == r, pltpu.roll(tile, (first + r * stride) % LANES, 1), out)
    return out


def half_kernel(sz, block_hbm, occ_hbm, out_hbm, block_ref, occ_ref, out_ref, block_sem, occ_sem, out_sem):
    count = KX * sz.rows
    occ_copy = pltpu.make_async_copy(occ_hbm, occ_ref, occ_sem)
    block_copy = pltpu.make_async_copy(block_hbm, block_ref, block_sem)
    occ_copy.start()
    block_copy.start()
    place = lax.broadcasted_iota(jnp.int32, (count, sz.occ), 0)
    band = lax.broadcasted_iota(jnp.int32, (count, sz.occ), 1)
    inner = place % sz.rows
    pick = ((place // sz.rows * sz.bands + inner == band) & (inner < sz.bands)).astype(BF16)
    occ_copy.wait()
    terms = [split(occ_ref[:, part]) for part in range(2)]
    left_high = jnp.concatenate([dot(pick, terms[0][0]), -dot(pick, terms[1][0])], axis=0).astype(BF16)
    left_low = jnp.concatenate([dot(pick, terms[0][1]), -dot(pick, terms[1][1])], axis=0).astype(BF16)
    left = jnp.concatenate([left_high, left_low], axis=0)
    fill = jnp.zeros((sz.basis, LANES - sz.rest), F32)
    row = lax.broadcasted_iota(jnp.int32, (SUBLANES, LANES), 0)
    lane = lax.broadcasted_iota(jnp.int32, (SUBLANES, LANES), 1)
    block_copy.wait()
    for p in range(sz.slab):
        high, low = split(jnp.concatenate([block_ref[:, p], fill], axis=1))
        half = dot(left, high)
        half = half[: 2 * count] + half[2 * count :] + dot(left_high, low)
        real, imag = half[:count], half[count:]
        for z in range(KX):
            near = slice(z * sz.rows, z * sz.rows + SUBLANES)
            far = slice(z * sz.rows + SUBLANES, (z + 1) * sz.rows)
            tails = []
            for part, value in enumerate((real, imag)):
                head, last = value[near, sz.main :], value[far, sz.main :]
                tails.append(head + pltpu.roll(jnp.where(lane < sz.gap, last, 0.0), sz.rest, 1))
                spare = jnp.where(lane < sz.gap, 0.0, last)
                spare = staggered(spare, row, LANES - sz.gap, SEGMENT)
                for c in range(sz.columns):
                    lanes = slice(c * LANES, (c + 1) * LANES)
                    rows = slice(c * SEGMENTS, (c + 1) * SEGMENTS)
                    kept = jnp.sum(spare[rows], axis=0, keepdims=True)
                    tile = part * sz.columns + c
                    out_ref[z, p, tile] = value[near, lanes]
                    out_ref[z, p, 2 * sz.columns + tile] = jnp.where(row == SUBLANES - 1, kept, value[far, lanes])
            out_ref[z, p, sz.tail] = tails[0] + pltpu.roll(tails[1], HALF_LANES, 1)
        pltpu.make_async_copy(out_ref.at[:, p], out_hbm.at[:, p], out_sem.at[p]).start()
    for p in range(sz.slab):
        pltpu.make_async_copy(out_ref.at[:, p], out_hbm.at[:, p], out_sem.at[p]).wait()


def half_bands(sz, blocks, occ_coeff):
    anywhere = pl.BlockSpec(memory_space=pl.ANY)
    return pl.pallas_call(
        functools.partial(half_kernel, sz),
        out_shape=jax.ShapeDtypeStruct((KX, KY, sz.tail + 1, SUBLANES, LANES), F32),
        in_specs=[anywhere, anywhere],
        out_specs=anywhere,
        scratch_shapes=[
            pltpu.VMEM((sz.basis, sz.slab, sz.basis), F32),
            pltpu.VMEM((sz.occ, 2, sz.basis), F32),
            pltpu.VMEM((KX, KY, sz.tail + 1, SUBLANES, LANES), F32),
            pltpu.SemaphoreType.DMA,
            pltpu.SemaphoreType.DMA,
            pltpu.SemaphoreType.DMA((sz.slab,)),
        ],
        compiler_params=pltpu.CompilerParams(vmem_limit_bytes=60 << 20),
        cost_estimate=pl.CostEstimate(flops=10**10, bytes_accessed=60_000_000, transcendentals=0),
    )(blocks[0].transpose(1, 0, 2), occ_coeff.transpose(2, 0, 1))


def four_points(zero, one, two, three, turn):
    even, odd = zero + two, one + three
    lift, lean = zero - two, turn(one - three)
    return even + odd, lift + lean, even - odd, lift - lean


class Pair:
    def __init__(self, real, imag):
        self.real, self.imag = real, imag

    def __add__(self, other):
        return Pair(self.real + other.real, self.imag + other.imag)

    def __sub__(self, other):
        return Pair(self.real - other.real, self.imag - other.imag)

    def turned(self):
        return Pair(-self.imag, self.real)


def lattice_kernel(sz, place_ref, offset_ref, cells_ref, *refs):
    outs, grid_ref, slot_ref = refs[:KY], refs[KY], refs[KY + 1]
    plane, seat = place_ref[0], place_ref[1]
    for cell in range(KX * KY):
        slot_ref[(offset_ref[0, cell] & 3) * KY + (offset_ref[1, cell] & 3)] = cell
    slots = [slot_ref[n] for n in range(KX * KY)]
    real_half = lax.broadcasted_iota(jnp.int32, (SUBLANES, LANES), 1) < HALF_LANES

    def turn_rest(value):
        moved = pltpu.roll(value, HALF_LANES, 1)
        return jnp.where(real_half, -moved, moved)

    def transform(load, turn, store):
        firsts = [four_points(*[load(slots[n * KY + m]) for n in range(KX)], turn) for m in range(KY)]
        for a in range(KX):
            seconds = four_points(*[firsts[m][a] for m in range(KY)], turn)
            for b in range(KY):
                store(a, b, seconds[b])

    for h in range(2):
        for c in range(sz.columns):
            near = 2 * sz.columns * h + c
            far = near + sz.columns

            def load(cell):
                return Pair(cells_ref[cell, near], cells_ref[cell, far])

            def store(a, b, value):
                grid_ref[b, a ^ plane, near] = value.real
                grid_ref[b, a ^ plane, far] = value.imag

            transform(load, Pair.turned, store)

    def load_rest(cell):
        return cells_ref[cell, sz.tail]

    def store_rest(a, b, value):
        grid_ref[b, a ^ plane, sz.tail] = value

    transform(load_rest, turn_rest, store_rest)
    for step in range(KY):
        outs[step][...] = grid_ref[step ^ seat]


def lattice_sum(sz, place, cell_offsets, cells):
    shape = jax.ShapeDtypeStruct((KX, sz.tail + 1, SUBLANES, LANES), F32)
    whole = pl.BlockSpec(memory_space=pltpu.VMEM)
    scalars = pl.BlockSpec(memory_space=pltpu.SMEM)
    return pl.pallas_call(
        functools.partial(lattice_kernel, sz),
        out_shape=[shape] * KY,
        in_specs=[scalars, scalars, whole],
        out_specs=[whole] * KY,
        scratch_shapes=[
            pltpu.VMEM((KY, KX, sz.tail + 1, SUBLANES, LANES), F32),
            pltpu.SMEM((KX * KY,), jnp.int32),
        ],
        compiler_params=pltpu.CompilerParams(vmem_limit_bytes=32 << 20),
    )(place, cell_offsets, cells)


def band_kernel(sz, place_ref, *refs):
    halves, rights, outs = refs[:KY], refs[KY : KY + KX], refs[KY + KX : 2 * KY + KX]
    left_ref, band_ref, tile_ref = refs[2 * KY + KX :]
    seat = place_ref[1]
    count = KY * sz.rows
    row = lax.broadcasted_iota(jnp.int32, (SUBLANES, LANES), 0)
    lane = lax.broadcasted_iota(jnp.int32, (SUBLANES, LANES), 1)
    low_lanes = lax.broadcasted_iota(jnp.int32, (2 * count, LANES), 1) < HALF_LANES
    for step in range(KY):
        left_ref[:, step ^ seat] = halves[step][...]

    for k in range(KX):
        left = left_ref[k]
        near, rest = [], []
        for part in range(2):
            tiles = []
            for c in range(sz.columns):
                first = part * sz.columns + c
                halves_of = [left[:, first], left[:, 2 * sz.columns + first]]
                tiles.append(jnp.stack(halves_of, axis=1).reshape(count, LANES))
            near.append(jnp.concatenate(tiles, axis=1))
            for p in range(KY):
                tail = left[p, sz.tail]
                head = pltpu.roll(tail, HALF_LANES, 1) if part else tail
                kept = [left[p, 2 * sz.columns + part * sz.columns + c] for c in range(sz.columns)]
                spare = jnp.concatenate(
                    [jnp.broadcast_to(tile[SUBLANES - 1 :], (SEGMENTS, LANES)) for tile in kept], axis=0
                )[:SUBLANES]
                spare = staggered(spare, row, sz.gap, LANES - SEGMENT)
                rest += [head, jnp.where(lane < sz.gap, pltpu.roll(head, LANES - sz.rest, 1), spare)]
        near_high, near_low = split(jnp.concatenate(near, axis=0))
        rest_high = jnp.concatenate(rest, axis=0)
        rest_low = rest_high - rest_high.astype(BF16).astype(F32)
        both = jnp.where(low_lanes, rest_high, pltpu.roll(rest_low, HALF_LANES, 1)).astype(BF16)
        rest_three = jnp.concatenate([both, rest_high.astype(BF16)[:, :HALF_LANES]], axis=1)
        right = rights[k]
        band = dot(jnp.concatenate([near_high, near_low], axis=0), right[: sz.main])
        band = band[: 2 * count] + band[2 * count :]
        band += dot(near_high, right[sz.main : 2 * sz.main]) + dot(rest_three, right[2 * sz.main :])
        width = 2 * LANES
        top, bottom = band[:count], band[count:]
        real = top[:, :width] - bottom[:, width:]
        imag = top[:, width:] + bottom[:, :width]
        for h in range(2):
            lanes = slice(h * LANES, (h + 1) * LANES)
            band_ref[h, 0] = real[:, lanes]
            band_ref[h, 1] = imag[:, lanes]
        for i in range(sz.bands):
            for h in range(2):
                for part in range(2):
                    tile_ref[2 * i + h, part * KY : (part + 1) * KY] = band_ref[
                        h, part, pl.ds(i, KY, stride=sz.rows)
                    ]
        for step in range(KY):
            first = (step ^ seat) * sz.chunks // 2
            for n in range(sz.tiles):
                outs[step][k, n] = tile_ref[first + n]


def band_product(sz, place, halves, rights):
    shape = jax.ShapeDtypeStruct((KX, sz.tiles, 2 * KY, LANES), F32)
    whole = pl.BlockSpec(memory_space=pltpu.VMEM)
    scalars = pl.BlockSpec(memory_space=pltpu.SMEM)
    return pl.pallas_call(
        functools.partial(band_kernel, sz),
        out_shape=[shape] * KY,
        in_specs=[scalars] + [whole] * (KY + KX),
        out_specs=[whole] * KY,
        scratch_shapes=[
            pltpu.VMEM((KX, KY, sz.tail + 1, SUBLANES, LANES), F32),
            pltpu.VMEM((2, 2, KY * sz.rows, LANES), F32),
            pltpu.VMEM((2 * sz.bands, 2 * KY, LANES), F32),
        ],
        compiler_params=pltpu.CompilerParams(vmem_limit_bytes=32 << 20),
    )(place, *halves, *rights)


def regroup_kernel(sz, place_ref, transfer_ref, *refs):
    sources, out_hbm = refs[:KY], refs[KY]
    row_ref, out_ref, sems = refs[KY + 1 :]
    plane, seat = place_ref[0], place_ref[1]
    lane = lax.broadcasted_iota(jnp.int32, (2 * KY, LANES), 1)
    cells = KX * KY
    starts = list(range(0, sz.pairs, LANES))
    pieces = [starts[i : i + PIECE] for i in range(0, len(starts), PIECE)]
    targets = [
        transfer_ref[(k ^ plane) * KY + (step ^ seat)] for step in range(KY) for k in range(KX)
    ]

    def piece_copy(index):
        first = pieces[index][0]
        span = pl.ds(first, min(pieces[index][-1] + LANES, sz.pairs) - first)
        return pltpu.make_async_copy(out_ref.at[:, span], out_hbm.at[:, span], sems.at[index])

    def place_rows(odd):
        for index, piece in enumerate(pieces):
            for first in piece:
                last = min(first + LANES, sz.pairs)
                for source, row in enumerate(targets):
                    step, k = divmod(source, KX)
                    value = None
                    for u in range(first // sz.chunk, (last - 1) // sz.chunk + 1):
                        tile = sources[step][k, (u + odd) // 2]
                        shift = (sz.chunk * u - HALF_LANES * (u + odd)) % LANES
                        moved = pltpu.roll(tile, shift, 1) if shift else tile
                        value = moved if value is None else jnp.where(lane < sz.chunk * u - first, value, moved)
                    row_ref[first // LANES, pl.ds(row, 2 * KY, stride=cells)] = value
                out_ref[:, first:last] = row_ref[first // LANES, :, : last - first]
            piece_copy(index).start()

    @pl.when(seat % 2 == 0)
    def _():
        place_rows(0)

    @pl.when(seat % 2 == 1)
    def _():
        place_rows(1)

    for index in range(len(pieces)):
        piece_copy(index).wait()


def regroup(sz, place, transfer_index, sources):
    whole = pl.BlockSpec(memory_space=pltpu.VMEM)
    scalars = pl.BlockSpec(memory_space=pltpu.SMEM)
    rows = 2 * KY * KX * KY
    tiles = -(-sz.pairs // LANES)
    return pl.pallas_call(
        functools.partial(regroup_kernel, sz),
        out_shape=jax.ShapeDtypeStruct((rows, sz.pairs), F32),
        in_specs=[scalars, scalars] + [whole] * KY,
        out_specs=pl.BlockSpec(memory_space=pl.ANY),
        scratch_shapes=[
            pltpu.VMEM((tiles, rows, LANES), F32),
            pltpu.VMEM((rows, sz.pairs), F32),
            pltpu.SemaphoreType.DMA((-(-tiles // PIECE),)),
        ],
        compiler_params=pltpu.CompilerParams(vmem_limit_bytes=32 << 20),
    )(place, transfer_index, *sources)


def spread_kernel(sz, in_ref, out_ref):
    low_lanes = lax.broadcasted_iota(jnp.int32, (sz.basis, LANES), 1) < HALF_LANES
    fill = jnp.zeros((sz.basis, LANES - sz.vir_half), F32)
    for part in range(2):
        value = jnp.concatenate([in_ref[:, part], fill], axis=1)
        out_ref[part] = jnp.where(low_lanes, value, pltpu.roll(value, HALF_LANES - sz.chunk, 1))


def spread(sz, value, flops):
    whole = pl.BlockSpec(memory_space=pltpu.VMEM)
    return pl.pallas_call(
        functools.partial(spread_kernel, sz),
        out_shape=jax.ShapeDtypeStruct((2, sz.basis, LANES), F32),
        in_specs=[whole],
        out_specs=whole,
        compiler_params=pltpu.CompilerParams(vmem_limit_bytes=32 << 20),
        cost_estimate=pl.CostEstimate(flops=flops, bytes_accessed=flops // 100, transcendentals=0),
    )(value)


def columns_kernel(sz, place_ref, own_ref, other_ref, out_ref):
    core = place_ref[2]
    under = jnp.zeros((sz.gap, LANES), F32)
    for part in range(2):
        mine, theirs = [jnp.concatenate([ref[part], under], axis=0) for ref in (own_ref, other_ref)]
        for h, value in enumerate([jnp.where(core == 0, mine, theirs), jnp.where(core == 0, theirs, mine)]):
            lanes = slice((2 * part + h) * LANES, (2 * part + h + 1) * LANES)
            high, low = split(value)
            out_ref[: sz.main, lanes] = high[: sz.main]
            out_ref[sz.main : 2 * sz.main, lanes] = low[: sz.main]
            for place, term in enumerate((high, high, low)):
                first = 2 * sz.main + place * HALF_LANES
                out_ref[first : first + HALF_LANES, lanes] = term[sz.main :]


def columns(sz, place, own, other, flops):
    whole = pl.BlockSpec(memory_space=pltpu.VMEM)
    scalars = pl.BlockSpec(memory_space=pltpu.SMEM)
    return pl.pallas_call(
        functools.partial(columns_kernel, sz),
        out_shape=jax.ShapeDtypeStruct((sz.depth, 4 * LANES), BF16),
        in_specs=[scalars, whole, whole],
        out_specs=whole,
        compiler_params=pltpu.CompilerParams(vmem_limit_bytes=32 << 20),
        cost_estimate=pl.CostEstimate(flops=flops, bytes_accessed=flops // 100, transcendentals=0),
    )(place, own, other)


def swap(value, step):
    return lax.ppermute(value, "cell", [(d, d ^ step) for d in range(KX * KY)])


def swap_cores(value):
    return lax.ppermute(value, "aux", [(0, 1), (1, 0)])


def by_planes(blocks, cell_offsets, occ_coeff, vir_coeff, transfer_index):
    sz = Sizes(blocks, occ_coeff, vir_coeff)
    me = lax.axis_index("cell")
    place = jnp.stack([me // KY, me % KY, lax.axis_index("aux")]).astype(jnp.int32)
    long, short = 10**10, 10**6
    home = vir_coeff[0].transpose(1, 0, 2)
    across = spread(sz, swap(home, 2 * KY), long)
    beside = spread(sz, swap(home, KY), long)
    corner = swap(across, KY)
    ours = spread(sz, home, short)
    rights = [columns(sz, place, v, swap_cores(v), short) for v in (ours, beside, across)]
    sent = half_bands(sz, blocks, occ_coeff).reshape(KX * KY, sz.tail + 1, SUBLANES, LANES)
    cells = lax.all_to_all(sent, "cell", split_axis=0, concat_axis=0, tiled=True)
    points = list(lattice_sum(sz, place, cell_offsets, cells))
    rights.append(columns(sz, place, corner, swap_cores(corner), short))
    halves = [points[0]] + [swap(points[s], s) for s in range(1, KY)]
    bands = band_product(sz, place, halves, rights)
    sources = [bands[0]] + [swap(bands[s], s) for s in range(1, KY)]
    out = regroup(sz, place, transfer_index, sources)
    return out.reshape(2, sz.slab, KX * KY, sz.pairs)


def on_device(blocks, cell_offsets, occ_coeff, vir_coeff, transfer_index):
    arrays = (blocks, cell_offsets, occ_coeff, vir_coeff, transfer_index)
    if Sizes.fit(lax.axis_size("cell"), lax.axis_size("aux"), blocks, occ_coeff, vir_coeff):
        return by_planes(*arrays)
    return by_entries(*arrays)


def solution(mesh):
    placed = (P("cell", "aux", None, None), P(), P(), P("cell", None, None, "aux"), P())
    return jax.shard_map(
        on_device,
        mesh=mesh,
        in_specs=placed,
        out_specs=P(None, "aux", None, "cell"),
        check_vma=False,
    )
```

```python
import functools
import math

import jax
import jax.numpy as jnp
from jax import lax
from jax.experimental import pallas as pl
from jax.experimental.pallas import tpu as pltpu
from jax.sharding import PartitionSpec as P

KX = 4
KY = 4
LANES = 128
HALF_LANES = 64
SEGMENT = 32
PIECE = 4
SUBLANES = 8
SEGMENTS = LANES // SEGMENT
BF16 = jnp.bfloat16
F32 = jnp.float32


def phase_tables(cell_offsets, cell_count):
    depth = cell_count // (KX * KY)
    points = jnp.arange(cell_count, dtype=jnp.int32)
    along_a = points // (KY * depth)
    along_b = points // depth % KY
    along_c = points % depth
    turns = (
        along_a[:, None] * cell_offsets[0][None, :] * (KY * depth)
        + along_b[:, None] * cell_offsets[1][None, :] * (KX * depth)
        + along_c[:, None] * cell_offsets[2][None, :] * (KX * KY)
    ) % cell_count
    angles = 2.0 * math.pi / cell_count * turns.astype(jnp.float32)
    return (jnp.cos(angles), jnp.sin(angles))


def matmul(left, right):
    return jnp.dot(left, right, precision=lax.Precision.HIGHEST, preferred_element_type=jnp.float32)


def contract(form, left, right):
    return jnp.einsum(form, left, right, precision=lax.Precision.HIGHEST)


def by_entries(blocks, cell_offsets, occ_coeff, vir_coeff, transfer_index):
    cell_count = lax.axis_size("cell")
    slab_rows = blocks.shape[1]
    basis_size = blocks.shape[2]
    occupied = occ_coeff.shape[2]
    cosines, sines = phase_tables(cell_offsets, cell_count)
    occ_real, occ_imag = (occ_coeff[0], occ_coeff[1])
    flattened = blocks.reshape(1, -1)
    arrived = lax.all_to_all(flattened, "cell", split_axis=1, concat_axis=0, tiled=True)
    grid_real = matmul(cosines, arrived)
    grid_imag = matmul(sines, arrived)
    back_real, back_imag = (
        lax.all_to_all(grid_real, "cell", split_axis=0, concat_axis=1, tiled=True),
        lax.all_to_all(grid_imag, "cell", split_axis=0, concat_axis=1, tiled=True),
    )
    spec_real = back_real.reshape(slab_rows, basis_size, basis_size)
    spec_imag = back_imag.reshape(slab_rows, basis_size, basis_size)
    half_real = contract("mi,pmn->pin", occ_real, spec_real) + contract(
        "mi,pmn->pin", occ_imag, spec_imag
    )
    half_imag = contract("mi,pmn->pin", occ_real, spec_imag) - contract(
        "mi,pmn->pin", occ_imag, spec_real
    )
    rows_real = half_real.reshape(slab_rows * occupied, basis_size)
    rows_imag = half_imag.reshape(slab_rows * occupied, basis_size)
    column_piece = lax.all_gather(vir_coeff, "aux", axis=3, tiled=True)
    coef_real = column_piece[0, 0]
    coef_imag = column_piece[0, 1]
    part_real = matmul(rows_real, coef_real) - matmul(rows_imag, coef_imag)
    part_imag = matmul(rows_real, coef_imag) + matmul(rows_imag, coef_real)
    banded = jnp.stack([part_real, part_imag])
    pair_rows = banded.reshape(2, slab_rows, 1, -1)
    regrouped = lax.all_to_all(pair_rows, "cell", split_axis=3, concat_axis=2, tiled=True)
    source = jnp.argsort(transfer_index)
    return jnp.take(regrouped, source, axis=2)


def cost(flops):
    return pl.CostEstimate(flops=flops, bytes_accessed=flops // 100, transcendentals=0)


def split(value):
    high = value.astype(BF16)
    return high, (value - high.astype(F32)).astype(BF16)


def dot(left, right):
    return jnp.dot(left, right, preferred_element_type=F32)


class Sizes:
    def __init__(self, blocks, occ_coeff, vir_coeff):
        self.slab = blocks.shape[1]
        self.basis = blocks.shape[2]
        self.occ = occ_coeff.shape[2]
        self.vir_half = vir_coeff.shape[3]
        self.main = self.basis // LANES * LANES
        self.rest = self.basis - self.main
        self.columns = self.main // LANES
        self.gap = HALF_LANES - self.rest
        self.depth = 2 * self.main + 3 * HALF_LANES
        self.bands = self.occ // KX
        self.rows = 2 * SUBLANES
        self.tail = 4 * self.columns
        self.chunk = self.vir_half // 2
        self.chunks = 4 * self.bands // KY
        self.tiles = self.chunks // 2 + 1
        self.pairs = self.chunk * self.chunks

    @staticmethod
    def fit(cells, aux, blocks, occ_coeff, vir_coeff):
        basis, occ, half = blocks.shape[2], occ_coeff.shape[2], vir_coeff.shape[3]
        return (
            cells == KX * KY
            and aux == 2
            and blocks.shape[1] == KY
            and occ % KX == 0
            and occ // KX % 2 == 1
            and basis > LANES
            and HALF_LANES // 2 <= basis % LANES <= HALF_LANES // 2 + SEGMENT // 2
            and SUBLANES <= occ // KX < 2 * SUBLANES
            and occ // KX - SUBLANES <= basis // LANES * (LANES // SEGMENT)
            and half % 2 == 0
            and HALF_LANES - 8 < half // 2 <= HALF_LANES
        )


def staggered(tile, row, first, stride):
    out = pltpu.roll(tile, first % LANES, 1)
    for r in range(1, SEGMENTS):
        out = jnp.where(row % SEGMENTS == r, pltpu.roll(tile, (first + r * stride) % LANES, 1), out)
    return out


def half_kernel(sz, block_hbm, occ_hbm, out_hbm, block_ref, occ_ref, out_ref, block_sem, occ_sem, out_sem):
    count = KX * sz.rows
    occ_copy = pltpu.make_async_copy(occ_hbm, occ_ref, occ_sem)
    block_copy = pltpu.make_async_copy(block_hbm, block_ref, block_sem)
    occ_copy.start()
    block_copy.start()
    place = lax.broadcasted_iota(jnp.int32, (count, sz.occ), 0)
    band = lax.broadcasted_iota(jnp.int32, (count, sz.occ), 1)
    inner = place % sz.rows
    pick = ((place // sz.rows * sz.bands + inner == band) & (inner < sz.bands)).astype(BF16)
    occ_copy.wait()
    terms = [split(occ_ref[:, part]) for part in range(2)]
    left_high = jnp.concatenate([dot(pick, terms[0][0]), -dot(pick, terms[1][0])], axis=0).astype(BF16)
    left_low = jnp.concatenate([dot(pick, terms[0][1]), -dot(pick, terms[1][1])], axis=0).astype(BF16)
    left = jnp.concatenate([left_high, left_low], axis=0)
    fill = jnp.zeros((sz.basis, LANES - sz.rest), F32)
    row = lax.broadcasted_iota(jnp.int32, (SUBLANES, LANES), 0)
    lane = lax.broadcasted_iota(jnp.int32, (SUBLANES, LANES), 1)
    block_copy.wait()
    for p in range(sz.slab):
        high, low = split(jnp.concatenate([block_ref[:, p], fill], axis=1))
        half = dot(left, high)
        half = half[: 2 * count] + half[2 * count :] + dot(left_high, low)
        real, imag = half[:count], half[count:]
        for z in range(KX):
            near = slice(z * sz.rows, z * sz.rows + SUBLANES)
            far = slice(z * sz.rows + SUBLANES, (z + 1) * sz.rows)
            tails = []
            for part, value in enumerate((real, imag)):
                head, last = value[near, sz.main :], value[far, sz.main :]
                tails.append(head + pltpu.roll(jnp.where(lane < sz.gap, last, 0.0), sz.rest, 1))
                spare = jnp.where(lane < sz.gap, 0.0, last)
                spare = staggered(spare, row, LANES - sz.gap, SEGMENT)
                for c in range(sz.columns):
                    lanes = slice(c * LANES, (c + 1) * LANES)
                    rows = slice(c * SEGMENTS, (c + 1) * SEGMENTS)
                    kept = jnp.sum(spare[rows], axis=0, keepdims=True)
                    tile = part * sz.columns + c
                    out_ref[z, p, tile] = value[near, lanes]
                    out_ref[z, p, 2 * sz.columns + tile] = jnp.where(row == SUBLANES - 1, kept, value[far, lanes])
            out_ref[z, p, sz.tail] = tails[0] + pltpu.roll(tails[1], HALF_LANES, 1)
        pltpu.make_async_copy(out_ref.at[:, p], out_hbm.at[:, p], out_sem.at[p]).start()
    for p in range(sz.slab):
        pltpu.make_async_copy(out_ref.at[:, p], out_hbm.at[:, p], out_sem.at[p]).wait()


def half_bands(sz, blocks, occ_coeff):
    anywhere = pl.BlockSpec(memory_space=pl.ANY)
    return pl.pallas_call(
        functools.partial(half_kernel, sz),
        out_shape=jax.ShapeDtypeStruct((KX, KY, sz.tail + 1, SUBLANES, LANES), F32),
        in_specs=[anywhere, anywhere],
        out_specs=anywhere,
        scratch_shapes=[
            pltpu.VMEM((sz.basis, sz.slab, sz.basis), F32),
            pltpu.VMEM((sz.occ, 2, sz.basis), F32),
            pltpu.VMEM((KX, KY, sz.tail + 1, SUBLANES, LANES), F32),
            pltpu.SemaphoreType.DMA,
            pltpu.SemaphoreType.DMA,
            pltpu.SemaphoreType.DMA((sz.slab,)),
        ],
        compiler_params=pltpu.CompilerParams(vmem_limit_bytes=60 << 20),
        cost_estimate=cost(100000000000),
    )(blocks[0].transpose(1, 0, 2), occ_coeff.transpose(2, 0, 1))


def four_points(zero, one, two, three, turn):
    even, odd = zero + two, one + three
    lift, lean = zero - two, turn(one - three)
    return even + odd, lift + lean, even - odd, lift - lean


class Pair:
    def __init__(self, real, imag):
        self.real, self.imag = real, imag

    def __add__(self, other):
        return Pair(self.real + other.real, self.imag + other.imag)

    def __sub__(self, other):
        return Pair(self.real - other.real, self.imag - other.imag)

    def turned(self):
        return Pair(-self.imag, self.real)


def lattice_kernel(sz, place_ref, offset_ref, cells_ref, *refs):
    outs, grid_ref, slot_ref = refs[:KY], refs[KY], refs[KY + 1]
    plane, seat = place_ref[0], place_ref[1]
    for cell in range(KX * KY):
        slot_ref[(offset_ref[0, cell] & 3) * KY + (offset_ref[1, cell] & 3)] = cell
    slots = [slot_ref[n] for n in range(KX * KY)]
    real_half = lax.broadcasted_iota(jnp.int32, (SUBLANES, LANES), 1) < HALF_LANES

    def turn_rest(value):
        moved = pltpu.roll(value, HALF_LANES, 1)
        return jnp.where(real_half, -moved, moved)

    def transform(load, turn, store):
        firsts = [four_points(*[load(slots[n * KY + m]) for n in range(KX)], turn) for m in range(KY)]
        for a in range(KX):
            seconds = four_points(*[firsts[m][a] for m in range(KY)], turn)
            for b in range(KY):
                store(a, b, seconds[b])

    for h in range(2):
        for c in range(sz.columns):
            near = 2 * sz.columns * h + c
            far = near + sz.columns

            def load(cell):
                return Pair(cells_ref[cell, near], cells_ref[cell, far])

            def store(a, b, value):
                grid_ref[b, a ^ plane, near] = value.real
                grid_ref[b, a ^ plane, far] = value.imag

            transform(load, Pair.turned, store)

    def load_rest(cell):
        return cells_ref[cell, sz.tail]

    def store_rest(a, b, value):
        grid_ref[b, a ^ plane, sz.tail] = value

    transform(load_rest, turn_rest, store_rest)
    for step in range(KY):
        outs[step][...] = grid_ref[step ^ seat]


def lattice_sum(sz, place, cell_offsets, cells):
    shape = jax.ShapeDtypeStruct((KX, sz.tail + 1, SUBLANES, LANES), F32)
    whole = pl.BlockSpec(memory_space=pltpu.VMEM)
    scalars = pl.BlockSpec(memory_space=pltpu.SMEM)
    return pl.pallas_call(
        functools.partial(lattice_kernel, sz),
        out_shape=[shape] * KY,
        in_specs=[scalars, scalars, whole],
        out_specs=[whole] * KY,
        scratch_shapes=[
            pltpu.VMEM((KY, KX, sz.tail + 1, SUBLANES, LANES), F32),
            pltpu.SMEM((KX * KY,), jnp.int32),
        ],
        compiler_params=pltpu.CompilerParams(vmem_limit_bytes=32 << 20),
        cost_estimate=cost(100000000000),
    )(place, cell_offsets, cells)


def band_kernel(sz, place_ref, *refs):
    halves, rights, outs = refs[:KY], refs[KY : KY + KX], refs[KY + KX : 2 * KY + KX]
    left_ref, band_ref, tile_ref = refs[2 * KY + KX :]
    seat = place_ref[1]
    count = KY * sz.rows
    row = lax.broadcasted_iota(jnp.int32, (SUBLANES, LANES), 0)
    lane = lax.broadcasted_iota(jnp.int32, (SUBLANES, LANES), 1)
    low_lanes = lax.broadcasted_iota(jnp.int32, (2 * count, LANES), 1) < HALF_LANES
    for step in range(KY):
        left_ref[:, step ^ seat] = halves[step][...]

    for k in range(KX):
        left = left_ref[k]
        near, rest = [], []
        for part in range(2):
            tiles = []
            for c in range(sz.columns):
                first = part * sz.columns + c
                halves_of = [left[:, first], left[:, 2 * sz.columns + first]]
                tiles.append(jnp.stack(halves_of, axis=1).reshape(count, LANES))
            near.append(jnp.concatenate(tiles, axis=1))
            for p in range(KY):
                tail = left[p, sz.tail]
                head = pltpu.roll(tail, HALF_LANES, 1) if part else tail
                kept = [left[p, 2 * sz.columns + part * sz.columns + c] for c in range(sz.columns)]
                spare = jnp.concatenate(
                    [jnp.broadcast_to(tile[SUBLANES - 1 :], (SEGMENTS, LANES)) for tile in kept], axis=0
                )[:SUBLANES]
                spare = staggered(spare, row, sz.gap, LANES - SEGMENT)
                rest += [head, jnp.where(lane < sz.gap, pltpu.roll(head, LANES - sz.rest, 1), spare)]
        near_high, near_low = split(jnp.concatenate(near, axis=0))
        rest_high = jnp.concatenate(rest, axis=0)
        rest_low = rest_high - rest_high.astype(BF16).astype(F32)
        both = jnp.where(low_lanes, rest_high, pltpu.roll(rest_low, HALF_LANES, 1)).astype(BF16)
        rest_three = jnp.concatenate([both, rest_high.astype(BF16)[:, :HALF_LANES]], axis=1)
        right = rights[k]
        band = dot(jnp.concatenate([near_high, near_low], axis=0), right[: sz.main])
        band = band[: 2 * count] + band[2 * count :]
        band += dot(near_high, right[sz.main : 2 * sz.main]) + dot(rest_three, right[2 * sz.main :])
        width = 2 * LANES
        top, bottom = band[:count], band[count:]
        real = top[:, :width] - bottom[:, width:]
        imag = top[:, width:] + bottom[:, :width]
        for h in range(2):
            lanes = slice(h * LANES, (h + 1) * LANES)
            band_ref[h, 0] = real[:, lanes]
            band_ref[h, 1] = imag[:, lanes]
        for i in range(sz.bands):
            for h in range(2):
                for part in range(2):
                    tile_ref[2 * i + h, part * KY : (part + 1) * KY] = band_ref[
                        h, part, pl.ds(i, KY, stride=sz.rows)
                    ]
        for step in range(KY):
            first = (step ^ seat) * sz.chunks // 2
            for n in range(sz.tiles):
                outs[step][k, n] = tile_ref[first + n]


def band_product(sz, place, halves, rights):
    shape = jax.ShapeDtypeStruct((KX, sz.tiles, 2 * KY, LANES), F32)
    whole = pl.BlockSpec(memory_space=pltpu.VMEM)
    scalars = pl.BlockSpec(memory_space=pltpu.SMEM)
    return pl.pallas_call(
        functools.partial(band_kernel, sz),
        out_shape=[shape] * KY,
        in_specs=[scalars] + [whole] * (KY + KX),
        out_specs=[whole] * KY,
        scratch_shapes=[
            pltpu.VMEM((KX, KY, sz.tail + 1, SUBLANES, LANES), F32),
            pltpu.VMEM((2, 2, KY * sz.rows, LANES), F32),
            pltpu.VMEM((2 * sz.bands, 2 * KY, LANES), F32),
        ],
        compiler_params=pltpu.CompilerParams(vmem_limit_bytes=32 << 20),
        cost_estimate=cost(10000000000),
    )(place, *halves, *rights)


def regroup_kernel(sz, place_ref, transfer_ref, *refs):
    sources, out_hbm = refs[:KY], refs[KY]
    row_ref, out_ref, sems = refs[KY + 1 :]
    plane, seat = place_ref[0], place_ref[1]
    lane = lax.broadcasted_iota(jnp.int32, (2 * KY, LANES), 1)
    cells = KX * KY
    starts = list(range(0, sz.pairs, LANES))
    pieces = [starts[i : i + PIECE] for i in range(0, len(starts), PIECE)]
    targets = [
        transfer_ref[(k ^ plane) * KY + (step ^ seat)] for step in range(KY) for k in range(KX)
    ]

    def piece_copy(index):
        first = pieces[index][0]
        span = pl.ds(first, min(pieces[index][-1] + LANES, sz.pairs) - first)
        return pltpu.make_async_copy(out_ref.at[:, span], out_hbm.at[:, span], sems.at[index])

    def place_rows(odd):
        for index, piece in enumerate(pieces):
            for first in piece:
                last = min(first + LANES, sz.pairs)
                for source, row in enumerate(targets):
                    step, k = divmod(source, KX)
                    value = None
                    for u in range(first // sz.chunk, (last - 1) // sz.chunk + 1):
                        tile = sources[step][k, (u + odd) // 2]
                        shift = (sz.chunk * u - HALF_LANES * (u + odd)) % LANES
                        moved = pltpu.roll(tile, shift, 1) if shift else tile
                        value = moved if value is None else jnp.where(lane < sz.chunk * u - first, value, moved)
                    row_ref[first // LANES, pl.ds(row, 2 * KY, stride=cells)] = value
                out_ref[:, first:last] = row_ref[first // LANES, :, : last - first]
            piece_copy(index).start()

    @pl.when(seat % 2 == 0)
    def _():
        place_rows(0)

    @pl.when(seat % 2 == 1)
    def _():
        place_rows(1)

    for index in range(len(pieces)):
        piece_copy(index).wait()


def regroup(sz, place, transfer_index, sources):
    whole = pl.BlockSpec(memory_space=pltpu.VMEM)
    scalars = pl.BlockSpec(memory_space=pltpu.SMEM)
    rows = 2 * KY * KX * KY
    tiles = -(-sz.pairs // LANES)
    return pl.pallas_call(
        functools.partial(regroup_kernel, sz),
        out_shape=jax.ShapeDtypeStruct((rows, sz.pairs), F32),
        in_specs=[scalars, scalars] + [whole] * KY,
        out_specs=pl.BlockSpec(memory_space=pl.ANY),
        scratch_shapes=[
            pltpu.VMEM((tiles, rows, LANES), F32),
            pltpu.VMEM((rows, sz.pairs), F32),
            pltpu.SemaphoreType.DMA((-(-tiles // PIECE),)),
        ],
        compiler_params=pltpu.CompilerParams(vmem_limit_bytes=32 << 20),
    )(place, transfer_index, *sources)


def spread_kernel(sz, in_ref, *refs):
    out_ref = refs[-1]
    low_lanes = lax.broadcasted_iota(jnp.int32, (sz.basis, LANES), 1) < HALF_LANES
    fill = jnp.zeros((sz.basis, LANES - sz.vir_half), F32)
    for part in range(2):
        value = jnp.concatenate([in_ref[:, part], fill], axis=1)
        out_ref[part] = jnp.where(low_lanes, value, pltpu.roll(value, HALF_LANES - sz.chunk, 1))


def spread(sz, value, flops, *after):
    whole = pl.BlockSpec(memory_space=pltpu.VMEM)
    return pl.pallas_call(
        functools.partial(spread_kernel, sz),
        out_shape=jax.ShapeDtypeStruct((2, sz.basis, LANES), F32),
        in_specs=[whole] + [pl.BlockSpec(memory_space=pl.ANY)] * len(after),
        out_specs=whole,
        compiler_params=pltpu.CompilerParams(vmem_limit_bytes=32 << 20),
        cost_estimate=cost(flops),
    )(value, *after)


def copy_kernel(in_ref, *refs):
    refs[-1][...] = in_ref[...]


def copied(value, *after):
    whole = pl.BlockSpec(memory_space=pltpu.VMEM)
    return pl.pallas_call(
        copy_kernel,
        out_shape=jax.ShapeDtypeStruct(value.shape, F32),
        in_specs=[whole] + [pl.BlockSpec(memory_space=pl.ANY)] * len(after),
        out_specs=whole,
        compiler_params=pltpu.CompilerParams(vmem_limit_bytes=32 << 20),
        cost_estimate=cost(10**6),
    )(value, *after)


def columns_kernel(sz, place_ref, own_ref, other_ref, out_ref):
    core = place_ref[2]
    under = jnp.zeros((sz.gap, LANES), F32)
    for part in range(2):
        mine, theirs = [jnp.concatenate([ref[part], under], axis=0) for ref in (own_ref, other_ref)]
        for h, value in enumerate([jnp.where(core == 0, mine, theirs), jnp.where(core == 0, theirs, mine)]):
            lanes = slice((2 * part + h) * LANES, (2 * part + h + 1) * LANES)
            high, low = split(value)
            out_ref[: sz.main, lanes] = high[: sz.main]
            out_ref[sz.main : 2 * sz.main, lanes] = low[: sz.main]
            for place, term in enumerate((high, high, low)):
                first = 2 * sz.main + place * HALF_LANES
                out_ref[first : first + HALF_LANES, lanes] = term[sz.main :]


def columns(sz, place, own, other, flops):
    whole = pl.BlockSpec(memory_space=pltpu.VMEM)
    scalars = pl.BlockSpec(memory_space=pltpu.SMEM)
    return pl.pallas_call(
        functools.partial(columns_kernel, sz),
        out_shape=jax.ShapeDtypeStruct((sz.depth, 4 * LANES), BF16),
        in_specs=[scalars, whole, whole],
        out_specs=whole,
        compiler_params=pltpu.CompilerParams(vmem_limit_bytes=32 << 20),
        cost_estimate=cost(flops),
    )(place, own, other)


def swap(value, step):
    return lax.ppermute(value, "cell", [(d, d ^ step) for d in range(KX * KY)])


def swap_cores(value):
    return lax.ppermute(value, "aux", [(0, 1), (1, 0)])


def by_planes(blocks, cell_offsets, occ_coeff, vir_coeff, transfer_index):
    sz = Sizes(blocks, occ_coeff, vir_coeff)
    me = lax.axis_index("cell")
    place = jnp.stack([me // KY, me % KY, lax.axis_index("aux")]).astype(jnp.int32)
    home = vir_coeff[0].transpose(1, 0, 2)
    across = spread(sz, swap(home, 2 * KY), 10000000000)
    beside = spread(sz, swap(home, KY), 100000000)
    corner = swap(across, KY)
    sent = half_bands(sz, blocks, occ_coeff).reshape(KX * KY, sz.tail + 1, SUBLANES, LANES)
    cells = lax.all_to_all(sent, "cell", split_axis=0, concat_axis=0, tiled=True)
    points = list(lattice_sum(sz, place, cell_offsets, cells))
    halves = [points[0]] + [swap(points[s], s) for s in range(1, KY)]
    ours = spread(sz, home, 3000000000, beside)
    if 1 == 1:
        corner = copied(corner, points[0])
    if 1 in (2, 3):
        corner = copied(corner, halves[1 - 1])
    rights = [columns(sz, place, v, swap_cores(v), 10000000000) for v in (ours, beside, across)]
    rights.append(columns(sz, place, corner, swap_cores(corner), 1000000000))
    bands = band_product(sz, place, halves, rights)
    sources = [bands[0]] + [swap(bands[s], s) for s in range(1, KY)]
    out = regroup(sz, place, transfer_index, sources)
    return out.reshape(2, sz.slab, KX * KY, sz.pairs)


def on_device(blocks, cell_offsets, occ_coeff, vir_coeff, transfer_index):
    arrays = (blocks, cell_offsets, occ_coeff, vir_coeff, transfer_index)
    if Sizes.fit(lax.axis_size("cell"), lax.axis_size("aux"), blocks, occ_coeff, vir_coeff):
        return by_planes(*arrays)
    return by_entries(*arrays)


def solution(mesh):
    placed = (P("cell", "aux", None, None), P(), P(), P("cell", None, None, "aux"), P())
    return jax.shard_map(
        on_device,
        mesh=mesh,
        in_specs=placed,
        out_specs=P(None, "aux", None, "cell"),
        check_vma=False,
    )
```

```python
import functools
import math

import jax
import jax.numpy as jnp
from jax import lax
from jax.experimental import pallas as pl
from jax.experimental.pallas import tpu as pltpu
from jax.sharding import PartitionSpec as P

KX = 4
KY = 4
LANES = 128
HALF_LANES = 64
SEGMENT = 32
PIECE = 4
SUBLANES = 8
SEGMENTS = LANES // SEGMENT
BF16 = jnp.bfloat16
F32 = jnp.float32


def phase_tables(cell_offsets, cell_count):
    depth = cell_count // (KX * KY)
    points = jnp.arange(cell_count, dtype=jnp.int32)
    along_a = points // (KY * depth)
    along_b = points // depth % KY
    along_c = points % depth
    turns = (
        along_a[:, None] * cell_offsets[0][None, :] * (KY * depth)
        + along_b[:, None] * cell_offsets[1][None, :] * (KX * depth)
        + along_c[:, None] * cell_offsets[2][None, :] * (KX * KY)
    ) % cell_count
    angles = 2.0 * math.pi / cell_count * turns.astype(jnp.float32)
    return (jnp.cos(angles), jnp.sin(angles))


def matmul(left, right):
    return jnp.dot(left, right, precision=lax.Precision.HIGHEST, preferred_element_type=jnp.float32)


def contract(form, left, right):
    return jnp.einsum(form, left, right, precision=lax.Precision.HIGHEST)


def by_entries(blocks, cell_offsets, occ_coeff, vir_coeff, transfer_index):
    cell_count = lax.axis_size("cell")
    slab_rows = blocks.shape[1]
    basis_size = blocks.shape[2]
    occupied = occ_coeff.shape[2]
    cosines, sines = phase_tables(cell_offsets, cell_count)
    occ_real, occ_imag = (occ_coeff[0], occ_coeff[1])
    flattened = blocks.reshape(1, -1)
    arrived = lax.all_to_all(flattened, "cell", split_axis=1, concat_axis=0, tiled=True)
    grid_real = matmul(cosines, arrived)
    grid_imag = matmul(sines, arrived)
    back_real, back_imag = (
        lax.all_to_all(grid_real, "cell", split_axis=0, concat_axis=1, tiled=True),
        lax.all_to_all(grid_imag, "cell", split_axis=0, concat_axis=1, tiled=True),
    )
    spec_real = back_real.reshape(slab_rows, basis_size, basis_size)
    spec_imag = back_imag.reshape(slab_rows, basis_size, basis_size)
    half_real = contract("mi,pmn->pin", occ_real, spec_real) + contract(
        "mi,pmn->pin", occ_imag, spec_imag
    )
    half_imag = contract("mi,pmn->pin", occ_real, spec_imag) - contract(
        "mi,pmn->pin", occ_imag, spec_real
    )
    rows_real = half_real.reshape(slab_rows * occupied, basis_size)
    rows_imag = half_imag.reshape(slab_rows * occupied, basis_size)
    column_piece = lax.all_gather(vir_coeff, "aux", axis=3, tiled=True)
    coef_real = column_piece[0, 0]
    coef_imag = column_piece[0, 1]
    part_real = matmul(rows_real, coef_real) - matmul(rows_imag, coef_imag)
    part_imag = matmul(rows_real, coef_imag) + matmul(rows_imag, coef_real)
    banded = jnp.stack([part_real, part_imag])
    pair_rows = banded.reshape(2, slab_rows, 1, -1)
    regrouped = lax.all_to_all(pair_rows, "cell", split_axis=3, concat_axis=2, tiled=True)
    source = jnp.argsort(transfer_index)
    return jnp.take(regrouped, source, axis=2)


def cost(flops):
    return pl.CostEstimate(flops=flops, bytes_accessed=flops // 100, transcendentals=0)


def split(value):
    high = value.astype(BF16)
    return high, (value - high.astype(F32)).astype(BF16)


def dot(left, right):
    return jnp.dot(left, right, preferred_element_type=F32)


class Sizes:
    def __init__(self, blocks, occ_coeff, vir_coeff):
        self.slab = blocks.shape[1]
        self.basis = blocks.shape[2]
        self.occ = occ_coeff.shape[2]
        self.vir_half = vir_coeff.shape[3]
        self.main = self.basis // LANES * LANES
        self.rest = self.basis - self.main
        self.columns = self.main // LANES
        self.gap = HALF_LANES - self.rest
        self.depth = 2 * self.main + 3 * HALF_LANES
        self.bands = self.occ // KX
        self.rows = 2 * SUBLANES
        self.tail = 4 * self.columns
        self.pairs = 2 * self.vir_half * self.bands // KY
        self.full = self.pairs // LANES
        self.share = LANES // KX

    @staticmethod
    def fit(cells, aux, blocks, occ_coeff, vir_coeff):
        basis, occ, half = blocks.shape[2], occ_coeff.shape[2], vir_coeff.shape[3]
        return (
            cells == KX * KY
            and aux == 2
            and blocks.shape[1] == KY
            and occ % KX == 0
            and basis > LANES
            and HALF_LANES // 2 <= basis % LANES <= HALF_LANES // 2 + SEGMENT // 2
            and SUBLANES <= occ // KX < 2 * SUBLANES
            and occ // KX - SUBLANES <= basis // LANES * (LANES // SEGMENT)
            and HALF_LANES < half <= LANES
            and 2 * half * (occ // KX) % KY == 0
            and 2 * half * (occ // KX) // KY % LANES <= LANES // KX
        )


def staggered(tile, row, first, stride):
    out = pltpu.roll(tile, first % LANES, 1)
    for r in range(1, SEGMENTS):
        out = jnp.where(row % SEGMENTS == r, pltpu.roll(tile, (first + r * stride) % LANES, 1), out)
    return out


def half_kernel(sz, block_hbm, occ_hbm, out_hbm, block_ref, occ_ref, out_ref, block_sem, occ_sem, out_sem):
    count = KX * sz.rows
    occ_copy = pltpu.make_async_copy(occ_hbm, occ_ref, occ_sem)
    block_copy = pltpu.make_async_copy(block_hbm, block_ref, block_sem)
    occ_copy.start()
    block_copy.start()
    place = lax.broadcasted_iota(jnp.int32, (count, sz.occ), 0)
    band = lax.broadcasted_iota(jnp.int32, (count, sz.occ), 1)
    inner = place % sz.rows
    pick = ((place // sz.rows * sz.bands + inner == band) & (inner < sz.bands)).astype(BF16)
    occ_copy.wait()
    terms = [split(occ_ref[:, part]) for part in range(2)]
    left_high = jnp.concatenate([dot(pick, terms[0][0]), -dot(pick, terms[1][0])], axis=0).astype(BF16)
    left_low = jnp.concatenate([dot(pick, terms[0][1]), -dot(pick, terms[1][1])], axis=0).astype(BF16)
    left = jnp.concatenate([left_high, left_low], axis=0)
    fill = jnp.zeros((sz.basis, LANES - sz.rest), F32)
    row = lax.broadcasted_iota(jnp.int32, (SUBLANES, LANES), 0)
    lane = lax.broadcasted_iota(jnp.int32, (SUBLANES, LANES), 1)
    block_copy.wait()
    for p in range(sz.slab):
        high, low = split(jnp.concatenate([block_ref[:, p], fill], axis=1))
        half = dot(left, high)
        half = half[: 2 * count] + half[2 * count :] + dot(left_high, low)
        real, imag = half[:count], half[count:]
        for z in range(KX):
            near = slice(z * sz.rows, z * sz.rows + SUBLANES)
            far = slice(z * sz.rows + SUBLANES, (z + 1) * sz.rows)
            tails = []
            for part, value in enumerate((real, imag)):
                head, last = value[near, sz.main :], value[far, sz.main :]
                tails.append(head + pltpu.roll(jnp.where(lane < sz.gap, last, 0.0), sz.rest, 1))
                spare = jnp.where(lane < sz.gap, 0.0, last)
                spare = staggered(spare, row, LANES - sz.gap, SEGMENT)
                for c in range(sz.columns):
                    lanes = slice(c * LANES, (c + 1) * LANES)
                    rows = slice(c * SEGMENTS, (c + 1) * SEGMENTS)
                    kept = jnp.sum(spare[rows], axis=0, keepdims=True)
                    tile = part * sz.columns + c
                    out_ref[z, p, tile] = value[near, lanes]
                    out_ref[z, p, 2 * sz.columns + tile] = jnp.where(row == SUBLANES - 1, kept, value[far, lanes])
            out_ref[z, p, sz.tail] = tails[0] + pltpu.roll(tails[1], HALF_LANES, 1)
        pltpu.make_async_copy(out_ref.at[:, p], out_hbm.at[:, p], out_sem.at[p]).start()
    for p in range(sz.slab):
        pltpu.make_async_copy(out_ref.at[:, p], out_hbm.at[:, p], out_sem.at[p]).wait()


def half_bands(sz, blocks, occ_coeff):
    anywhere = pl.BlockSpec(memory_space=pl.ANY)
    return pl.pallas_call(
        functools.partial(half_kernel, sz),
        out_shape=jax.ShapeDtypeStruct((KX, KY, sz.tail + 1, SUBLANES, LANES), F32),
        in_specs=[anywhere, anywhere],
        out_specs=anywhere,
        scratch_shapes=[
            pltpu.VMEM((sz.basis, sz.slab, sz.basis), F32),
            pltpu.VMEM((sz.occ, 2, sz.basis), F32),
            pltpu.VMEM((KX, KY, sz.tail + 1, SUBLANES, LANES), F32),
            pltpu.SemaphoreType.DMA,
            pltpu.SemaphoreType.DMA,
            pltpu.SemaphoreType.DMA((sz.slab,)),
        ],
        compiler_params=pltpu.CompilerParams(vmem_limit_bytes=60 << 20),
        cost_estimate=cost(100000000000),
    )(blocks[0].transpose(1, 0, 2), occ_coeff.transpose(2, 0, 1))


def four_points(zero, one, two, three, turn):
    even, odd = zero + two, one + three
    lift, lean = zero - two, turn(one - three)
    return even + odd, lift + lean, even - odd, lift - lean


class Pair:
    def __init__(self, real, imag):
        self.real, self.imag = real, imag

    def __add__(self, other):
        return Pair(self.real + other.real, self.imag + other.imag)

    def __sub__(self, other):
        return Pair(self.real - other.real, self.imag - other.imag)

    def turned(self):
        return Pair(-self.imag, self.real)


def lattice_kernel(sz, place_ref, offset_ref, cells_ref, *refs):
    outs, grid_ref, slot_ref = refs[:KY], refs[KY], refs[KY + 1]
    plane, seat = place_ref[0], place_ref[1]
    for cell in range(KX * KY):
        slot_ref[(offset_ref[0, cell] & 3) * KY + (offset_ref[1, cell] & 3)] = cell
    slots = [slot_ref[n] for n in range(KX * KY)]
    real_half = lax.broadcasted_iota(jnp.int32, (SUBLANES, LANES), 1) < HALF_LANES

    def turn_rest(value):
        moved = pltpu.roll(value, HALF_LANES, 1)
        return jnp.where(real_half, -moved, moved)

    def transform(load, turn, store):
        firsts = [four_points(*[load(slots[n * KY + m]) for n in range(KX)], turn) for m in range(KY)]
        for a in range(KX):
            seconds = four_points(*[firsts[m][a] for m in range(KY)], turn)
            for b in range(KY):
                store(a, b, seconds[b])

    for h in range(2):
        for c in range(sz.columns):
            near = 2 * sz.columns * h + c
            far = near + sz.columns

            def load(cell):
                return Pair(cells_ref[cell, near], cells_ref[cell, far])

            def store(a, b, value):
                grid_ref[b, a ^ plane, near] = value.real
                grid_ref[b, a ^ plane, far] = value.imag

            transform(load, Pair.turned, store)

    def load_rest(cell):
        return cells_ref[cell, sz.tail]

    def store_rest(a, b, value):
        grid_ref[b, a ^ plane, sz.tail] = value

    transform(load_rest, turn_rest, store_rest)
    for step in range(KY):
        outs[step][...] = grid_ref[step ^ seat]


def lattice_sum(sz, place, cell_offsets, cells):
    shape = jax.ShapeDtypeStruct((KX, sz.tail + 1, SUBLANES, LANES), F32)
    whole = pl.BlockSpec(memory_space=pltpu.VMEM)
    scalars = pl.BlockSpec(memory_space=pltpu.SMEM)
    return pl.pallas_call(
        functools.partial(lattice_kernel, sz),
        out_shape=[shape] * KY,
        in_specs=[scalars, scalars, whole],
        out_specs=[whole] * KY,
        scratch_shapes=[
            pltpu.VMEM((KY, KX, sz.tail + 1, SUBLANES, LANES), F32),
            pltpu.SMEM((KX * KY,), jnp.int32),
        ],
        compiler_params=pltpu.CompilerParams(vmem_limit_bytes=32 << 20),
        cost_estimate=cost(100000000000),
    )(place, cell_offsets, cells)


def band_kernel(sz, place_ref, *refs):
    halves, rights, outs = refs[:KY], refs[KY : KY + KX], refs[KY + KX : 2 * KY + KX]
    left_ref, band_ref, tile_ref, pack_ref = refs[2 * KY + KX :]
    wide = lax.broadcasted_iota(jnp.int32, (2 * KY, LANES), 1)
    ends = [None] * KY
    seat = place_ref[1]
    count = KY * sz.rows
    row = lax.broadcasted_iota(jnp.int32, (SUBLANES, LANES), 0)
    lane = lax.broadcasted_iota(jnp.int32, (SUBLANES, LANES), 1)
    low_lanes = lax.broadcasted_iota(jnp.int32, (2 * count, LANES), 1) < HALF_LANES
    for step in range(KY):
        left_ref[:, step ^ seat] = halves[step][...]

    for k in range(KX):
        left = left_ref[k]
        near, rest = [], []
        for part in range(2):
            tiles = []
            for c in range(sz.columns):
                first = part * sz.columns + c
                halves_of = [left[:, first], left[:, 2 * sz.columns + first]]
                tiles.append(jnp.stack(halves_of, axis=1).reshape(count, LANES))
            near.append(jnp.concatenate(tiles, axis=1))
            for p in range(KY):
                tail = left[p, sz.tail]
                head = pltpu.roll(tail, HALF_LANES, 1) if part else tail
                kept = [left[p, 2 * sz.columns + part * sz.columns + c] for c in range(sz.columns)]
                spare = jnp.concatenate(
                    [jnp.broadcast_to(tile[SUBLANES - 1 :], (SEGMENTS, LANES)) for tile in kept], axis=0
                )[:SUBLANES]
                spare = staggered(spare, row, sz.gap, LANES - SEGMENT)
                rest += [head, jnp.where(lane < sz.gap, pltpu.roll(head, LANES - sz.rest, 1), spare)]
        near_high, near_low = split(jnp.concatenate(near, axis=0))
        rest_high = jnp.concatenate(rest, axis=0)
        rest_low = rest_high - rest_high.astype(BF16).astype(F32)
        both = jnp.where(low_lanes, rest_high, pltpu.roll(rest_low, HALF_LANES, 1)).astype(BF16)
        rest_three = jnp.concatenate([both, rest_high.astype(BF16)[:, :HALF_LANES]], axis=1)
        right = rights[k]
        band = dot(jnp.concatenate([near_high, near_low], axis=0), right[: sz.main])
        band = band[: 2 * count] + band[2 * count :]
        band += dot(near_high, right[sz.main : 2 * sz.main]) + dot(rest_three, right[2 * sz.main :])
        width = 2 * LANES
        top, bottom = band[:count], band[count:]
        real = top[:, :width] - bottom[:, width:]
        imag = top[:, width:] + bottom[:, :width]
        for h in range(2):
            lanes = slice(h * LANES, (h + 1) * LANES)
            band_ref[h, 0] = real[:, lanes]
            band_ref[h, 1] = imag[:, lanes]
        for i in range(sz.bands):
            for h in range(2):
                for part in range(2):
                    tile_ref[2 * i + h, part * KY : (part + 1) * KY] = band_ref[
                        h, part, pl.ds(i, KY, stride=sz.rows)
                    ]
        for target in range(KY):
            for first in range(0, sz.pairs, LANES):
                last = min(first + LANES, sz.pairs)
                value = None
                begin, end = target * sz.pairs + first, target * sz.pairs + last
                for tile in range(begin // sz.vir_half, (end - 1) // sz.vir_half + 1):
                    offset = tile * sz.vir_half - begin
                    moved = pltpu.roll(tile_ref[tile], offset % LANES, 1) if offset % LANES else tile_ref[tile]
                    value = moved if value is None else jnp.where(wide < offset, value, moved)
                if last - first == LANES:
                    pack_ref[target, k * sz.full + first // LANES] = value
                else:
                    moved = pltpu.roll(value, k * sz.share, 1) if k else value
                    ends[target] = moved if k == 0 else jnp.where(wide < k * sz.share, ends[target], moved)
    for target in range(KY):
        if ends[target] is not None:
            pack_ref[target, KX * sz.full] = ends[target]
    for step in range(KY):
        outs[step][...] = pack_ref[step ^ seat]


def band_product(sz, place, halves, rights):
    count = KX * sz.full + (sz.pairs % LANES > 0)
    shape = jax.ShapeDtypeStruct((count, 2 * KY, LANES), F32)
    whole = pl.BlockSpec(memory_space=pltpu.VMEM)
    scalars = pl.BlockSpec(memory_space=pltpu.SMEM)
    return pl.pallas_call(
        functools.partial(band_kernel, sz),
        out_shape=[shape] * KY,
        in_specs=[scalars] + [whole] * (KY + KX),
        out_specs=[whole] * KY,
        scratch_shapes=[
            pltpu.VMEM((KX, KY, sz.tail + 1, SUBLANES, LANES), F32),
            pltpu.VMEM((2, 2, KY * sz.rows, LANES), F32),
            pltpu.VMEM((2 * sz.bands, 2 * KY, LANES), F32),
            pltpu.VMEM((KY, count, 2 * KY, LANES), F32),
        ],
        compiler_params=pltpu.CompilerParams(vmem_limit_bytes=32 << 20),
        cost_estimate=cost(10000000000),
    )(place, *halves, *rights)


def regroup_kernel(sz, place_ref, transfer_ref, *refs):
    sources, out_hbm = refs[:KY], refs[KY]
    row_ref, out_ref, sems = refs[KY + 1 :]
    plane, seat = place_ref[0], place_ref[1]
    cells = KX * KY
    starts = list(range(0, sz.pairs, LANES))
    pieces = [starts[i : i + PIECE] for i in range(0, len(starts), PIECE)]
    copies = []
    for index, piece in enumerate(pieces):
        for first in piece:
            last = min(first + LANES, sz.pairs)
            for step in range(KY):
                for k in range(KX):
                    row = transfer_ref[(k ^ plane) * KY + (step ^ seat)]
                    if last - first == LANES:
                        tile = sources[step][k * sz.full + first // LANES]
                    else:
                        tile = sources[step][KX * sz.full]
                        tile = pltpu.roll(tile, LANES - k * sz.share, 1) if k else tile
                    row_ref[first // LANES, pl.ds(row, 2 * KY, stride=cells)] = tile
            out_ref[:, first:last] = row_ref[first // LANES, :, : last - first]
        span = pl.ds(piece[0], min(piece[-1] + LANES, sz.pairs) - piece[0])
        copies.append(pltpu.make_async_copy(out_ref.at[:, span], out_hbm.at[:, span], sems.at[index]))
        copies[-1].start()
    for copy in copies:
        copy.wait()


def regroup(sz, place, transfer_index, sources):
    whole = pl.BlockSpec(memory_space=pltpu.VMEM)
    scalars = pl.BlockSpec(memory_space=pltpu.SMEM)
    rows = 2 * KY * KX * KY
    tiles = -(-sz.pairs // LANES)
    return pl.pallas_call(
        functools.partial(regroup_kernel, sz),
        out_shape=jax.ShapeDtypeStruct((rows, sz.pairs), F32),
        in_specs=[scalars, scalars] + [whole] * KY,
        out_specs=pl.BlockSpec(memory_space=pl.ANY),
        scratch_shapes=[
            pltpu.VMEM((tiles, rows, LANES), F32),
            pltpu.VMEM((rows, sz.pairs), F32),
            pltpu.SemaphoreType.DMA((-(-tiles // PIECE),)),
        ],
        compiler_params=pltpu.CompilerParams(vmem_limit_bytes=32 << 20),
    )(place, transfer_index, *sources)


def spread_kernel(sz, in_ref, *refs):
    out_ref = refs[-1]
    fill = jnp.zeros((sz.basis, LANES - sz.vir_half), F32)
    for part in range(2):
        out_ref[part] = jnp.concatenate([in_ref[:, part], fill], axis=1)


def spread(sz, value, flops, *after):
    whole = pl.BlockSpec(memory_space=pltpu.VMEM)
    return pl.pallas_call(
        functools.partial(spread_kernel, sz),
        out_shape=jax.ShapeDtypeStruct((2, sz.basis, LANES), F32),
        in_specs=[whole] + [pl.BlockSpec(memory_space=pl.ANY)] * len(after),
        out_specs=whole,
        compiler_params=pltpu.CompilerParams(vmem_limit_bytes=32 << 20),
        cost_estimate=cost(flops),
    )(value, *after)


def copy_kernel(in_ref, *refs):
    refs[-1][...] = in_ref[...]


def copied(value, *after):
    whole = pl.BlockSpec(memory_space=pltpu.VMEM)
    return pl.pallas_call(
        copy_kernel,
        out_shape=jax.ShapeDtypeStruct(value.shape, F32),
        in_specs=[whole] + [pl.BlockSpec(memory_space=pl.ANY)] * len(after),
        out_specs=whole,
        compiler_params=pltpu.CompilerParams(vmem_limit_bytes=32 << 20),
        cost_estimate=cost(10**6),
    )(value, *after)


def columns_kernel(sz, place_ref, own_ref, other_ref, out_ref):
    core = place_ref[2]
    under = jnp.zeros((sz.gap, LANES), F32)
    for part in range(2):
        mine, theirs = [jnp.concatenate([ref[part], under], axis=0) for ref in (own_ref, other_ref)]
        for h, value in enumerate([jnp.where(core == 0, mine, theirs), jnp.where(core == 0, theirs, mine)]):
            lanes = slice((2 * part + h) * LANES, (2 * part + h + 1) * LANES)
            high, low = split(value)
            out_ref[: sz.main, lanes] = high[: sz.main]
            out_ref[sz.main : 2 * sz.main, lanes] = low[: sz.main]
            for place, term in enumerate((high, high, low)):
                first = 2 * sz.main + place * HALF_LANES
                out_ref[first : first + HALF_LANES, lanes] = term[sz.main :]


def columns(sz, place, own, other, flops):
    whole = pl.BlockSpec(memory_space=pltpu.VMEM)
    scalars = pl.BlockSpec(memory_space=pltpu.SMEM)
    return pl.pallas_call(
        functools.partial(columns_kernel, sz),
        out_shape=jax.ShapeDtypeStruct((sz.depth, 4 * LANES), BF16),
        in_specs=[scalars, whole, whole],
        out_specs=whole,
        compiler_params=pltpu.CompilerParams(vmem_limit_bytes=32 << 20),
        cost_estimate=cost(flops),
    )(place, own, other)


def swap(value, step):
    return lax.ppermute(value, "cell", [(d, d ^ step) for d in range(KX * KY)])


def swap_cores(value):
    return lax.ppermute(value, "aux", [(0, 1), (1, 0)])


def by_planes(blocks, cell_offsets, occ_coeff, vir_coeff, transfer_index):
    sz = Sizes(blocks, occ_coeff, vir_coeff)
    me = lax.axis_index("cell")
    place = jnp.stack([me // KY, me % KY, lax.axis_index("aux")]).astype(jnp.int32)
    home = vir_coeff[0].transpose(1, 0, 2)
    across = spread(sz, swap(home, 2 * KY), 10000000000)
    beside = spread(sz, swap(home, KY), 100000000)
    corner = swap(across, KY)
    sent = half_bands(sz, blocks, occ_coeff).reshape(KX * KY, sz.tail + 1, SUBLANES, LANES)
    cells = lax.all_to_all(sent, "cell", split_axis=0, concat_axis=0, tiled=True)
    points = list(lattice_sum(sz, place, cell_offsets, cells))
    halves = [points[0]] + [swap(points[s], s) for s in range(1, KY)]
    ours = spread(sz, home, 3000000000, beside)
    if 1 == 1:
        corner = copied(corner, points[0])
    if 1 in (2, 3):
        corner = copied(corner, halves[1 - 1])
    rights = [columns(sz, place, v, swap_cores(v), 10000000000) for v in (ours, beside, across)]
    rights.append(columns(sz, place, corner, swap_cores(corner), 1000000000))
    bands = band_product(sz, place, halves, rights)
    sources = [bands[0]] + [swap(bands[s], s) for s in range(1, KY)]
    out = regroup(sz, place, transfer_index, sources)
    return out.reshape(2, sz.slab, KX * KY, sz.pairs)


def on_device(blocks, cell_offsets, occ_coeff, vir_coeff, transfer_index):
    arrays = (blocks, cell_offsets, occ_coeff, vir_coeff, transfer_index)
    if Sizes.fit(lax.axis_size("cell"), lax.axis_size("aux"), blocks, occ_coeff, vir_coeff):
        return by_planes(*arrays)
    return by_entries(*arrays)


def solution(mesh):
    placed = (P("cell", "aux", None, None), P(), P(), P("cell", None, None, "aux"), P())
    return jax.shard_map(
        on_device,
        mesh=mesh,
        in_specs=placed,
        out_specs=P(None, "aux", None, "cell"),
        check_vma=False,
    )
```

```python
import functools
import math

import jax
import jax.numpy as jnp
from jax import lax
from jax.experimental import pallas as pl
from jax.experimental.pallas import tpu as pltpu
from jax.sharding import PartitionSpec as P

KX = 4
KY = 4
LANES = 128
HALF_LANES = 64
SEGMENT = 32
PIECE = 2
OUT = (0, 1, 2, 3)
BACK = (0, 3, 2, 1)
SUBLANES = 8
SEGMENTS = LANES // SEGMENT
BF16 = jnp.bfloat16
F32 = jnp.float32


def phase_tables(cell_offsets, cell_count):
    depth = cell_count // (KX * KY)
    points = jnp.arange(cell_count, dtype=jnp.int32)
    along_a = points // (KY * depth)
    along_b = points // depth % KY
    along_c = points % depth
    turns = (
        along_a[:, None] * cell_offsets[0][None, :] * (KY * depth)
        + along_b[:, None] * cell_offsets[1][None, :] * (KX * depth)
        + along_c[:, None] * cell_offsets[2][None, :] * (KX * KY)
    ) % cell_count
    angles = 2.0 * math.pi / cell_count * turns.astype(jnp.float32)
    return (jnp.cos(angles), jnp.sin(angles))


def matmul(left, right):
    return jnp.dot(left, right, precision=lax.Precision.HIGHEST, preferred_element_type=jnp.float32)


def contract(form, left, right):
    return jnp.einsum(form, left, right, precision=lax.Precision.HIGHEST)


def by_entries(blocks, cell_offsets, occ_coeff, vir_coeff, transfer_index):
    cell_count = lax.axis_size("cell")
    slab_rows = blocks.shape[1]
    basis_size = blocks.shape[2]
    occupied = occ_coeff.shape[2]
    cosines, sines = phase_tables(cell_offsets, cell_count)
    occ_real, occ_imag = (occ_coeff[0], occ_coeff[1])
    flattened = blocks.reshape(1, -1)
    arrived = lax.all_to_all(flattened, "cell", split_axis=1, concat_axis=0, tiled=True)
    grid_real = matmul(cosines, arrived)
    grid_imag = matmul(sines, arrived)
    back_real, back_imag = (
        lax.all_to_all(grid_real, "cell", split_axis=0, concat_axis=1, tiled=True),
        lax.all_to_all(grid_imag, "cell", split_axis=0, concat_axis=1, tiled=True),
    )
    spec_real = back_real.reshape(slab_rows, basis_size, basis_size)
    spec_imag = back_imag.reshape(slab_rows, basis_size, basis_size)
    half_real = contract("mi,pmn->pin", occ_real, spec_real) + contract(
        "mi,pmn->pin", occ_imag, spec_imag
    )
    half_imag = contract("mi,pmn->pin", occ_real, spec_imag) - contract(
        "mi,pmn->pin", occ_imag, spec_real
    )
    rows_real = half_real.reshape(slab_rows * occupied, basis_size)
    rows_imag = half_imag.reshape(slab_rows * occupied, basis_size)
    column_piece = lax.all_gather(vir_coeff, "aux", axis=3, tiled=True)
    coef_real = column_piece[0, 0]
    coef_imag = column_piece[0, 1]
    part_real = matmul(rows_real, coef_real) - matmul(rows_imag, coef_imag)
    part_imag = matmul(rows_real, coef_imag) + matmul(rows_imag, coef_real)
    banded = jnp.stack([part_real, part_imag])
    pair_rows = banded.reshape(2, slab_rows, 1, -1)
    regrouped = lax.all_to_all(pair_rows, "cell", split_axis=3, concat_axis=2, tiled=True)
    source = jnp.argsort(transfer_index)
    return jnp.take(regrouped, source, axis=2)


def cost(flops):
    return pl.CostEstimate(flops=flops, bytes_accessed=flops // 100, transcendentals=0)


def split(value):
    high = value.astype(BF16)
    return high, (value - high.astype(F32)).astype(BF16)


def dot(left, right):
    return jnp.dot(left, right, preferred_element_type=F32)


class Sizes:
    def __init__(self, blocks, occ_coeff, vir_coeff):
        self.slab = blocks.shape[1]
        self.basis = blocks.shape[2]
        self.occ = occ_coeff.shape[2]
        self.vir_half = vir_coeff.shape[3]
        self.main = self.basis // LANES * LANES
        self.rest = self.basis - self.main
        self.columns = self.main // LANES
        self.gap = HALF_LANES - self.rest
        self.depth = 2 * self.main + 3 * HALF_LANES
        self.bands = self.occ // KX
        self.rows = 2 * SUBLANES
        self.tail = 4 * self.columns
        self.pairs = 2 * self.vir_half * self.bands // KY
        self.full = self.pairs // LANES
        self.share = LANES // KX

    @staticmethod
    def fit(cells, aux, blocks, occ_coeff, vir_coeff):
        basis, occ, half = blocks.shape[2], occ_coeff.shape[2], vir_coeff.shape[3]
        return (
            cells == KX * KY
            and aux == 2
            and blocks.shape[1] == KY
            and occ % KX == 0
            and basis > LANES
            and HALF_LANES // 2 <= basis % LANES <= HALF_LANES // 2 + SEGMENT // 2
            and SUBLANES <= occ // KX < 2 * SUBLANES
            and occ // KX - SUBLANES <= basis // LANES * (LANES // SEGMENT)
            and HALF_LANES < half <= LANES
            and 2 * half * (occ // KX) % KY == 0
            and 2 * half * (occ // KX) // KY % LANES <= LANES // KX
        )


def staggered(tile, row, first, stride):
    out = pltpu.roll(tile, first % LANES, 1)
    for r in range(1, SEGMENTS):
        out = jnp.where(row % SEGMENTS == r, pltpu.roll(tile, (first + r * stride) % LANES, 1), out)
    return out


def half_kernel(sz, block_hbm, occ_hbm, out_hbm, block_ref, occ_ref, out_ref, block_sem, occ_sem, out_sem):
    count = KX * sz.rows
    occ_copy = pltpu.make_async_copy(occ_hbm, occ_ref, occ_sem)
    block_copy = pltpu.make_async_copy(block_hbm, block_ref, block_sem)
    occ_copy.start()
    block_copy.start()
    place = lax.broadcasted_iota(jnp.int32, (count, sz.occ), 0)
    band = lax.broadcasted_iota(jnp.int32, (count, sz.occ), 1)
    inner = place % sz.rows
    pick = ((place // sz.rows * sz.bands + inner == band) & (inner < sz.bands)).astype(BF16)
    occ_copy.wait()
    terms = [split(occ_ref[:, part]) for part in range(2)]
    left_high = jnp.concatenate([dot(pick, terms[0][0]), -dot(pick, terms[1][0])], axis=0).astype(BF16)
    left_low = jnp.concatenate([dot(pick, terms[0][1]), -dot(pick, terms[1][1])], axis=0).astype(BF16)
    left = jnp.concatenate([left_high, left_low], axis=0)
    fill = jnp.zeros((sz.basis, LANES - sz.rest), F32)
    row = lax.broadcasted_iota(jnp.int32, (SUBLANES, LANES), 0)
    lane = lax.broadcasted_iota(jnp.int32, (SUBLANES, LANES), 1)
    block_copy.wait()
    for p in range(sz.slab):
        high, low = split(jnp.concatenate([block_ref[:, p], fill], axis=1))
        half = dot(left, high)
        half = half[: 2 * count] + half[2 * count :] + dot(left_high, low)
        real, imag = half[:count], half[count:]
        for z in range(KX):
            near = slice(z * sz.rows, z * sz.rows + SUBLANES)
            far = slice(z * sz.rows + SUBLANES, (z + 1) * sz.rows)
            tails = []
            for part, value in enumerate((real, imag)):
                head, last = value[near, sz.main :], value[far, sz.main :]
                tails.append(head + pltpu.roll(jnp.where(lane < sz.gap, last, 0.0), sz.rest, 1))
                spare = jnp.where(lane < sz.gap, 0.0, last)
                spare = staggered(spare, row, LANES - sz.gap, SEGMENT)
                for c in range(sz.columns):
                    lanes = slice(c * LANES, (c + 1) * LANES)
                    rows = slice(c * SEGMENTS, (c + 1) * SEGMENTS)
                    kept = jnp.sum(spare[rows], axis=0, keepdims=True)
                    tile = part * sz.columns + c
                    out_ref[z, p, tile] = value[near, lanes]
                    out_ref[z, p, 2 * sz.columns + tile] = jnp.where(row == SUBLANES - 1, kept, value[far, lanes])
            out_ref[z, p, sz.tail] = tails[0] + pltpu.roll(tails[1], HALF_LANES, 1)
        pltpu.make_async_copy(out_ref.at[:, p], out_hbm.at[:, p], out_sem.at[p]).start()
    for p in range(sz.slab):
        pltpu.make_async_copy(out_ref.at[:, p], out_hbm.at[:, p], out_sem.at[p]).wait()


def half_bands(sz, blocks, occ_coeff):
    anywhere = pl.BlockSpec(memory_space=pl.ANY)
    return pl.pallas_call(
        functools.partial(half_kernel, sz),
        out_shape=jax.ShapeDtypeStruct((KX, KY, sz.tail + 1, SUBLANES, LANES), F32),
        in_specs=[anywhere, anywhere],
        out_specs=anywhere,
        scratch_shapes=[
            pltpu.VMEM((sz.basis, sz.slab, sz.basis), F32),
            pltpu.VMEM((sz.occ, 2, sz.basis), F32),
            pltpu.VMEM((KX, KY, sz.tail + 1, SUBLANES, LANES), F32),
            pltpu.SemaphoreType.DMA,
            pltpu.SemaphoreType.DMA,
            pltpu.SemaphoreType.DMA((sz.slab,)),
        ],
        compiler_params=pltpu.CompilerParams(vmem_limit_bytes=60 << 20),
        cost_estimate=cost(100000000000),
    )(blocks[0].transpose(1, 0, 2), occ_coeff.transpose(2, 0, 1))


def four_points(zero, one, two, three, turn):
    even, odd = zero + two, one + three
    lift, lean = zero - two, turn(one - three)
    return even + odd, lift + lean, even - odd, lift - lean


class Pair:
    def __init__(self, real, imag):
        self.real, self.imag = real, imag

    def __add__(self, other):
        return Pair(self.real + other.real, self.imag + other.imag)

    def __sub__(self, other):
        return Pair(self.real - other.real, self.imag - other.imag)

    def turned(self):
        return Pair(-self.imag, self.real)


def lattice_kernel(sz, place_ref, offset_ref, cells_ref, *refs):
    outs, grid_ref, slot_ref = refs[:KY], refs[KY], refs[KY + 1]
    plane, seat = place_ref[0], place_ref[1]
    for cell in range(KX * KY):
        slot_ref[(offset_ref[0, cell] & 3) * KY + (offset_ref[1, cell] & 3)] = cell
    slots = [slot_ref[n] for n in range(KX * KY)]
    real_half = lax.broadcasted_iota(jnp.int32, (SUBLANES, LANES), 1) < HALF_LANES

    def turn_rest(value):
        moved = pltpu.roll(value, HALF_LANES, 1)
        return jnp.where(real_half, -moved, moved)

    def transform(load, turn, store):
        firsts = [four_points(*[load(slots[n * KY + m]) for n in range(KX)], turn) for m in range(KY)]
        for a in range(KX):
            seconds = four_points(*[firsts[m][a] for m in range(KY)], turn)
            for b in range(KY):
                store(a, b, seconds[b])

    for h in range(2):
        for c in range(sz.columns):
            near = 2 * sz.columns * h + c
            far = near + sz.columns

            def load(cell):
                return Pair(cells_ref[cell, near], cells_ref[cell, far])

            def store(a, b, value):
                grid_ref[b, a ^ plane, near] = value.real
                grid_ref[b, a ^ plane, far] = value.imag

            transform(load, Pair.turned, store)

    def load_rest(cell):
        return cells_ref[cell, sz.tail]

    def store_rest(a, b, value):
        grid_ref[b, a ^ plane, sz.tail] = value

    transform(load_rest, turn_rest, store_rest)
    for out_ref, step in zip(outs, OUT):
        out_ref[...] = grid_ref[step ^ seat]


def lattice_sum(sz, place, cell_offsets, cells):
    shape = jax.ShapeDtypeStruct((KX, sz.tail + 1, SUBLANES, LANES), F32)
    whole = pl.BlockSpec(memory_space=pltpu.VMEM)
    scalars = pl.BlockSpec(memory_space=pltpu.SMEM)
    return pl.pallas_call(
        functools.partial(lattice_kernel, sz),
        out_shape=[shape] * KY,
        in_specs=[scalars, scalars, whole],
        out_specs=[whole] * KY,
        scratch_shapes=[
            pltpu.VMEM((KY, KX, sz.tail + 1, SUBLANES, LANES), F32),
            pltpu.SMEM((KX * KY,), jnp.int32),
        ],
        compiler_params=pltpu.CompilerParams(vmem_limit_bytes=32 << 20),
        cost_estimate=cost(100000000000),
    )(place, cell_offsets, cells)


def band_kernel(sz, place_ref, *refs):
    halves, rights, outs = refs[:KY], refs[KY : KY + KX], refs[KY + KX : 2 * KY + KX]
    left_ref, band_ref, tile_ref, pack_ref = refs[2 * KY + KX :]
    wide = lax.broadcasted_iota(jnp.int32, (2 * KY, LANES), 1)
    ends = [None] * KY
    seat = place_ref[1]
    count = KY * sz.rows
    row = lax.broadcasted_iota(jnp.int32, (SUBLANES, LANES), 0)
    lane = lax.broadcasted_iota(jnp.int32, (SUBLANES, LANES), 1)
    low_lanes = lax.broadcasted_iota(jnp.int32, (2 * count, LANES), 1) < HALF_LANES
    for place, step in enumerate(OUT):
        left_ref[:, step ^ seat] = halves[place][...]

    for k in range(KX):
        left = left_ref[k]
        near, rest = [], []
        for part in range(2):
            tiles = []
            for c in range(sz.columns):
                first = part * sz.columns + c
                halves_of = [left[:, first], left[:, 2 * sz.columns + first]]
                tiles.append(jnp.stack(halves_of, axis=1).reshape(count, LANES))
            near.append(jnp.concatenate(tiles, axis=1))
            for p in range(KY):
                tail = left[p, sz.tail]
                head = pltpu.roll(tail, HALF_LANES, 1) if part else tail
                kept = [left[p, 2 * sz.columns + part * sz.columns + c] for c in range(sz.columns)]
                spare = jnp.concatenate(
                    [jnp.broadcast_to(tile[SUBLANES - 1 :], (SEGMENTS, LANES)) for tile in kept], axis=0
                )[:SUBLANES]
                spare = staggered(spare, row, sz.gap, LANES - SEGMENT)
                rest += [head, jnp.where(lane < sz.gap, pltpu.roll(head, LANES - sz.rest, 1), spare)]
        near_high, near_low = split(jnp.concatenate(near, axis=0))
        rest_high = jnp.concatenate(rest, axis=0)
        rest_low = rest_high - rest_high.astype(BF16).astype(F32)
        both = jnp.where(low_lanes, rest_high, pltpu.roll(rest_low, HALF_LANES, 1)).astype(BF16)
        rest_three = jnp.concatenate([both, rest_high.astype(BF16)[:, :HALF_LANES]], axis=1)
        right = rights[k]
        band = dot(jnp.concatenate([near_high, near_low], axis=0), right[: sz.main])
        band = band[: 2 * count] + band[2 * count :]
        band += dot(near_high, right[sz.main : 2 * sz.main]) + dot(rest_three, right[2 * sz.main :])
        width = 2 * LANES
        top, bottom = band[:count], band[count:]
        real = top[:, :width] - bottom[:, width:]
        imag = top[:, width:] + bottom[:, :width]
        for h in range(2):
            lanes = slice(h * LANES, (h + 1) * LANES)
            band_ref[h, 0] = real[:, lanes]
            band_ref[h, 1] = imag[:, lanes]
        for i in range(sz.bands):
            for h in range(2):
                for part in range(2):
                    tile_ref[2 * i + h, part * KY : (part + 1) * KY] = band_ref[
                        h, part, pl.ds(i, KY, stride=sz.rows)
                    ]
        for target in range(KY):
            for first in range(0, sz.pairs, LANES):
                last = min(first + LANES, sz.pairs)
                value = None
                begin, end = target * sz.pairs + first, target * sz.pairs + last
                for tile in range(begin // sz.vir_half, (end - 1) // sz.vir_half + 1):
                    offset = tile * sz.vir_half - begin
                    moved = pltpu.roll(tile_ref[tile], offset % LANES, 1) if offset % LANES else tile_ref[tile]
                    value = moved if value is None else jnp.where(wide < offset, value, moved)
                if last - first == LANES:
                    pack_ref[target, k * sz.full + first // LANES] = value
                else:
                    moved = pltpu.roll(value, k * sz.share, 1) if k else value
                    ends[target] = moved if k == 0 else jnp.where(wide < k * sz.share, ends[target], moved)
    for target in range(KY):
        if ends[target] is not None:
            pack_ref[target, KX * sz.full] = ends[target]
    for out_ref, step in zip(outs, BACK):
        out_ref[...] = pack_ref[step ^ seat]


def band_product(sz, place, halves, rights):
    count = KX * sz.full + (sz.pairs % LANES > 0)
    shape = jax.ShapeDtypeStruct((count, 2 * KY, LANES), F32)
    whole = pl.BlockSpec(memory_space=pltpu.VMEM)
    scalars = pl.BlockSpec(memory_space=pltpu.SMEM)
    return pl.pallas_call(
        functools.partial(band_kernel, sz),
        out_shape=[shape] * KY,
        in_specs=[scalars] + [whole] * (KY + KX),
        out_specs=[whole] * KY,
        scratch_shapes=[
            pltpu.VMEM((KX, KY, sz.tail + 1, SUBLANES, LANES), F32),
            pltpu.VMEM((2, 2, KY * sz.rows, LANES), F32),
            pltpu.VMEM((2 * sz.bands, 2 * KY, LANES), F32),
            pltpu.VMEM((KY, count, 2 * KY, LANES), F32),
        ],
        compiler_params=pltpu.CompilerParams(vmem_limit_bytes=32 << 20),
        cost_estimate=cost(10000000000),
    )(place, *halves, *rights)


def regroup_kernel(sz, place_ref, transfer_ref, *refs):
    sources, out_hbm = refs[:KY], refs[KY]
    row_ref, out_ref, sems = refs[KY + 1 :]
    plane, seat = place_ref[0], place_ref[1]
    cells = KX * KY
    starts = list(range(0, sz.pairs, LANES))
    pieces = [starts[i : i + PIECE] for i in range(0, len(starts), PIECE)]
    copies = []
    for index, piece in enumerate(pieces):
        for first in piece:
            last = min(first + LANES, sz.pairs)
            for source, step in enumerate(BACK):
                for k in range(KX):
                    row = transfer_ref[(k ^ plane) * KY + (step ^ seat)]
                    if last - first == LANES:
                        tile = sources[source][k * sz.full + first // LANES]
                    else:
                        tile = sources[source][KX * sz.full]
                        tile = pltpu.roll(tile, LANES - k * sz.share, 1) if k else tile
                    row_ref[first // LANES, pl.ds(row, 2 * KY, stride=cells)] = tile
            out_ref[:, first:last] = row_ref[first // LANES, :, : last - first]
        span = pl.ds(piece[0], min(piece[-1] + LANES, sz.pairs) - piece[0])
        copies.append(pltpu.make_async_copy(out_ref.at[:, span], out_hbm.at[:, span], sems.at[index]))
        copies[-1].start()
    for copy in copies:
        copy.wait()


def regroup(sz, place, transfer_index, sources):
    whole = pl.BlockSpec(memory_space=pltpu.VMEM)
    scalars = pl.BlockSpec(memory_space=pltpu.SMEM)
    rows = 2 * KY * KX * KY
    tiles = -(-sz.pairs // LANES)
    return pl.pallas_call(
        functools.partial(regroup_kernel, sz),
        out_shape=jax.ShapeDtypeStruct((rows, sz.pairs), F32),
        in_specs=[scalars, scalars] + [whole] * KY,
        out_specs=pl.BlockSpec(memory_space=pl.ANY),
        scratch_shapes=[
            pltpu.VMEM((tiles, rows, LANES), F32),
            pltpu.VMEM((rows, sz.pairs), F32),
            pltpu.SemaphoreType.DMA((-(-tiles // PIECE),)),
        ],
        compiler_params=pltpu.CompilerParams(vmem_limit_bytes=32 << 20),
    )(place, transfer_index, *sources)


def spread_kernel(sz, in_ref, *refs):
    out_ref = refs[-1]
    fill = jnp.zeros((sz.basis, LANES - sz.vir_half), F32)
    for part in range(2):
        out_ref[part] = jnp.concatenate([in_ref[:, part], fill], axis=1)


def spread(sz, value, flops, *after):
    whole = pl.BlockSpec(memory_space=pltpu.VMEM)
    return pl.pallas_call(
        functools.partial(spread_kernel, sz),
        out_shape=jax.ShapeDtypeStruct((2, sz.basis, LANES), F32),
        in_specs=[whole] + [pl.BlockSpec(memory_space=pl.ANY)] * len(after),
        out_specs=whole,
        compiler_params=pltpu.CompilerParams(vmem_limit_bytes=32 << 20),
        cost_estimate=cost(flops),
    )(value, *after)


def copy_kernel(in_ref, *refs):
    refs[-1][...] = in_ref[...]


def copied(value, *after):
    whole = pl.BlockSpec(memory_space=pltpu.VMEM)
    return pl.pallas_call(
        copy_kernel,
        out_shape=jax.ShapeDtypeStruct(value.shape, F32),
        in_specs=[whole] + [pl.BlockSpec(memory_space=pl.ANY)] * len(after),
        out_specs=whole,
        compiler_params=pltpu.CompilerParams(vmem_limit_bytes=32 << 20),
        cost_estimate=cost(10**6),
    )(value, *after)


def columns_kernel(sz, place_ref, own_ref, other_ref, out_ref):
    core = place_ref[2]
    under = jnp.zeros((sz.gap, LANES), F32)
    for part in range(2):
        mine, theirs = [jnp.concatenate([ref[part], under], axis=0) for ref in (own_ref, other_ref)]
        for h, value in enumerate([jnp.where(core == 0, mine, theirs), jnp.where(core == 0, theirs, mine)]):
            lanes = slice((2 * part + h) * LANES, (2 * part + h + 1) * LANES)
            high, low = split(value)
            out_ref[: sz.main, lanes] = high[: sz.main]
            out_ref[sz.main : 2 * sz.main, lanes] = low[: sz.main]
            for place, term in enumerate((high, high, low)):
                first = 2 * sz.main + place * HALF_LANES
                out_ref[first : first + HALF_LANES, lanes] = term[sz.main :]


def columns(sz, place, own, other, flops):
    whole = pl.BlockSpec(memory_space=pltpu.VMEM)
    scalars = pl.BlockSpec(memory_space=pltpu.SMEM)
    return pl.pallas_call(
        functools.partial(columns_kernel, sz),
        out_shape=jax.ShapeDtypeStruct((sz.depth, 4 * LANES), BF16),
        in_specs=[scalars, whole, whole],
        out_specs=whole,
        compiler_params=pltpu.CompilerParams(vmem_limit_bytes=32 << 20),
        cost_estimate=cost(flops),
    )(place, own, other)


def swap(value, step):
    return lax.ppermute(value, "cell", [(d, d ^ step) for d in range(KX * KY)])


def swap_cores(value):
    return lax.ppermute(value, "aux", [(0, 1), (1, 0)])


def by_planes(blocks, cell_offsets, occ_coeff, vir_coeff, transfer_index):
    sz = Sizes(blocks, occ_coeff, vir_coeff)
    me = lax.axis_index("cell")
    place = jnp.stack([me // KY, me % KY, lax.axis_index("aux")]).astype(jnp.int32)
    home = vir_coeff[0].transpose(1, 0, 2)
    across = spread(sz, swap(home, 2 * KY), 10000000000)
    beside = spread(sz, swap(home, KY), 100000000)
    corner = swap(across, KY)
    sent = half_bands(sz, blocks, occ_coeff).reshape(KX * KY, sz.tail + 1, SUBLANES, LANES)
    cells = lax.all_to_all(sent, "cell", split_axis=0, concat_axis=0, tiled=True)
    points = list(lattice_sum(sz, place, cell_offsets, cells))
    halves = [points[0]] + [swap(part, step) for part, step in zip(points[1:], OUT[1:])]
    ours = spread(sz, home, 3000000000, beside)
    if 1 == 1:
        corner = copied(corner, points[0])
    if 1 in (2, 3):
        corner = copied(corner, halves[1 - 1])
    rights = [columns(sz, place, v, swap_cores(v), 10000000000) for v in (ours, beside, across)]
    rights.append(columns(sz, place, corner, swap_cores(corner), 1000000000))
    bands = band_product(sz, place, halves, rights)
    sources = [bands[0]] + [swap(band, step) for band, step in zip(bands[1:], BACK[1:])]
    out = regroup(sz, place, transfer_index, sources)
    return out.reshape(2, sz.slab, KX * KY, sz.pairs)


def on_device(blocks, cell_offsets, occ_coeff, vir_coeff, transfer_index):
    arrays = (blocks, cell_offsets, occ_coeff, vir_coeff, transfer_index)
    if Sizes.fit(lax.axis_size("cell"), lax.axis_size("aux"), blocks, occ_coeff, vir_coeff):
        return by_planes(*arrays)
    return by_entries(*arrays)


def solution(mesh):
    placed = (P("cell", "aux", None, None), P(), P(), P("cell", None, None, "aux"), P())
    return jax.shard_map(
        on_device,
        mesh=mesh,
        in_specs=placed,
        out_specs=P(None, "aux", None, "cell"),
        check_vma=False,
    )
```

```python
import functools
import math

import jax
import jax.numpy as jnp
from jax import lax
from jax.experimental import pallas as pl
from jax.experimental.pallas import tpu as pltpu
from jax.sharding import PartitionSpec as P

KX = 4
KY = 4
LANES = 128
HALF_LANES = 64
SEGMENT = 32
PIECE = 2
OUT = (0, 1, 2, 3)
BACK = (0, 3, 2, 1)
SUBLANES = 8
SEGMENTS = LANES // SEGMENT
BF16 = jnp.bfloat16
F32 = jnp.float32


def phase_tables(cell_offsets, cell_count):
    depth = cell_count // (KX * KY)
    points = jnp.arange(cell_count, dtype=jnp.int32)
    along_a = points // (KY * depth)
    along_b = points // depth % KY
    along_c = points % depth
    turns = (
        along_a[:, None] * cell_offsets[0][None, :] * (KY * depth)
        + along_b[:, None] * cell_offsets[1][None, :] * (KX * depth)
        + along_c[:, None] * cell_offsets[2][None, :] * (KX * KY)
    ) % cell_count
    angles = 2.0 * math.pi / cell_count * turns.astype(jnp.float32)
    return (jnp.cos(angles), jnp.sin(angles))


def matmul(left, right):
    return jnp.dot(left, right, precision=lax.Precision.HIGHEST, preferred_element_type=jnp.float32)


def contract(form, left, right):
    return jnp.einsum(form, left, right, precision=lax.Precision.HIGHEST)


def by_entries(blocks, cell_offsets, occ_coeff, vir_coeff, transfer_index):
    cell_count = lax.axis_size("cell")
    slab_rows = blocks.shape[1]
    basis_size = blocks.shape[2]
    occupied = occ_coeff.shape[2]
    cosines, sines = phase_tables(cell_offsets, cell_count)
    occ_real, occ_imag = (occ_coeff[0], occ_coeff[1])
    flattened = blocks.reshape(1, -1)
    arrived = lax.all_to_all(flattened, "cell", split_axis=1, concat_axis=0, tiled=True)
    grid_real = matmul(cosines, arrived)
    grid_imag = matmul(sines, arrived)
    back_real, back_imag = (
        lax.all_to_all(grid_real, "cell", split_axis=0, concat_axis=1, tiled=True),
        lax.all_to_all(grid_imag, "cell", split_axis=0, concat_axis=1, tiled=True),
    )
    spec_real = back_real.reshape(slab_rows, basis_size, basis_size)
    spec_imag = back_imag.reshape(slab_rows, basis_size, basis_size)
    half_real = contract("mi,pmn->pin", occ_real, spec_real) + contract(
        "mi,pmn->pin", occ_imag, spec_imag
    )
    half_imag = contract("mi,pmn->pin", occ_real, spec_imag) - contract(
        "mi,pmn->pin", occ_imag, spec_real
    )
    rows_real = half_real.reshape(slab_rows * occupied, basis_size)
    rows_imag = half_imag.reshape(slab_rows * occupied, basis_size)
    column_piece = lax.all_gather(vir_coeff, "aux", axis=3, tiled=True)
    coef_real = column_piece[0, 0]
    coef_imag = column_piece[0, 1]
    part_real = matmul(rows_real, coef_real) - matmul(rows_imag, coef_imag)
    part_imag = matmul(rows_real, coef_imag) + matmul(rows_imag, coef_real)
    banded = jnp.stack([part_real, part_imag])
    pair_rows = banded.reshape(2, slab_rows, 1, -1)
    regrouped = lax.all_to_all(pair_rows, "cell", split_axis=3, concat_axis=2, tiled=True)
    source = jnp.argsort(transfer_index)
    return jnp.take(regrouped, source, axis=2)


def cost(flops):
    return pl.CostEstimate(flops=flops, bytes_accessed=flops // 100, transcendentals=0)


def split(value):
    high = value.astype(BF16)
    return high, (value - high.astype(F32)).astype(BF16)


def dot(left, right):
    return jnp.dot(left, right, preferred_element_type=F32)


class Sizes:
    def __init__(self, blocks, occ_coeff, vir_coeff):
        self.slab = blocks.shape[1]
        self.basis = blocks.shape[2]
        self.occ = occ_coeff.shape[2]
        self.vir_half = vir_coeff.shape[3]
        self.main = self.basis // LANES * LANES
        self.rest = self.basis - self.main
        self.columns = self.main // LANES
        self.gap = HALF_LANES - self.rest
        self.depth = 2 * self.main + 3 * HALF_LANES
        self.bands = self.occ // KX
        self.rows = 2 * SUBLANES
        self.tail = 4 * self.columns
        self.pairs = 2 * self.vir_half * self.bands // KY
        self.full = self.pairs // LANES
        self.share = LANES // KX

    @staticmethod
    def fit(cells, aux, blocks, occ_coeff, vir_coeff):
        basis, occ, half = blocks.shape[2], occ_coeff.shape[2], vir_coeff.shape[3]
        return (
            cells == KX * KY
            and aux == 2
            and blocks.shape[1] == KY
            and occ % KX == 0
            and basis > LANES
            and HALF_LANES // 2 <= basis % LANES <= HALF_LANES // 2 + SEGMENT // 2
            and SUBLANES <= occ // KX < 2 * SUBLANES
            and occ // KX - SUBLANES <= basis // LANES * (LANES // SEGMENT)
            and HALF_LANES < half <= LANES
            and 2 * half * (occ // KX) % KY == 0
            and 2 * half * (occ // KX) // KY % LANES <= LANES // KX
        )


def staggered(tile, row, first, stride):
    out = pltpu.roll(tile, first % LANES, 1)
    for r in range(1, SEGMENTS):
        out = jnp.where(row % SEGMENTS == r, pltpu.roll(tile, (first + r * stride) % LANES, 1), out)
    return out


def half_kernel(sz, block_hbm, occ_hbm, out_hbm, block_ref, occ_ref, out_ref, block_sem, occ_sem, out_sem):
    count = KX * sz.rows
    occ_copy = pltpu.make_async_copy(occ_hbm, occ_ref, occ_sem)
    block_copy = pltpu.make_async_copy(block_hbm, block_ref, block_sem)
    occ_copy.start()
    block_copy.start()
    place = lax.broadcasted_iota(jnp.int32, (count, sz.occ), 0)
    band = lax.broadcasted_iota(jnp.int32, (count, sz.occ), 1)
    inner = place % sz.rows
    pick = ((place // sz.rows * sz.bands + inner == band) & (inner < sz.bands)).astype(BF16)
    occ_copy.wait()
    terms = [split(occ_ref[:, part]) for part in range(2)]
    left_high = jnp.concatenate([dot(pick, terms[0][0]), -dot(pick, terms[1][0])], axis=0).astype(BF16)
    left_low = jnp.concatenate([dot(pick, terms[0][1]), -dot(pick, terms[1][1])], axis=0).astype(BF16)
    left = jnp.concatenate([left_high, left_low], axis=0)
    fill = jnp.zeros((sz.basis, LANES - sz.rest), F32)
    row = lax.broadcasted_iota(jnp.int32, (SUBLANES, LANES), 0)
    lane = lax.broadcasted_iota(jnp.int32, (SUBLANES, LANES), 1)
    block_copy.wait()
    for p in range(sz.slab):
        high, low = split(jnp.concatenate([block_ref[:, p], fill], axis=1))
        half = dot(left, high)
        half = half[: 2 * count] + half[2 * count :] + dot(left_high, low)
        real, imag = half[:count], half[count:]
        for z in range(KX):
            near = slice(z * sz.rows, z * sz.rows + SUBLANES)
            far = slice(z * sz.rows + SUBLANES, (z + 1) * sz.rows)
            tails = []
            for part, value in enumerate((real, imag)):
                head, last = value[near, sz.main :], value[far, sz.main :]
                tails.append(head + pltpu.roll(jnp.where(lane < sz.gap, last, 0.0), sz.rest, 1))
                spare = jnp.where(lane < sz.gap, 0.0, last)
                spare = staggered(spare, row, LANES - sz.gap, SEGMENT)
                for c in range(sz.columns):
                    lanes = slice(c * LANES, (c + 1) * LANES)
                    rows = slice(c * SEGMENTS, (c + 1) * SEGMENTS)
                    kept = jnp.sum(spare[rows], axis=0, keepdims=True)
                    tile = part * sz.columns + c
                    out_ref[z, p, tile] = value[near, lanes]
                    out_ref[z, p, 2 * sz.columns + tile] = jnp.where(row == SUBLANES - 1, kept, value[far, lanes])
            out_ref[z, p, sz.tail] = tails[0] + pltpu.roll(tails[1], HALF_LANES, 1)
        pltpu.make_async_copy(out_ref.at[:, p], out_hbm.at[:, p], out_sem.at[p]).start()
    for p in range(sz.slab):
        pltpu.make_async_copy(out_ref.at[:, p], out_hbm.at[:, p], out_sem.at[p]).wait()


def half_bands(sz, blocks, occ_coeff):
    anywhere = pl.BlockSpec(memory_space=pl.ANY)
    return pl.pallas_call(
        functools.partial(half_kernel, sz),
        out_shape=jax.ShapeDtypeStruct((KX, KY, sz.tail + 1, SUBLANES, LANES), F32),
        in_specs=[anywhere, anywhere],
        out_specs=anywhere,
        scratch_shapes=[
            pltpu.VMEM((sz.basis, sz.slab, sz.basis), F32),
            pltpu.VMEM((sz.occ, 2, sz.basis), F32),
            pltpu.VMEM((KX, KY, sz.tail + 1, SUBLANES, LANES), F32),
            pltpu.SemaphoreType.DMA,
            pltpu.SemaphoreType.DMA,
            pltpu.SemaphoreType.DMA((sz.slab,)),
        ],
        compiler_params=pltpu.CompilerParams(vmem_limit_bytes=60 << 20),
        cost_estimate=cost(10**11),
    )(blocks[0].transpose(1, 0, 2), occ_coeff.transpose(2, 0, 1))


def four_points(zero, one, two, three, turn):
    even, odd = zero + two, one + three
    lift, lean = zero - two, turn(one - three)
    return even + odd, lift + lean, even - odd, lift - lean


class Pair:
    def __init__(self, real, imag):
        self.real, self.imag = real, imag

    def __add__(self, other):
        return Pair(self.real + other.real, self.imag + other.imag)

    def __sub__(self, other):
        return Pair(self.real - other.real, self.imag - other.imag)

    def turned(self):
        return Pair(-self.imag, self.real)


def lattice_kernel(sz, place_ref, offset_ref, cells_ref, *refs):
    outs, grid_ref, slot_ref = refs[:KY], refs[KY], refs[KY + 1]
    plane, seat = place_ref[0], place_ref[1]
    for cell in range(KX * KY):
        slot_ref[(offset_ref[0, cell] & 3) * KY + (offset_ref[1, cell] & 3)] = cell
    slots = [slot_ref[n] for n in range(KX * KY)]
    real_half = lax.broadcasted_iota(jnp.int32, (SUBLANES, LANES), 1) < HALF_LANES

    def turn_rest(value):
        moved = pltpu.roll(value, HALF_LANES, 1)
        return jnp.where(real_half, -moved, moved)

    def transform(load, turn, store):
        firsts = [four_points(*[load(slots[n * KY + m]) for n in range(KX)], turn) for m in range(KY)]
        for a in range(KX):
            seconds = four_points(*[firsts[m][a] for m in range(KY)], turn)
            for b in range(KY):
                store(a, b, seconds[b])

    for h in range(2):
        for c in range(sz.columns):
            near = 2 * sz.columns * h + c
            far = near + sz.columns

            def load(cell):
                return Pair(cells_ref[cell, near], cells_ref[cell, far])

            def store(a, b, value):
                grid_ref[b, a ^ plane, near] = value.real
                grid_ref[b, a ^ plane, far] = value.imag

            transform(load, Pair.turned, store)

    def load_rest(cell):
        return cells_ref[cell, sz.tail]

    def store_rest(a, b, value):
        grid_ref[b, a ^ plane, sz.tail] = value

    transform(load_rest, turn_rest, store_rest)
    for out_ref, step in zip(outs, OUT):
        out_ref[...] = grid_ref[step ^ seat]


def lattice_sum(sz, place, cell_offsets, cells):
    shape = jax.ShapeDtypeStruct((KX, sz.tail + 1, SUBLANES, LANES), F32)
    whole = pl.BlockSpec(memory_space=pltpu.VMEM)
    scalars = pl.BlockSpec(memory_space=pltpu.SMEM)
    return pl.pallas_call(
        functools.partial(lattice_kernel, sz),
        out_shape=[shape] * KY,
        in_specs=[scalars, scalars, whole],
        out_specs=[whole] * KY,
        scratch_shapes=[
            pltpu.VMEM((KY, KX, sz.tail + 1, SUBLANES, LANES), F32),
            pltpu.SMEM((KX * KY,), jnp.int32),
        ],
        compiler_params=pltpu.CompilerParams(vmem_limit_bytes=32 << 20),
        cost_estimate=cost(10**11),
    )(place, cell_offsets, cells)


def band_kernel(sz, place_ref, *refs):
    halves, rights, outs = refs[:KY], refs[KY : KY + KX], refs[KY + KX : 2 * KY + KX]
    left_ref, band_ref, tile_ref, pack_ref = refs[2 * KY + KX :]
    wide = lax.broadcasted_iota(jnp.int32, (2 * KY, LANES), 1)
    ends = [None] * KY
    seat = place_ref[1]
    count = KY * sz.rows
    row = lax.broadcasted_iota(jnp.int32, (SUBLANES, LANES), 0)
    lane = lax.broadcasted_iota(jnp.int32, (SUBLANES, LANES), 1)
    low_lanes = lax.broadcasted_iota(jnp.int32, (2 * count, LANES), 1) < HALF_LANES
    for place, step in enumerate(OUT):
        left_ref[:, step ^ seat] = halves[place][...]

    for k in range(KX):
        left = left_ref[k]
        near, rest = [], []
        for part in range(2):
            tiles = []
            for c in range(sz.columns):
                first = part * sz.columns + c
                halves_of = [left[:, first], left[:, 2 * sz.columns + first]]
                tiles.append(jnp.stack(halves_of, axis=1).reshape(count, LANES))
            near.append(jnp.concatenate(tiles, axis=1))
            for p in range(KY):
                tail = left[p, sz.tail]
                head = pltpu.roll(tail, HALF_LANES, 1) if part else tail
                kept = [left[p, 2 * sz.columns + part * sz.columns + c] for c in range(sz.columns)]
                spare = jnp.concatenate(
                    [jnp.broadcast_to(tile[SUBLANES - 1 :], (SEGMENTS, LANES)) for tile in kept], axis=0
                )[:SUBLANES]
                spare = staggered(spare, row, sz.gap, LANES - SEGMENT)
                rest += [head, jnp.where(lane < sz.gap, pltpu.roll(head, LANES - sz.rest, 1), spare)]
        near_high, near_low = split(jnp.concatenate(near, axis=0))
        rest_high = jnp.concatenate(rest, axis=0)
        rest_low = rest_high - rest_high.astype(BF16).astype(F32)
        both = jnp.where(low_lanes, rest_high, pltpu.roll(rest_low, HALF_LANES, 1)).astype(BF16)
        rest_three = jnp.concatenate([both, rest_high.astype(BF16)[:, :HALF_LANES]], axis=1)
        right = rights[k]
        band = dot(jnp.concatenate([near_high, near_low], axis=0), right[: sz.main])
        band = band[: 2 * count] + band[2 * count :]
        band += dot(near_high, right[sz.main : 2 * sz.main]) + dot(rest_three, right[2 * sz.main :])
        width = 2 * LANES
        top, bottom = band[:count], band[count:]
        real = top[:, :width] - bottom[:, width:]
        imag = top[:, width:] + bottom[:, :width]
        for h in range(2):
            lanes = slice(h * LANES, (h + 1) * LANES)
            band_ref[h, 0] = real[:, lanes]
            band_ref[h, 1] = imag[:, lanes]
        for i in range(sz.bands):
            for h in range(2):
                for part in range(2):
                    tile_ref[2 * i + h, part * KY : (part + 1) * KY] = band_ref[
                        h, part, pl.ds(i, KY, stride=sz.rows)
                    ]
        for target in range(KY):
            for first in range(0, sz.pairs, LANES):
                last = min(first + LANES, sz.pairs)
                value = None
                begin, end = target * sz.pairs + first, target * sz.pairs + last
                for tile in range(begin // sz.vir_half, (end - 1) // sz.vir_half + 1):
                    offset = tile * sz.vir_half - begin
                    moved = pltpu.roll(tile_ref[tile], offset % LANES, 1) if offset % LANES else tile_ref[tile]
                    value = moved if value is None else jnp.where(wide < offset, value, moved)
                if last - first == LANES:
                    pack_ref[target, k * sz.full + first // LANES] = value
                else:
                    moved = pltpu.roll(value, k * sz.share, 1) if k else value
                    ends[target] = moved if k == 0 else jnp.where(wide < k * sz.share, ends[target], moved)
    for target in range(KY):
        if ends[target] is not None:
            pack_ref[target, KX * sz.full] = ends[target]
    for out_ref, step in zip(outs, BACK):
        out_ref[...] = pack_ref[step ^ seat]


def band_product(sz, place, halves, rights):
    count = KX * sz.full + (sz.pairs % LANES > 0)
    shape = jax.ShapeDtypeStruct((count, 2 * KY, LANES), F32)
    whole = pl.BlockSpec(memory_space=pltpu.VMEM)
    scalars = pl.BlockSpec(memory_space=pltpu.SMEM)
    return pl.pallas_call(
        functools.partial(band_kernel, sz),
        out_shape=[shape] * KY,
        in_specs=[scalars] + [whole] * (KY + KX),
        out_specs=[whole] * KY,
        scratch_shapes=[
            pltpu.VMEM((KX, KY, sz.tail + 1, SUBLANES, LANES), F32),
            pltpu.VMEM((2, 2, KY * sz.rows, LANES), F32),
            pltpu.VMEM((2 * sz.bands, 2 * KY, LANES), F32),
            pltpu.VMEM((KY, count, 2 * KY, LANES), F32),
        ],
        compiler_params=pltpu.CompilerParams(vmem_limit_bytes=32 << 20),
        cost_estimate=cost(10**10),
    )(place, *halves, *rights)


def regroup_kernel(sz, place_ref, transfer_ref, *refs):
    sources, out_hbm = refs[:KY], refs[KY]
    row_ref, out_ref, sems = refs[KY + 1 :]
    plane, seat = place_ref[0], place_ref[1]
    cells = KX * KY
    starts = list(range(0, sz.pairs, LANES))
    pieces = [starts[i : i + PIECE] for i in range(0, len(starts), PIECE)]
    copies = []
    for index, piece in enumerate(pieces):
        for first in piece:
            last = min(first + LANES, sz.pairs)
            for source, step in enumerate(BACK):
                for k in range(KX):
                    row = transfer_ref[(k ^ plane) * KY + (step ^ seat)]
                    if last - first == LANES:
                        tile = sources[source][k * sz.full + first // LANES]
                    else:
                        tile = sources[source][KX * sz.full]
                        tile = pltpu.roll(tile, LANES - k * sz.share, 1) if k else tile
                    row_ref[first // LANES, pl.ds(row, 2 * KY, stride=cells)] = tile
            out_ref[:, first:last] = row_ref[first // LANES, :, : last - first]
        span = pl.ds(piece[0], min(piece[-1] + LANES, sz.pairs) - piece[0])
        copies.append(pltpu.make_async_copy(out_ref.at[:, span], out_hbm.at[:, span], sems.at[index]))
        copies[-1].start()
    for copy in copies:
        copy.wait()


def regroup(sz, place, transfer_index, sources):
    whole = pl.BlockSpec(memory_space=pltpu.VMEM)
    scalars = pl.BlockSpec(memory_space=pltpu.SMEM)
    rows = 2 * KY * KX * KY
    tiles = -(-sz.pairs // LANES)
    return pl.pallas_call(
        functools.partial(regroup_kernel, sz),
        out_shape=jax.ShapeDtypeStruct((rows, sz.pairs), F32),
        in_specs=[scalars, scalars] + [whole] * KY,
        out_specs=pl.BlockSpec(memory_space=pl.ANY),
        scratch_shapes=[
            pltpu.VMEM((tiles, rows, LANES), F32),
            pltpu.VMEM((rows, sz.pairs), F32),
            pltpu.SemaphoreType.DMA((-(-tiles // PIECE),)),
        ],
        compiler_params=pltpu.CompilerParams(vmem_limit_bytes=32 << 20),
    )(place, transfer_index, *sources)


def spread_kernel(sz, in_ref, *refs):
    out_ref = refs[-1]
    fill = jnp.zeros((sz.basis, LANES - sz.vir_half), F32)
    for part in range(2):
        out_ref[part] = jnp.concatenate([in_ref[:, part], fill], axis=1)


def spread(sz, value, flops, *after):
    whole = pl.BlockSpec(memory_space=pltpu.VMEM)
    return pl.pallas_call(
        functools.partial(spread_kernel, sz),
        out_shape=jax.ShapeDtypeStruct((2, sz.basis, LANES), F32),
        in_specs=[whole] + [pl.BlockSpec(memory_space=pl.ANY)] * len(after),
        out_specs=whole,
        compiler_params=pltpu.CompilerParams(vmem_limit_bytes=32 << 20),
        cost_estimate=cost(flops),
    )(value, *after)


def copy_kernel(in_ref, *refs):
    refs[-1][...] = in_ref[...]


def copied(value, *after):
    whole = pl.BlockSpec(memory_space=pltpu.VMEM)
    return pl.pallas_call(
        copy_kernel,
        out_shape=jax.ShapeDtypeStruct(value.shape, F32),
        in_specs=[whole] + [pl.BlockSpec(memory_space=pl.ANY)] * len(after),
        out_specs=whole,
        compiler_params=pltpu.CompilerParams(vmem_limit_bytes=32 << 20),
        cost_estimate=cost(10**6),
    )(value, *after)


def columns_kernel(sz, place_ref, own_ref, other_ref, out_ref):
    core = place_ref[2]
    under = jnp.zeros((sz.gap, LANES), F32)
    for part in range(2):
        mine, theirs = [jnp.concatenate([ref[part], under], axis=0) for ref in (own_ref, other_ref)]
        for h, value in enumerate([jnp.where(core == 0, mine, theirs), jnp.where(core == 0, theirs, mine)]):
            lanes = slice((2 * part + h) * LANES, (2 * part + h + 1) * LANES)
            high, low = split(value)
            out_ref[: sz.main, lanes] = high[: sz.main]
            out_ref[sz.main : 2 * sz.main, lanes] = low[: sz.main]
            for place, term in enumerate((high, high, low)):
                first = 2 * sz.main + place * HALF_LANES
                out_ref[first : first + HALF_LANES, lanes] = term[sz.main :]


def columns(sz, place, own, other, flops):
    whole = pl.BlockSpec(memory_space=pltpu.VMEM)
    scalars = pl.BlockSpec(memory_space=pltpu.SMEM)
    return pl.pallas_call(
        functools.partial(columns_kernel, sz),
        out_shape=jax.ShapeDtypeStruct((sz.depth, 4 * LANES), BF16),
        in_specs=[scalars, whole, whole],
        out_specs=whole,
        compiler_params=pltpu.CompilerParams(vmem_limit_bytes=32 << 20),
        cost_estimate=cost(flops),
    )(place, own, other)


def swap(value, step):
    return lax.ppermute(value, "cell", [(d, d ^ step) for d in range(KX * KY)])


def swap_cores(value):
    return lax.ppermute(value, "aux", [(0, 1), (1, 0)])


def by_planes(blocks, cell_offsets, occ_coeff, vir_coeff, transfer_index):
    sz = Sizes(blocks, occ_coeff, vir_coeff)
    me = lax.axis_index("cell")
    place = jnp.stack([me // KY, me % KY, lax.axis_index("aux")]).astype(jnp.int32)
    home = vir_coeff[0].transpose(1, 0, 2)
    across = spread(sz, swap(home, 2 * KY), 10**10)
    beside = spread(sz, swap(home, KY), 10**8)
    corner = swap(across, KY)
    sent = half_bands(sz, blocks, occ_coeff).reshape(KX * KY, sz.tail + 1, SUBLANES, LANES)
    cells = lax.all_to_all(sent, "cell", split_axis=0, concat_axis=0, tiled=True)
    points = list(lattice_sum(sz, place, cell_offsets, cells))
    halves = [points[0]] + [swap(part, step) for part, step in zip(points[1:], OUT[1:])]
    ours = spread(sz, home, 3 * 10**9, beside)
    corner = copied(corner, points[0])
    rights = [columns(sz, place, v, swap_cores(v), 10**10) for v in (ours, beside, across)]
    rights.append(columns(sz, place, corner, swap_cores(corner), 10**9))
    bands = band_product(sz, place, halves, rights)
    sources = [bands[0]] + [swap(band, step) for band, step in zip(bands[1:], BACK[1:])]
    out = regroup(sz, place, transfer_index, sources)
    return out.reshape(2, sz.slab, KX * KY, sz.pairs)


def on_device(blocks, cell_offsets, occ_coeff, vir_coeff, transfer_index):
    arrays = (blocks, cell_offsets, occ_coeff, vir_coeff, transfer_index)
    if Sizes.fit(lax.axis_size("cell"), lax.axis_size("aux"), blocks, occ_coeff, vir_coeff):
        return by_planes(*arrays)
    return by_entries(*arrays)


def solution(mesh):
    placed = (P("cell", "aux", None, None), P(), P(), P("cell", None, None, "aux"), P())
    return jax.shard_map(
        on_device,
        mesh=mesh,
        in_specs=placed,
        out_specs=P(None, "aux", None, "cell"),
        check_vma=False,
    )
```

```python
import functools
import math

import jax
import jax.numpy as jnp
from jax import lax
from jax.experimental import pallas as pl
from jax.experimental.pallas import tpu as pltpu
from jax.sharding import PartitionSpec as P

KX = 4
KY = 4
LANES = 128
HALF_LANES = 64
SEGMENT = 32
PIECE = 2
OUT = (0, 1, 2, 3)
BACK = (0, 3, 2, 1)
SUBLANES = 8
SEGMENTS = LANES // SEGMENT
BF16 = jnp.bfloat16
F32 = jnp.float32


def phase_tables(cell_offsets, cell_count):
    depth = cell_count // (KX * KY)
    points = jnp.arange(cell_count, dtype=jnp.int32)
    along_a = points // (KY * depth)
    along_b = points // depth % KY
    along_c = points % depth
    turns = (
        along_a[:, None] * cell_offsets[0][None, :] * (KY * depth)
        + along_b[:, None] * cell_offsets[1][None, :] * (KX * depth)
        + along_c[:, None] * cell_offsets[2][None, :] * (KX * KY)
    ) % cell_count
    angles = 2.0 * math.pi / cell_count * turns.astype(jnp.float32)
    return (jnp.cos(angles), jnp.sin(angles))


def matmul(left, right):
    return jnp.dot(left, right, precision=lax.Precision.HIGHEST, preferred_element_type=jnp.float32)


def contract(form, left, right):
    return jnp.einsum(form, left, right, precision=lax.Precision.HIGHEST)


def by_entries(blocks, cell_offsets, occ_coeff, vir_coeff, transfer_index):
    cell_count = lax.axis_size("cell")
    slab_rows = blocks.shape[1]
    basis_size = blocks.shape[2]
    occupied = occ_coeff.shape[2]
    cosines, sines = phase_tables(cell_offsets, cell_count)
    occ_real, occ_imag = (occ_coeff[0], occ_coeff[1])
    flattened = blocks.reshape(1, -1)
    arrived = lax.all_to_all(flattened, "cell", split_axis=1, concat_axis=0, tiled=True)
    grid_real = matmul(cosines, arrived)
    grid_imag = matmul(sines, arrived)
    back_real, back_imag = (
        lax.all_to_all(grid_real, "cell", split_axis=0, concat_axis=1, tiled=True),
        lax.all_to_all(grid_imag, "cell", split_axis=0, concat_axis=1, tiled=True),
    )
    spec_real = back_real.reshape(slab_rows, basis_size, basis_size)
    spec_imag = back_imag.reshape(slab_rows, basis_size, basis_size)
    half_real = contract("mi,pmn->pin", occ_real, spec_real) + contract(
        "mi,pmn->pin", occ_imag, spec_imag
    )
    half_imag = contract("mi,pmn->pin", occ_real, spec_imag) - contract(
        "mi,pmn->pin", occ_imag, spec_real
    )
    rows_real = half_real.reshape(slab_rows * occupied, basis_size)
    rows_imag = half_imag.reshape(slab_rows * occupied, basis_size)
    column_piece = lax.all_gather(vir_coeff, "aux", axis=3, tiled=True)
    coef_real = column_piece[0, 0]
    coef_imag = column_piece[0, 1]
    part_real = matmul(rows_real, coef_real) - matmul(rows_imag, coef_imag)
    part_imag = matmul(rows_real, coef_imag) + matmul(rows_imag, coef_real)
    banded = jnp.stack([part_real, part_imag])
    pair_rows = banded.reshape(2, slab_rows, 1, -1)
    regrouped = lax.all_to_all(pair_rows, "cell", split_axis=3, concat_axis=2, tiled=True)
    source = jnp.argsort(transfer_index)
    return jnp.take(regrouped, source, axis=2)


def cost(flops):
    return pl.CostEstimate(flops=flops, bytes_accessed=flops // 100, transcendentals=0)


def split(value):
    high = value.astype(BF16)
    return high, (value - high.astype(F32)).astype(BF16)


def dot(left, right):
    return jnp.dot(left, right, preferred_element_type=F32)


class Sizes:
    def __init__(self, blocks, occ_coeff, vir_coeff):
        self.slab = blocks.shape[1]
        self.basis = blocks.shape[2]
        self.occ = occ_coeff.shape[2]
        self.vir_half = vir_coeff.shape[3]
        self.main = self.basis // LANES * LANES
        self.rest = self.basis - self.main
        self.columns = self.main // LANES
        self.gap = HALF_LANES - self.rest
        self.depth = 2 * self.main + 3 * HALF_LANES
        self.bands = self.occ // KX
        self.rows = 2 * SUBLANES
        self.tail = 4 * self.columns
        self.pairs = 2 * self.vir_half * self.bands // KY
        self.full = self.pairs // LANES
        self.share = LANES // KX

    @staticmethod
    def fit(cells, aux, blocks, occ_coeff, vir_coeff):
        basis, occ, half = blocks.shape[2], occ_coeff.shape[2], vir_coeff.shape[3]
        return (
            cells == KX * KY
            and aux == 2
            and blocks.shape[1] == KY
            and occ % KX == 0
            and basis > LANES
            and HALF_LANES // 2 <= basis % LANES <= HALF_LANES // 2 + SEGMENT // 2
            and SUBLANES <= occ // KX < 2 * SUBLANES
            and occ // KX - SUBLANES <= basis // LANES * (LANES // SEGMENT)
            and HALF_LANES < half <= LANES
            and 2 * half * (occ // KX) % KY == 0
            and 2 * half * (occ // KX) // KY % LANES <= LANES // KX
        )


def staggered(tile, row, first, stride):
    out = pltpu.roll(tile, first % LANES, 1)
    for r in range(1, SEGMENTS):
        out = jnp.where(row % SEGMENTS == r, pltpu.roll(tile, (first + r * stride) % LANES, 1), out)
    return out


def half_kernel(sz, block_hbm, occ_hbm, out_hbm, block_ref, occ_ref, out_ref, block_sem, occ_sem, out_sem):
    count = KX * sz.rows
    occ_copy = pltpu.make_async_copy(occ_hbm, occ_ref, occ_sem)
    block_copy = pltpu.make_async_copy(block_hbm, block_ref, block_sem)
    occ_copy.start()
    block_copy.start()
    place = lax.broadcasted_iota(jnp.int32, (count, sz.occ), 0)
    band = lax.broadcasted_iota(jnp.int32, (count, sz.occ), 1)
    inner = place % sz.rows
    pick = ((place // sz.rows * sz.bands + inner == band) & (inner < sz.bands)).astype(BF16)
    occ_copy.wait()
    terms = [split(occ_ref[:, part]) for part in range(2)]
    left_high = jnp.concatenate([dot(pick, terms[0][0]), -dot(pick, terms[1][0])], axis=0).astype(BF16)
    left_low = jnp.concatenate([dot(pick, terms[0][1]), -dot(pick, terms[1][1])], axis=0).astype(BF16)
    left = jnp.concatenate([left_high, left_low], axis=0)
    fill = jnp.zeros((sz.basis, LANES - sz.rest), F32)
    row = lax.broadcasted_iota(jnp.int32, (SUBLANES, LANES), 0)
    lane = lax.broadcasted_iota(jnp.int32, (SUBLANES, LANES), 1)
    block_copy.wait()
    for p in range(sz.slab):
        high, low = split(jnp.concatenate([block_ref[:, p], fill], axis=1))
        half = dot(left, high)
        half = half[: 2 * count] + half[2 * count :] + dot(left_high, low)
        real, imag = half[:count], half[count:]
        for z in range(KX):
            near = slice(z * sz.rows, z * sz.rows + SUBLANES)
            far = slice(z * sz.rows + SUBLANES, (z + 1) * sz.rows)
            tails = []
            for part, value in enumerate((real, imag)):
                head, last = value[near, sz.main :], value[far, sz.main :]
                tails.append(head + pltpu.roll(jnp.where(lane < sz.gap, last, 0.0), sz.rest, 1))
                spare = jnp.where(lane < sz.gap, 0.0, last)
                spare = staggered(spare, row, LANES - sz.gap, SEGMENT)
                for c in range(sz.columns):
                    lanes = slice(c * LANES, (c + 1) * LANES)
                    rows = slice(c * SEGMENTS, (c + 1) * SEGMENTS)
                    kept = jnp.sum(spare[rows], axis=0, keepdims=True)
                    tile = part * sz.columns + c
                    out_ref[z, p, tile] = value[near, lanes]
                    out_ref[z, p, 2 * sz.columns + tile] = jnp.where(row == SUBLANES - 1, kept, value[far, lanes])
            out_ref[z, p, sz.tail] = tails[0] + pltpu.roll(tails[1], HALF_LANES, 1)
        pltpu.make_async_copy(out_ref.at[:, p], out_hbm.at[:, p], out_sem.at[p]).start()
    for p in range(sz.slab):
        pltpu.make_async_copy(out_ref.at[:, p], out_hbm.at[:, p], out_sem.at[p]).wait()


def half_bands(sz, blocks, occ_coeff):
    anywhere = pl.BlockSpec(memory_space=pl.ANY)
    return pl.pallas_call(
        functools.partial(half_kernel, sz),
        out_shape=jax.ShapeDtypeStruct((KX, KY, sz.tail + 1, SUBLANES, LANES), F32),
        in_specs=[anywhere, anywhere],
        out_specs=anywhere,
        scratch_shapes=[
            pltpu.VMEM((sz.basis, sz.slab, sz.basis), F32),
            pltpu.VMEM((sz.occ, 2, sz.basis), F32),
            pltpu.VMEM((KX, KY, sz.tail + 1, SUBLANES, LANES), F32),
            pltpu.SemaphoreType.DMA,
            pltpu.SemaphoreType.DMA,
            pltpu.SemaphoreType.DMA((sz.slab,)),
        ],
        compiler_params=pltpu.CompilerParams(vmem_limit_bytes=60 << 20),
        cost_estimate=cost(10**11),
    )(blocks[0].transpose(1, 0, 2), occ_coeff.transpose(2, 0, 1))


def four_points(zero, one, two, three, turn):
    even, odd = zero + two, one + three
    lift, lean = zero - two, turn(one - three)
    return even + odd, lift + lean, even - odd, lift - lean


class Pair:
    def __init__(self, real, imag):
        self.real, self.imag = real, imag

    def __add__(self, other):
        return Pair(self.real + other.real, self.imag + other.imag)

    def __sub__(self, other):
        return Pair(self.real - other.real, self.imag - other.imag)

    def turned(self):
        return Pair(-self.imag, self.real)


def lattice_kernel(sz, place_ref, offset_ref, cells_ref, *refs):
    outs, grid_ref, slot_ref = refs[:KY], refs[KY], refs[KY + 1]
    plane, seat = place_ref[0], place_ref[1]
    for cell in range(KX * KY):
        slot_ref[(offset_ref[0, cell] & 3) * KY + (offset_ref[1, cell] & 3)] = cell
    slots = [slot_ref[n] for n in range(KX * KY)]
    real_half = lax.broadcasted_iota(jnp.int32, (SUBLANES, LANES), 1) < HALF_LANES

    def turn_rest(value):
        moved = pltpu.roll(value, HALF_LANES, 1)
        return jnp.where(real_half, -moved, moved)

    def transform(load, turn, store):
        firsts = [four_points(*[load(slots[n * KY + m]) for n in range(KX)], turn) for m in range(KY)]
        for a in range(KX):
            seconds = four_points(*[firsts[m][a] for m in range(KY)], turn)
            for b in range(KY):
                store(a, b, seconds[b])

    for h in range(2):
        for c in range(sz.columns):
            near = 2 * sz.columns * h + c
            far = near + sz.columns

            def load(cell):
                return Pair(cells_ref[cell, near], cells_ref[cell, far])

            def store(a, b, value):
                grid_ref[b, a ^ plane, near] = value.real
                grid_ref[b, a ^ plane, far] = value.imag

            transform(load, Pair.turned, store)

    def load_rest(cell):
        return cells_ref[cell, sz.tail]

    def store_rest(a, b, value):
        grid_ref[b, a ^ plane, sz.tail] = value

    transform(load_rest, turn_rest, store_rest)
    for out_ref, step in zip(outs, OUT):
        out_ref[...] = grid_ref[step ^ seat]


def lattice_sum(sz, place, cell_offsets, cells):
    shape = jax.ShapeDtypeStruct((KX, sz.tail + 1, SUBLANES, LANES), F32)
    whole = pl.BlockSpec(memory_space=pltpu.VMEM)
    scalars = pl.BlockSpec(memory_space=pltpu.SMEM)
    return pl.pallas_call(
        functools.partial(lattice_kernel, sz),
        out_shape=[shape] * KY,
        in_specs=[scalars, scalars, whole],
        out_specs=[whole] * KY,
        scratch_shapes=[
            pltpu.VMEM((KY, KX, sz.tail + 1, SUBLANES, LANES), F32),
            pltpu.SMEM((KX * KY,), jnp.int32),
        ],
        compiler_params=pltpu.CompilerParams(vmem_limit_bytes=32 << 20),
        cost_estimate=cost(10**11),
    )(place, cell_offsets, cells)


def band_kernel(sz, place_ref, *refs):
    halves, rights, outs = refs[:KY], refs[KY : KY + KX], refs[KY + KX : 2 * KY + KX]
    left_ref, band_ref, tile_ref, pack_ref = refs[2 * KY + KX :]
    wide = lax.broadcasted_iota(jnp.int32, (2 * KY, LANES), 1)
    ends = [None] * KY
    seat = place_ref[1]
    count = KY * sz.rows
    row = lax.broadcasted_iota(jnp.int32, (SUBLANES, LANES), 0)
    lane = lax.broadcasted_iota(jnp.int32, (SUBLANES, LANES), 1)
    low_lanes = lax.broadcasted_iota(jnp.int32, (2 * count, LANES), 1) < HALF_LANES
    for place, step in enumerate(OUT):
        left_ref[:, step ^ seat] = halves[place][...]

    for k in range(KX):
        left = left_ref[k]
        near, rest = [], []
        for part in range(2):
            tiles = []
            for c in range(sz.columns):
                first = part * sz.columns + c
                halves_of = [left[:, first], left[:, 2 * sz.columns + first]]
                tiles.append(jnp.stack(halves_of, axis=1).reshape(count, LANES))
            near.append(jnp.concatenate(tiles, axis=1))
            for p in range(KY):
                tail = left[p, sz.tail]
                head = pltpu.roll(tail, HALF_LANES, 1) if part else tail
                kept = [left[p, 2 * sz.columns + part * sz.columns + c] for c in range(sz.columns)]
                spare = jnp.concatenate(
                    [jnp.broadcast_to(tile[SUBLANES - 1 :], (SEGMENTS, LANES)) for tile in kept], axis=0
                )[:SUBLANES]
                spare = staggered(spare, row, sz.gap, LANES - SEGMENT)
                rest += [head, jnp.where(lane < sz.gap, pltpu.roll(head, LANES - sz.rest, 1), spare)]
        near_high, near_low = split(jnp.concatenate(near, axis=0))
        rest_high = jnp.concatenate(rest, axis=0)
        rest_low = rest_high - rest_high.astype(BF16).astype(F32)
        both = jnp.where(low_lanes, rest_high, pltpu.roll(rest_low, HALF_LANES, 1)).astype(BF16)
        rest_three = jnp.concatenate([both, rest_high.astype(BF16)[:, :HALF_LANES]], axis=1)
        right = rights[k]
        band = dot(jnp.concatenate([near_high, near_low], axis=0), right[: sz.main])
        band = band[: 2 * count] + band[2 * count :]
        band += dot(near_high, right[sz.main : 2 * sz.main]) + dot(rest_three, right[2 * sz.main :])
        width = 2 * LANES
        top, bottom = band[:count], band[count:]
        real = top[:, :width] - bottom[:, width:]
        imag = top[:, width:] + bottom[:, :width]
        for h in range(2):
            lanes = slice(h * LANES, (h + 1) * LANES)
            band_ref[h, 0] = real[:, lanes]
            band_ref[h, 1] = imag[:, lanes]
        for i in range(sz.bands):
            for h in range(2):
                for part in range(2):
                    tile_ref[2 * i + h, part * KY : (part + 1) * KY] = band_ref[
                        h, part, pl.ds(i, KY, stride=sz.rows)
                    ]
        for target in range(KY):
            for first in range(0, sz.pairs, LANES):
                last = min(first + LANES, sz.pairs)
                value = None
                begin, end = target * sz.pairs + first, target * sz.pairs + last
                for tile in range(begin // sz.vir_half, (end - 1) // sz.vir_half + 1):
                    offset = tile * sz.vir_half - begin
                    moved = pltpu.roll(tile_ref[tile], offset % LANES, 1) if offset % LANES else tile_ref[tile]
                    value = moved if value is None else jnp.where(wide < offset, value, moved)
                if last - first == LANES:
                    pack_ref[target, k * sz.full + first // LANES] = value
                else:
                    moved = pltpu.roll(value, k * sz.share, 1) if k else value
                    ends[target] = moved if k == 0 else jnp.where(wide < k * sz.share, ends[target], moved)
    for target in range(KY):
        if ends[target] is not None:
            pack_ref[target, KX * sz.full] = ends[target]
    for out_ref, step in zip(outs, BACK):
        out_ref[...] = pack_ref[step ^ seat]


def band_product(sz, place, halves, rights):
    count = KX * sz.full + (sz.pairs % LANES > 0)
    shape = jax.ShapeDtypeStruct((count, 2 * KY, LANES), F32)
    whole = pl.BlockSpec(memory_space=pltpu.VMEM)
    scalars = pl.BlockSpec(memory_space=pltpu.SMEM)
    return pl.pallas_call(
        functools.partial(band_kernel, sz),
        out_shape=[shape] * KY,
        in_specs=[scalars] + [whole] * (KY + KX),
        out_specs=[whole] * KY,
        scratch_shapes=[
            pltpu.VMEM((KX, KY, sz.tail + 1, SUBLANES, LANES), F32),
            pltpu.VMEM((2, 2, KY * sz.rows, LANES), F32),
            pltpu.VMEM((2 * sz.bands, 2 * KY, LANES), F32),
            pltpu.VMEM((KY, count, 2 * KY, LANES), F32),
        ],
        compiler_params=pltpu.CompilerParams(vmem_limit_bytes=32 << 20),
        cost_estimate=cost(10**10),
    )(place, *halves, *rights)


def regroup_kernel(sz, place_ref, transfer_ref, *refs):
    sources, out_hbm = refs[:KY], refs[KY]
    row_ref, out_ref, sems = refs[KY + 1 :]
    plane, seat = place_ref[0], place_ref[1]
    cells = KX * KY
    starts = list(range(0, sz.pairs, LANES))
    pieces = [starts[i : i + PIECE] for i in range(0, len(starts), PIECE)]
    copies = []
    for index, piece in enumerate(pieces):
        for first in piece:
            last = min(first + LANES, sz.pairs)
            for source, step in enumerate(BACK):
                for k in range(KX):
                    row = transfer_ref[(k ^ plane) * KY + (step ^ seat)]
                    if last - first == LANES:
                        tile = sources[source][k * sz.full + first // LANES]
                    else:
                        tile = sources[source][KX * sz.full]
                        tile = pltpu.roll(tile, LANES - k * sz.share, 1) if k else tile
                    row_ref[first // LANES, pl.ds(row, 2 * KY, stride=cells)] = tile
            out_ref[:, first:last] = row_ref[first // LANES, :, : last - first]
        span = pl.ds(piece[0], min(piece[-1] + LANES, sz.pairs) - piece[0])
        copies.append(pltpu.make_async_copy(out_ref.at[:, span], out_hbm.at[:, span], sems.at[index]))
        copies[-1].start()
    for copy in copies:
        copy.wait()


def regroup(sz, place, transfer_index, sources):
    whole = pl.BlockSpec(memory_space=pltpu.VMEM)
    scalars = pl.BlockSpec(memory_space=pltpu.SMEM)
    rows = 2 * KY * KX * KY
    tiles = -(-sz.pairs // LANES)
    return pl.pallas_call(
        functools.partial(regroup_kernel, sz),
        out_shape=jax.ShapeDtypeStruct((rows, sz.pairs), F32),
        in_specs=[scalars, scalars] + [whole] * KY,
        out_specs=pl.BlockSpec(memory_space=pl.ANY),
        scratch_shapes=[
            pltpu.VMEM((tiles, rows, LANES), F32),
            pltpu.VMEM((rows, sz.pairs), F32),
            pltpu.SemaphoreType.DMA((-(-tiles // PIECE),)),
        ],
        compiler_params=pltpu.CompilerParams(vmem_limit_bytes=32 << 20),
    )(place, transfer_index, *sources)


def spread_kernel(sz, in_ref, *refs):
    out_ref = refs[-1]
    fill = jnp.zeros((sz.basis, LANES - sz.vir_half), F32)
    for part in range(2):
        out_ref[part] = jnp.concatenate([in_ref[:, part], fill], axis=1)


def spread(sz, value, flops, *after):
    whole = pl.BlockSpec(memory_space=pltpu.VMEM)
    return pl.pallas_call(
        functools.partial(spread_kernel, sz),
        out_shape=jax.ShapeDtypeStruct((2, sz.basis, LANES), F32),
        in_specs=[whole] + [pl.BlockSpec(memory_space=pl.ANY)] * len(after),
        out_specs=whole,
        compiler_params=pltpu.CompilerParams(vmem_limit_bytes=32 << 20),
        cost_estimate=cost(flops),
    )(value, *after)


def copy_kernel(in_ref, *refs):
    refs[-1][...] = in_ref[...]


def copied(value, *after):
    whole = pl.BlockSpec(memory_space=pltpu.VMEM)
    return pl.pallas_call(
        copy_kernel,
        out_shape=jax.ShapeDtypeStruct(value.shape, F32),
        in_specs=[whole] + [pl.BlockSpec(memory_space=pl.ANY)] * len(after),
        out_specs=whole,
        compiler_params=pltpu.CompilerParams(vmem_limit_bytes=32 << 20),
        cost_estimate=cost(10**6),
    )(value, *after)


def columns_kernel(sz, place_ref, own_ref, other_ref, out_ref):
    core = place_ref[2]
    under = jnp.zeros((sz.gap, LANES), F32)
    for part in range(2):
        mine, theirs = [jnp.concatenate([ref[part], under], axis=0) for ref in (own_ref, other_ref)]
        for h, value in enumerate([jnp.where(core == 0, mine, theirs), jnp.where(core == 0, theirs, mine)]):
            lanes = slice((2 * part + h) * LANES, (2 * part + h + 1) * LANES)
            high, low = split(value)
            out_ref[: sz.main, lanes] = high[: sz.main]
            out_ref[sz.main : 2 * sz.main, lanes] = low[: sz.main]
            for place, term in enumerate((high, high, low)):
                first = 2 * sz.main + place * HALF_LANES
                out_ref[first : first + HALF_LANES, lanes] = term[sz.main :]


def columns(sz, place, own, other, flops):
    whole = pl.BlockSpec(memory_space=pltpu.VMEM)
    scalars = pl.BlockSpec(memory_space=pltpu.SMEM)
    return pl.pallas_call(
        functools.partial(columns_kernel, sz),
        out_shape=jax.ShapeDtypeStruct((sz.depth, 4 * LANES), BF16),
        in_specs=[scalars, whole, whole],
        out_specs=whole,
        compiler_params=pltpu.CompilerParams(vmem_limit_bytes=32 << 20),
        cost_estimate=cost(flops),
    )(place, own, other)


def swap(value, step):
    return lax.ppermute(value, "cell", [(d, d ^ step) for d in range(KX * KY)])


def swap_cores(value):
    return lax.ppermute(value, "aux", [(0, 1), (1, 0)])


def by_planes(blocks, cell_offsets, occ_coeff, vir_coeff, transfer_index):
    sz = Sizes(blocks, occ_coeff, vir_coeff)
    me = lax.axis_index("cell")
    place = jnp.stack([me // KY, me % KY, lax.axis_index("aux")]).astype(jnp.int32)
    home = vir_coeff[0].transpose(1, 0, 2)
    across = spread(sz, swap(home, 3 * KY), 10**10)
    beside = spread(sz, swap(home, KY), 10**8)
    corner = swap(across, KY)
    sent = half_bands(sz, blocks, occ_coeff).reshape(KX * KY, sz.tail + 1, SUBLANES, LANES)
    cells = lax.all_to_all(sent, "cell", split_axis=0, concat_axis=0, tiled=True)
    points = list(lattice_sum(sz, place, cell_offsets, cells))
    halves = [points[0]] + [swap(part, step) for part, step in zip(points[1:], OUT[1:])]
    ours = spread(sz, home, 3 * 10**9, beside)
    corner = copied(corner, points[0])
    rights = [columns(sz, place, v, swap_cores(v), 10**10) for v in (ours, beside, across)]
    rights.insert(2, columns(sz, place, corner, swap_cores(corner), 10**9))
    bands = band_product(sz, place, halves, rights)
    sources = [bands[0]] + [swap(band, step) for band, step in zip(bands[1:], BACK[1:])]
    out = regroup(sz, place, transfer_index, sources)
    return out.reshape(2, sz.slab, KX * KY, sz.pairs)


def on_device(blocks, cell_offsets, occ_coeff, vir_coeff, transfer_index):
    arrays = (blocks, cell_offsets, occ_coeff, vir_coeff, transfer_index)
    if Sizes.fit(lax.axis_size("cell"), lax.axis_size("aux"), blocks, occ_coeff, vir_coeff):
        return by_planes(*arrays)
    return by_entries(*arrays)


def solution(mesh):
    placed = (P("cell", "aux", None, None), P(), P(), P("cell", None, None, "aux"), P())
    return jax.shard_map(
        on_device,
        mesh=mesh,
        in_specs=placed,
        out_specs=P(None, "aux", None, "cell"),
        check_vma=False,
    )
```

```python
import functools
import math

import jax
import jax.numpy as jnp
from jax import lax
from jax.experimental import pallas as pl
from jax.experimental.pallas import tpu as pltpu
from jax.sharding import PartitionSpec as P

KX = 4
KY = 4
LANES = 128
HALF_LANES = 64
SEGMENT = 32
PIECE = 2
OUT = (0, 1, 2, 3)
BACK = (0, 3, 1, 2)
SUBLANES = 8
SEGMENTS = LANES // SEGMENT
BF16 = jnp.bfloat16
F32 = jnp.float32


def phase_tables(cell_offsets, cell_count):
    depth = cell_count // (KX * KY)
    points = jnp.arange(cell_count, dtype=jnp.int32)
    along_a = points // (KY * depth)
    along_b = points // depth % KY
    along_c = points % depth
    turns = (
        along_a[:, None] * cell_offsets[0][None, :] * (KY * depth)
        + along_b[:, None] * cell_offsets[1][None, :] * (KX * depth)
        + along_c[:, None] * cell_offsets[2][None, :] * (KX * KY)
    ) % cell_count
    angles = 2.0 * math.pi / cell_count * turns.astype(jnp.float32)
    return (jnp.cos(angles), jnp.sin(angles))


def matmul(left, right):
    return jnp.dot(left, right, precision=lax.Precision.HIGHEST, preferred_element_type=jnp.float32)


def contract(form, left, right):
    return jnp.einsum(form, left, right, precision=lax.Precision.HIGHEST)


def by_entries(blocks, cell_offsets, occ_coeff, vir_coeff, transfer_index):
    cell_count = lax.axis_size("cell")
    slab_rows = blocks.shape[1]
    basis_size = blocks.shape[2]
    occupied = occ_coeff.shape[2]
    cosines, sines = phase_tables(cell_offsets, cell_count)
    occ_real, occ_imag = (occ_coeff[0], occ_coeff[1])
    flattened = blocks.reshape(1, -1)
    arrived = lax.all_to_all(flattened, "cell", split_axis=1, concat_axis=0, tiled=True)
    grid_real = matmul(cosines, arrived)
    grid_imag = matmul(sines, arrived)
    back_real, back_imag = (
        lax.all_to_all(grid_real, "cell", split_axis=0, concat_axis=1, tiled=True),
        lax.all_to_all(grid_imag, "cell", split_axis=0, concat_axis=1, tiled=True),
    )
    spec_real = back_real.reshape(slab_rows, basis_size, basis_size)
    spec_imag = back_imag.reshape(slab_rows, basis_size, basis_size)
    half_real = contract("mi,pmn->pin", occ_real, spec_real) + contract(
        "mi,pmn->pin", occ_imag, spec_imag
    )
    half_imag = contract("mi,pmn->pin", occ_real, spec_imag) - contract(
        "mi,pmn->pin", occ_imag, spec_real
    )
    rows_real = half_real.reshape(slab_rows * occupied, basis_size)
    rows_imag = half_imag.reshape(slab_rows * occupied, basis_size)
    column_piece = lax.all_gather(vir_coeff, "aux", axis=3, tiled=True)
    coef_real = column_piece[0, 0]
    coef_imag = column_piece[0, 1]
    part_real = matmul(rows_real, coef_real) - matmul(rows_imag, coef_imag)
    part_imag = matmul(rows_real, coef_imag) + matmul(rows_imag, coef_real)
    banded = jnp.stack([part_real, part_imag])
    pair_rows = banded.reshape(2, slab_rows, 1, -1)
    regrouped = lax.all_to_all(pair_rows, "cell", split_axis=3, concat_axis=2, tiled=True)
    source = jnp.argsort(transfer_index)
    return jnp.take(regrouped, source, axis=2)


def cost(flops):
    return pl.CostEstimate(flops=flops, bytes_accessed=flops // 100, transcendentals=0)


def split(value):
    high = value.astype(BF16)
    return high, (value - high.astype(F32)).astype(BF16)


def dot(left, right):
    return jnp.dot(left, right, preferred_element_type=F32)


class Sizes:
    def __init__(self, blocks, occ_coeff, vir_coeff):
        self.slab = blocks.shape[1]
        self.basis = blocks.shape[2]
        self.occ = occ_coeff.shape[2]
        self.vir_half = vir_coeff.shape[3]
        self.main = self.basis // LANES * LANES
        self.rest = self.basis - self.main
        self.columns = self.main // LANES
        self.gap = HALF_LANES - self.rest
        self.depth = 2 * self.main + 3 * HALF_LANES
        self.bands = self.occ // KX
        self.rows = 2 * SUBLANES
        self.tail = 4 * self.columns
        self.pairs = 2 * self.vir_half * self.bands // KY
        self.full = self.pairs // LANES
        self.share = LANES // KX

    @staticmethod
    def fit(cells, aux, blocks, occ_coeff, vir_coeff):
        basis, occ, half = blocks.shape[2], occ_coeff.shape[2], vir_coeff.shape[3]
        return (
            cells == KX * KY
            and aux == 2
            and blocks.shape[1] == KY
            and occ % KX == 0
            and basis > LANES
            and HALF_LANES // 2 <= basis % LANES <= HALF_LANES // 2 + SEGMENT // 2
            and SUBLANES <= occ // KX < 2 * SUBLANES
            and occ // KX - SUBLANES <= basis // LANES * (LANES // SEGMENT)
            and HALF_LANES < half <= LANES
            and 2 * half * (occ // KX) % KY == 0
            and 2 * half * (occ // KX) // KY % LANES <= LANES // KX
        )


def staggered(tile, row, first, stride):
    out = pltpu.roll(tile, first % LANES, 1)
    for r in range(1, SEGMENTS):
        out = jnp.where(row % SEGMENTS == r, pltpu.roll(tile, (first + r * stride) % LANES, 1), out)
    return out


def half_kernel(sz, block_hbm, occ_hbm, out_hbm, block_ref, occ_ref, out_ref, block_sem, occ_sem, out_sem):
    count = KX * sz.rows
    occ_copy = pltpu.make_async_copy(occ_hbm, occ_ref, occ_sem)
    block_copy = pltpu.make_async_copy(block_hbm, block_ref, block_sem)
    occ_copy.start()
    block_copy.start()
    place = lax.broadcasted_iota(jnp.int32, (count, sz.occ), 0)
    band = lax.broadcasted_iota(jnp.int32, (count, sz.occ), 1)
    inner = place % sz.rows
    pick = ((place // sz.rows * sz.bands + inner == band) & (inner < sz.bands)).astype(BF16)
    occ_copy.wait()
    terms = [split(occ_ref[:, part]) for part in range(2)]
    left_high = jnp.concatenate([dot(pick, terms[0][0]), -dot(pick, terms[1][0])], axis=0).astype(BF16)
    left_low = jnp.concatenate([dot(pick, terms[0][1]), -dot(pick, terms[1][1])], axis=0).astype(BF16)
    left = jnp.concatenate([left_high, left_low], axis=0)
    fill = jnp.zeros((sz.basis, LANES - sz.rest), F32)
    row = lax.broadcasted_iota(jnp.int32, (SUBLANES, LANES), 0)
    lane = lax.broadcasted_iota(jnp.int32, (SUBLANES, LANES), 1)
    block_copy.wait()
    for p in range(sz.slab):
        high, low = split(jnp.concatenate([block_ref[:, p], fill], axis=1))
        half = dot(left, high)
        half = half[: 2 * count] + half[2 * count :] + dot(left_high, low)
        real, imag = half[:count], half[count:]
        for z in range(KX):
            near = slice(z * sz.rows, z * sz.rows + SUBLANES)
            far = slice(z * sz.rows + SUBLANES, (z + 1) * sz.rows)
            tails = []
            for part, value in enumerate((real, imag)):
                head, last = value[near, sz.main :], value[far, sz.main :]
                tails.append(head + pltpu.roll(jnp.where(lane < sz.gap, last, 0.0), sz.rest, 1))
                spare = jnp.where(lane < sz.gap, 0.0, last)
                spare = staggered(spare, row, LANES - sz.gap, SEGMENT)
                for c in range(sz.columns):
                    lanes = slice(c * LANES, (c + 1) * LANES)
                    rows = slice(c * SEGMENTS, (c + 1) * SEGMENTS)
                    kept = jnp.sum(spare[rows], axis=0, keepdims=True)
                    tile = part * sz.columns + c
                    out_ref[z, p, tile] = value[near, lanes]
                    out_ref[z, p, 2 * sz.columns + tile] = jnp.where(row == SUBLANES - 1, kept, value[far, lanes])
            out_ref[z, p, sz.tail] = tails[0] + pltpu.roll(tails[1], HALF_LANES, 1)
        pltpu.make_async_copy(out_ref.at[:, p], out_hbm.at[:, p], out_sem.at[p]).start()
    for p in range(sz.slab):
        pltpu.make_async_copy(out_ref.at[:, p], out_hbm.at[:, p], out_sem.at[p]).wait()


def half_bands(sz, blocks, occ_coeff):
    anywhere = pl.BlockSpec(memory_space=pl.ANY)
    return pl.pallas_call(
        functools.partial(half_kernel, sz),
        out_shape=jax.ShapeDtypeStruct((KX, KY, sz.tail + 1, SUBLANES, LANES), F32),
        in_specs=[anywhere, anywhere],
        out_specs=anywhere,
        scratch_shapes=[
            pltpu.VMEM((sz.basis, sz.slab, sz.basis), F32),
            pltpu.VMEM((sz.occ, 2, sz.basis), F32),
            pltpu.VMEM((KX, KY, sz.tail + 1, SUBLANES, LANES), F32),
            pltpu.SemaphoreType.DMA,
            pltpu.SemaphoreType.DMA,
            pltpu.SemaphoreType.DMA((sz.slab,)),
        ],
        compiler_params=pltpu.CompilerParams(vmem_limit_bytes=60 << 20),
        cost_estimate=cost(10**11),
    )(blocks[0].transpose(1, 0, 2), occ_coeff.transpose(2, 0, 1))


def four_points(zero, one, two, three, turn):
    even, odd = zero + two, one + three
    lift, lean = zero - two, turn(one - three)
    return even + odd, lift + lean, even - odd, lift - lean


class Pair:
    def __init__(self, real, imag):
        self.real, self.imag = real, imag

    def __add__(self, other):
        return Pair(self.real + other.real, self.imag + other.imag)

    def __sub__(self, other):
        return Pair(self.real - other.real, self.imag - other.imag)

    def turned(self):
        return Pair(-self.imag, self.real)


def lattice_kernel(sz, place_ref, offset_ref, cells_ref, *refs):
    outs, grid_ref, slot_ref = refs[:KY], refs[KY], refs[KY + 1]
    plane, seat = place_ref[0], place_ref[1]
    for cell in range(KX * KY):
        slot_ref[(offset_ref[0, cell] & 3) * KY + (offset_ref[1, cell] & 3)] = cell
    slots = [slot_ref[n] for n in range(KX * KY)]
    real_half = lax.broadcasted_iota(jnp.int32, (SUBLANES, LANES), 1) < HALF_LANES

    def turn_rest(value):
        moved = pltpu.roll(value, HALF_LANES, 1)
        return jnp.where(real_half, -moved, moved)

    def transform(load, turn, store):
        firsts = [four_points(*[load(slots[n * KY + m]) for n in range(KX)], turn) for m in range(KY)]
        for a in range(KX):
            seconds = four_points(*[firsts[m][a] for m in range(KY)], turn)
            for b in range(KY):
                store(a, b, seconds[b])

    for h in range(2):
        for c in range(sz.columns):
            near = 2 * sz.columns * h + c
            far = near + sz.columns

            def load(cell):
                return Pair(cells_ref[cell, near], cells_ref[cell, far])

            def store(a, b, value):
                grid_ref[b, a ^ plane, near] = value.real
                grid_ref[b, a ^ plane, far] = value.imag

            transform(load, Pair.turned, store)

    def load_rest(cell):
        return cells_ref[cell, sz.tail]

    def store_rest(a, b, value):
        grid_ref[b, a ^ plane, sz.tail] = value

    transform(load_rest, turn_rest, store_rest)
    for out_ref, step in zip(outs, OUT):
        out_ref[...] = grid_ref[step ^ seat]


def lattice_sum(sz, place, cell_offsets, cells):
    shape = jax.ShapeDtypeStruct((KX, sz.tail + 1, SUBLANES, LANES), F32)
    whole = pl.BlockSpec(memory_space=pltpu.VMEM)
    scalars = pl.BlockSpec(memory_space=pltpu.SMEM)
    return pl.pallas_call(
        functools.partial(lattice_kernel, sz),
        out_shape=[shape] * KY,
        in_specs=[scalars, scalars, whole],
        out_specs=[whole] * KY,
        scratch_shapes=[
            pltpu.VMEM((KY, KX, sz.tail + 1, SUBLANES, LANES), F32),
            pltpu.SMEM((KX * KY,), jnp.int32),
        ],
        compiler_params=pltpu.CompilerParams(vmem_limit_bytes=32 << 20),
        cost_estimate=cost(10**11),
    )(place, cell_offsets, cells)


def band_kernel(sz, place_ref, *refs):
    halves, rights, outs = refs[:KY], refs[KY : KY + KX], refs[KY + KX : 2 * KY + KX]
    left_ref, band_ref, tile_ref, pack_ref = refs[2 * KY + KX :]
    wide = lax.broadcasted_iota(jnp.int32, (2 * KY, LANES), 1)
    ends = [None] * KY
    seat = place_ref[1]
    count = KY * sz.rows
    row = lax.broadcasted_iota(jnp.int32, (SUBLANES, LANES), 0)
    lane = lax.broadcasted_iota(jnp.int32, (SUBLANES, LANES), 1)
    low_lanes = lax.broadcasted_iota(jnp.int32, (2 * count, LANES), 1) < HALF_LANES
    for place, step in enumerate(OUT):
        left_ref[:, step ^ seat] = halves[place][...]

    for k in range(KX):
        left = left_ref[k]
        near, rest = [], []
        for part in range(2):
            tiles = []
            for c in range(sz.columns):
                first = part * sz.columns + c
                halves_of = [left[:, first], left[:, 2 * sz.columns + first]]
                tiles.append(jnp.stack(halves_of, axis=1).reshape(count, LANES))
            near.append(jnp.concatenate(tiles, axis=1))
            for p in range(KY):
                tail = left[p, sz.tail]
                head = pltpu.roll(tail, HALF_LANES, 1) if part else tail
                kept = [left[p, 2 * sz.columns + part * sz.columns + c] for c in range(sz.columns)]
                spare = jnp.concatenate(
                    [jnp.broadcast_to(tile[SUBLANES - 1 :], (SEGMENTS, LANES)) for tile in kept], axis=0
                )[:SUBLANES]
                spare = staggered(spare, row, sz.gap, LANES - SEGMENT)
                rest += [head, jnp.where(lane < sz.gap, pltpu.roll(head, LANES - sz.rest, 1), spare)]
        near_high, near_low = split(jnp.concatenate(near, axis=0))
        rest_high = jnp.concatenate(rest, axis=0)
        rest_low = rest_high - rest_high.astype(BF16).astype(F32)
        both = jnp.where(low_lanes, rest_high, pltpu.roll(rest_low, HALF_LANES, 1)).astype(BF16)
        rest_three = jnp.concatenate([both, rest_high.astype(BF16)[:, :HALF_LANES]], axis=1)
        right = rights[k]
        band = dot(jnp.concatenate([near_high, near_low], axis=0), right[: sz.main])
        band = band[: 2 * count] + band[2 * count :]
        band += dot(near_high, right[sz.main : 2 * sz.main]) + dot(rest_three, right[2 * sz.main :])
        width = 2 * LANES
        top, bottom = band[:count], band[count:]
        real = top[:, :width] - bottom[:, width:]
        imag = top[:, width:] + bottom[:, :width]
        for h in range(2):
            lanes = slice(h * LANES, (h + 1) * LANES)
            band_ref[h, 0] = real[:, lanes]
            band_ref[h, 1] = imag[:, lanes]
        for i in range(sz.bands):
            for h in range(2):
                for part in range(2):
                    tile_ref[2 * i + h, part * KY : (part + 1) * KY] = band_ref[
                        h, part, pl.ds(i, KY, stride=sz.rows)
                    ]
        for target in range(KY):
            for first in range(0, sz.pairs, LANES):
                last = min(first + LANES, sz.pairs)
                value = None
                begin, end = target * sz.pairs + first, target * sz.pairs + last
                for tile in range(begin // sz.vir_half, (end - 1) // sz.vir_half + 1):
                    offset = tile * sz.vir_half - begin
                    moved = pltpu.roll(tile_ref[tile], offset % LANES, 1) if offset % LANES else tile_ref[tile]
                    value = moved if value is None else jnp.where(wide < offset, value, moved)
                if last - first == LANES:
                    pack_ref[target, k * sz.full + first // LANES] = value
                else:
                    moved = pltpu.roll(value, k * sz.share, 1) if k else value
                    ends[target] = moved if k == 0 else jnp.where(wide < k * sz.share, ends[target], moved)
    for target in range(KY):
        if ends[target] is not None:
            pack_ref[target, KX * sz.full] = ends[target]
    for out_ref, step in zip(outs, BACK):
        out_ref[...] = pack_ref[step ^ seat]


def band_product(sz, place, halves, rights):
    count = KX * sz.full + (sz.pairs % LANES > 0)
    shape = jax.ShapeDtypeStruct((count, 2 * KY, LANES), F32)
    whole = pl.BlockSpec(memory_space=pltpu.VMEM)
    scalars = pl.BlockSpec(memory_space=pltpu.SMEM)
    return pl.pallas_call(
        functools.partial(band_kernel, sz),
        out_shape=[shape] * KY,
        in_specs=[scalars] + [whole] * (KY + KX),
        out_specs=[whole] * KY,
        scratch_shapes=[
            pltpu.VMEM((KX, KY, sz.tail + 1, SUBLANES, LANES), F32),
            pltpu.VMEM((2, 2, KY * sz.rows, LANES), F32),
            pltpu.VMEM((2 * sz.bands, 2 * KY, LANES), F32),
            pltpu.VMEM((KY, count, 2 * KY, LANES), F32),
        ],
        compiler_params=pltpu.CompilerParams(vmem_limit_bytes=32 << 20),
        cost_estimate=cost(10**10),
    )(place, *halves, *rights)


def regroup_kernel(sz, place_ref, transfer_ref, *refs):
    sources, out_hbm = refs[:KY], refs[KY]
    row_ref, out_ref, sems = refs[KY + 1 :]
    plane, seat = place_ref[0], place_ref[1]
    cells = KX * KY
    starts = list(range(0, sz.pairs, LANES))
    pieces = [starts[i : i + PIECE] for i in range(0, len(starts), PIECE)]
    copies = []
    for index, piece in enumerate(pieces):
        for first in piece:
            last = min(first + LANES, sz.pairs)
            for source, step in enumerate(BACK):
                for k in range(KX):
                    row = transfer_ref[(k ^ plane) * KY + (step ^ seat)]
                    if last - first == LANES:
                        tile = sources[source][k * sz.full + first // LANES]
                    else:
                        tile = sources[source][KX * sz.full]
                        tile = pltpu.roll(tile, LANES - k * sz.share, 1) if k else tile
                    row_ref[first // LANES, pl.ds(row, 2 * KY, stride=cells)] = tile
            out_ref[:, first:last] = row_ref[first // LANES, :, : last - first]
        span = pl.ds(piece[0], min(piece[-1] + LANES, sz.pairs) - piece[0])
        copies.append(pltpu.make_async_copy(out_ref.at[:, span], out_hbm.at[:, span], sems.at[index]))
        copies[-1].start()
    for copy in copies:
        copy.wait()


def regroup(sz, place, transfer_index, sources):
    whole = pl.BlockSpec(memory_space=pltpu.VMEM)
    scalars = pl.BlockSpec(memory_space=pltpu.SMEM)
    rows = 2 * KY * KX * KY
    tiles = -(-sz.pairs // LANES)
    return pl.pallas_call(
        functools.partial(regroup_kernel, sz),
        out_shape=jax.ShapeDtypeStruct((rows, sz.pairs), F32),
        in_specs=[scalars, scalars] + [whole] * KY,
        out_specs=pl.BlockSpec(memory_space=pl.ANY),
        scratch_shapes=[
            pltpu.VMEM((tiles, rows, LANES), F32),
            pltpu.VMEM((rows, sz.pairs), F32),
            pltpu.SemaphoreType.DMA((-(-tiles // PIECE),)),
        ],
        compiler_params=pltpu.CompilerParams(vmem_limit_bytes=32 << 20),
    )(place, transfer_index, *sources)


def spread_kernel(sz, in_ref, *refs):
    out_ref = refs[-1]
    fill = jnp.zeros((sz.basis, LANES - sz.vir_half), F32)
    for part in range(2):
        out_ref[part] = jnp.concatenate([in_ref[:, part], fill], axis=1)


def spread(sz, value, flops, *after):
    whole = pl.BlockSpec(memory_space=pltpu.VMEM)
    return pl.pallas_call(
        functools.partial(spread_kernel, sz),
        out_shape=jax.ShapeDtypeStruct((2, sz.basis, LANES), F32),
        in_specs=[whole] + [pl.BlockSpec(memory_space=pl.ANY)] * len(after),
        out_specs=whole,
        compiler_params=pltpu.CompilerParams(vmem_limit_bytes=32 << 20),
        cost_estimate=cost(flops),
    )(value, *after)


def copy_kernel(in_ref, *refs):
    refs[-1][...] = in_ref[...]


def copied(value, *after):
    whole = pl.BlockSpec(memory_space=pltpu.VMEM)
    return pl.pallas_call(
        copy_kernel,
        out_shape=jax.ShapeDtypeStruct(value.shape, F32),
        in_specs=[whole] + [pl.BlockSpec(memory_space=pl.ANY)] * len(after),
        out_specs=whole,
        compiler_params=pltpu.CompilerParams(vmem_limit_bytes=32 << 20),
        cost_estimate=cost(10**6),
    )(value, *after)


def columns_kernel(sz, place_ref, own_ref, other_ref, out_ref):
    core = place_ref[2]
    under = jnp.zeros((sz.gap, LANES), F32)
    for part in range(2):
        mine, theirs = [jnp.concatenate([ref[part], under], axis=0) for ref in (own_ref, other_ref)]
        for h, value in enumerate([jnp.where(core == 0, mine, theirs), jnp.where(core == 0, theirs, mine)]):
            lanes = slice((2 * part + h) * LANES, (2 * part + h + 1) * LANES)
            high, low = split(value)
            out_ref[: sz.main, lanes] = high[: sz.main]
            out_ref[sz.main : 2 * sz.main, lanes] = low[: sz.main]
            for place, term in enumerate((high, high, low)):
                first = 2 * sz.main + place * HALF_LANES
                out_ref[first : first + HALF_LANES, lanes] = term[sz.main :]


def columns(sz, place, own, other, flops):
    whole = pl.BlockSpec(memory_space=pltpu.VMEM)
    scalars = pl.BlockSpec(memory_space=pltpu.SMEM)
    return pl.pallas_call(
        functools.partial(columns_kernel, sz),
        out_shape=jax.ShapeDtypeStruct((sz.depth, 4 * LANES), BF16),
        in_specs=[scalars, whole, whole],
        out_specs=whole,
        compiler_params=pltpu.CompilerParams(vmem_limit_bytes=32 << 20),
        cost_estimate=cost(flops),
    )(place, own, other)


def swap(value, step):
    return lax.ppermute(value, "cell", [(d, d ^ step) for d in range(KX * KY)])


def swap_cores(value):
    return lax.ppermute(value, "aux", [(0, 1), (1, 0)])


def by_planes(blocks, cell_offsets, occ_coeff, vir_coeff, transfer_index):
    sz = Sizes(blocks, occ_coeff, vir_coeff)
    me = lax.axis_index("cell")
    place = jnp.stack([me // KY, me % KY, lax.axis_index("aux")]).astype(jnp.int32)
    home = vir_coeff[0].transpose(1, 0, 2)
    across = spread(sz, swap(home, 3 * KY), 10**10)
    beside = spread(sz, swap(home, KY), 10**8)
    corner = swap(across, KY)
    sent = half_bands(sz, blocks, occ_coeff).reshape(KX * KY, sz.tail + 1, SUBLANES, LANES)
    cells = lax.all_to_all(sent, "cell", split_axis=0, concat_axis=0, tiled=True)
    points = list(lattice_sum(sz, place, cell_offsets, cells))
    halves = [points[0]] + [swap(part, step) for part, step in zip(points[1:], OUT[1:])]
    ours = spread(sz, home, 3 * 10**9, beside)
    corner = copied(corner, points[0])
    rights = [columns(sz, place, v, swap_cores(v), 10**10) for v in (ours, beside, across)]
    rights.insert(2, columns(sz, place, corner, swap_cores(corner), 10**9))
    bands = band_product(sz, place, halves, rights)
    sources = [bands[0]] + [swap(band, step) for band, step in zip(bands[1:], BACK[1:])]
    out = regroup(sz, place, transfer_index, sources)
    return out.reshape(2, sz.slab, KX * KY, sz.pairs)


def on_device(blocks, cell_offsets, occ_coeff, vir_coeff, transfer_index):
    arrays = (blocks, cell_offsets, occ_coeff, vir_coeff, transfer_index)
    if Sizes.fit(lax.axis_size("cell"), lax.axis_size("aux"), blocks, occ_coeff, vir_coeff):
        return by_planes(*arrays)
    return by_entries(*arrays)


def solution(mesh):
    placed = (P("cell", "aux", None, None), P(), P(), P("cell", None, None, "aux"), P())
    return jax.shard_map(
        on_device,
        mesh=mesh,
        in_specs=placed,
        out_specs=P(None, "aux", None, "cell"),
        check_vma=False,
    )
```
